32 devices in a mesh: dp: 8 (over y, x, core), tensor: 4 (over z).
Axes of the slice: x: 2, y: 2, z: 4, core: 2. Of those that a mesh axis runs over, the one named last changes fastest.
Arguments:
- inputs: bfloat16 [32, 1024, 768], P('dp', 'tensor'), may hold values from -6 to 6
- doc_ids: int32 [32, 1024], P('dp'), may hold values from 0 to 2, as said below
- ln1_gain: float32 [768], replicated, may hold values from 0.1 to 1.9
- ln1_bias: float32 [768], replicated, may hold values from -1.5 to 1.5
- w_qkv: bfloat16 [768, 3, 768], P(None, None, 'tensor'), may hold values from -0.21875 to 0.21875
- b_qv: float32 [2, 768], P(None, 'tensor'), may hold values from -1.5 to 1.5
- w_out: bfloat16 [768, 768], P('tensor'), may hold values from -1.75 to 1.75
- out_bias: float32 [768], replicated, may hold values from -1.5 to 1.5
- ln2_gain: float32 [768], replicated, may hold values from 0.1 to 1.9
- ln2_bias: float32 [768], replicated, may hold values from -1.5 to 1.5
- w_up: bfloat16 [768, 3072], P(None, 'tensor'), may hold values from -0.21875 to 0.21875
- b_up: float32 [3072], P('tensor'), may hold values from -1.5 to 1.5
- w_down: bfloat16 [3072, 768], P('tensor'), may hold values from -0.15625 to 0.15625
- down_bias: float32 [768], replicated, may hold values from -1.5 to 1.5
- cotangent: bfloat16 [32, 1024, 768], P('dp', 'tensor'), may hold values from -6 to 6
Outputs:
- block_out: bfloat16 [32, 1024, 768], P('dp', 'tensor')
- grad_inputs: bfloat16 [32, 1024, 768], P('dp', 'tensor')
- grad_ln1_gain: float32 [768], P(('dp', 'tensor'))
- grad_ln1_bias: float32 [768], P(('dp', 'tensor'))
- grad_w_qkv: float32 [768, 3, 768], P('dp', None, 'tensor')
- grad_b_qv: float32 [2, 768], P(None, ('tensor', 'dp'))
- grad_w_out: float32 [768, 768], P('tensor', 'dp')
- grad_out_bias: float32 [768], P(('dp', 'tensor'))
- grad_ln2_gain: float32 [768], P(('dp', 'tensor'))
- grad_ln2_bias: float32 [768], P(('dp', 'tensor'))
- grad_w_up: float32 [768, 3072], P('dp', 'tensor')
- grad_b_up: float32 [3072], P(('tensor', 'dp'))
- grad_w_down: float32 [3072, 768], P('tensor', 'dp')
- grad_down_bias: float32 [768], P(('dp', 'tensor'))
The draws below stay inside these ranges and needn't reach their ends.
Inputs may be any that keep to these rules, and one draw needn't show every extreme that they name: `doc_ids`: along every row the ids start at 0, never fall, and a document ends where the id changes; every row holds one document of exactly 769 tokens, its longest.
All inputs are finite; a program needn't handle non-finite values.
Results may differ from the reference program's by a relative error of at most 0.02.
Values may be sent and summed in bfloat16 or wider, within the bound.
No kernel may reach another device: no remote copies, remote signals or barrier semaphores. Data moves between devices by JAX's collectives and lax.ppermute only.
A program may use at most 320 MiB of HBM per device.

```python
import jax
import jax.numpy as jnp
from jax import lax

D = 768
FF = 3072
SEQ = 1024
ROWS_DEV = 4
ROWS = 32
LONG_DOC = 769
N_DP = 8


def draw_doc_ids(key, part):
    key = jax.random.fold_in(key, 11)
    key_start = jax.random.fold_in(key, 1)
    starts = jax.random.randint(key_start, (ROWS, 1), 0, SEQ - LONG_DOC + 1)
    first_row = jnp.arange(ROWS, dtype=jnp.int32)[:, None] == 0
    starts = jnp.where(first_row, 1, starts)
    places = jnp.arange(SEQ, dtype=jnp.int32)[None, :]
    boundary = (places == starts) | (places == starts + LONG_DOC)
    boundary = boundary & (places > 0)
    return jnp.cumsum(boundary.astype(jnp.int32), axis=1).astype(jnp.int32)


def block_levels(stream_key, shape, cuts, low, largest):
    def one(axis_at, parts):
        heights = jax.random.uniform(jax.random.fold_in(jax.random.fold_in(stream_key, 6), axis_at), (parts,), jnp.float32, low / len(cuts), largest / len(cuts))
        return jnp.repeat(jnp.exp(heights), shape[axis_at] // parts).reshape((-1,) + (1,) * (len(shape) - axis_at - 1))

    factor_of = one(*cuts[0])
    for cut in cuts[1:]:
        factor_of = factor_of * one(*cut)
    return factor_of


def normal_values(own_key, extent, scale, limit, shards=(), held_as=jnp.bfloat16):
    drawn = jax.random.normal(own_key, extent, jnp.float32) * scale
    if len(shards) > 0:
        drawn = block_levels(own_key, extent, shards, -0.22, 0.18) * drawn
    return jnp.clip(drawn, min=-limit, max=limit).astype(held_as)


def setup_inputs(seed: int = 0) -> dict:
    key_list = jax.random.split(jax.random.key(seed), 16)
    inputs = normal_values(key_list[0], (ROWS, SEQ, D), 1.0, 6.0, ((0, 8), (1, 4)))
    doc_ids = draw_doc_ids(jax.random.fold_in(key_list[15], 71), 0)
    ln1_gain = jnp.clip(1.0 + 0.18 * jax.random.normal(key_list[2], (D,), jnp.float32), 0.1, 1.9)
    ln1_bias = normal_values(key_list[3], (D,), 0.3, 1.5, (), jnp.float32)
    w_qkv = normal_values(key_list[4], (D, 3, D), D ** -0.5, 0.21875, ((2, 4),))
    b_qv = normal_values(key_list[5], (2, D), 0.3, 1.5, ((1, 4),), jnp.float32)
    w_out = normal_values(key_list[6], (D, D), (D // 64) ** -0.5, 1.75, ((0, 4),))
    out_bias = normal_values(key_list[7], (D,), 0.3, 1.5, (), jnp.float32)
    ln2_gain = jnp.clip(1.0 + 0.18 * jax.random.normal(key_list[8], (D,), jnp.float32), 0.1, 1.9)
    ln2_bias = normal_values(key_list[9], (D,), 0.3, 1.5, (), jnp.float32)
    w_up = normal_values(key_list[10], (D, FF), D ** -0.5, 0.21875, ((1, 4),))
    b_up = normal_values(key_list[11], (FF,), 0.3, 1.5, ((0, 4),), jnp.float32)
    w_down = normal_values(key_list[12], (FF, D), (FF // 2) ** -0.5, 0.15625, ((0, 4),))
    down_bias = normal_values(key_list[13], (D,), 0.3, 1.5, (), jnp.float32)
    cotangent = normal_values(key_list[14], (ROWS, SEQ, D), 1.0, 6.0, ((0, 8), (1, 4)))
    return {"inputs": inputs, "doc_ids": doc_ids, "ln1_gain": ln1_gain, "ln1_bias": ln1_bias, "w_qkv": w_qkv, "b_qv": b_qv, "w_out": w_out, "out_bias": out_bias, "ln2_gain": ln2_gain, "ln2_bias": ln2_bias, "w_up": w_up, "b_up": b_up, "w_down": w_down, "down_bias": down_bias, "cotangent": cotangent}


@jax.custom_vjp
def low(v):
    return lax.optimization_barrier(v.astype(jnp.bfloat16)).astype(jnp.float32)

@jax.custom_vjp
def low_back(v):
    return v

def low_keep(v):
    return (low(v), None)

def low_pass(kept, grad):
    return (grad,)

def back_keep(v):
    return (v, None)

def back_low(kept, grad):
    return (low(grad),)
low.defvjp(low_keep, low_pass)
low_back.defvjp(back_keep, back_low)
precise_dot = lax.Precision.HIGHEST

def both_ways(value_in):
    return low(low_back(value_in))

def norm_rows(value_in, gain, bias):
    mean_row = lax.optimization_barrier(jnp.mean(value_in, axis=-1, keepdims=True))
    centred = value_in - mean_row
    variance = lax.optimization_barrier(jnp.mean(centred * centred, axis=-1, keepdims=True))
    return centred * lax.rsqrt(variance + 1e-05) * gain + bias

def attend_row(query_row, key_row, value_row, doc_row):
    seq_len = query_row.shape[0]
    scores = jnp.einsum('qhe,khe->hqk', query_row, key_row, precision=precise_dot) * 0.125
    scores = low_back(scores)
    places = jnp.arange(seq_len)
    allowed = (doc_row[:, None] == doc_row[None, :]) & (places[:, None] >= places[None, :])
    scores = jnp.where(allowed[None], scores, -1e+30)
    top_row = lax.optimization_barrier(jnp.max(scores, axis=-1, keepdims=True))
    expo = jnp.exp(scores - top_row)
    probs_low = low(expo / lax.optimization_barrier(jnp.sum(expo, axis=-1, keepdims=True)))
    return jnp.einsum('hqk,khe->qhe', probs_low, value_row, precision=precise_dot)

def block_forward(inputs_f, docs, ln1_gain, ln1_bias, w_qkv, b_qv, w_out, out_bias, ln2_gain, ln2_bias, w_up, b_up, w_down, down_bias):
    n_rows, seq_len, model_width = inputs_f.shape
    head_count = model_width // 64
    normed_one = low(norm_rows(inputs_f, ln1_gain, ln1_bias))
    projected = jnp.einsum('rld,dcm->rlcm', normed_one, w_qkv, precision=precise_dot)
    queries = both_ways(projected[:, :, 0] + b_qv[0])
    keyed = both_ways(projected[:, :, 1])
    valued = both_ways(projected[:, :, 2] + b_qv[1])

    def by_head(tensor_in):
        return tensor_in.reshape(n_rows, seq_len, head_count, 64)

    def one_row(items):
        return attend_row(items[0], items[1], items[2], items[3])
    attended = lax.map(jax.checkpoint(one_row), (by_head(queries), by_head(keyed), by_head(valued), docs))
    attended = both_ways(attended.reshape(n_rows, seq_len, model_width))
    mixed = inputs_f + low_back(jnp.einsum('rlm,md->rld', attended, w_out, precision=precise_dot)) + out_bias
    normed_two = low(norm_rows(mixed, ln2_gain, ln2_bias))
    pre_act = low_back(jnp.einsum('rld,df->rlf', normed_two, w_up, precision=precise_dot) + b_up)
    activated = low(jax.nn.gelu(pre_act, approximate=True))
    return mixed + low_back(jnp.einsum('rlf,fd->rld', activated, w_down, precision=precise_dot)) + down_bias

def reference(inputs, doc_ids, ln1_gain, ln1_bias, w_qkv, b_qv, w_out, out_bias, ln2_gain, ln2_bias, w_up, b_up, w_down, down_bias, cotangent):
    params = tuple((item.astype(jnp.float32) for item in (ln1_gain, ln1_bias, w_qkv, b_qv, w_out, out_bias, ln2_gain, ln2_bias, w_up, b_up, w_down, down_bias)))
    groups = inputs.astype(jnp.float32).reshape(N_DP, ROWS_DEV, SEQ, D)
    doc_groups = doc_ids.reshape(N_DP, ROWS_DEV, SEQ)
    cot_groups = cotangent.astype(jnp.float32).reshape(N_DP, ROWS_DEV, SEQ, D)

    def one_group(totals, batch):
        group_in, group_docs, group_cot = batch

        def forward(group_x, *weights):
            return block_forward(group_x, group_docs, *weights)
        result, pullback = jax.vjp(forward, group_in, *params)
        grads = pullback(group_cot)
        totals = tuple((total + grad_item for total, grad_item in zip(totals, grads[1:])))
        return (totals, (result.astype(jnp.bfloat16), grads[0].astype(jnp.bfloat16)))
    zeros = tuple((jnp.zeros_like(item) for item in params))
    totals, (outputs, input_grads) = lax.scan(one_group, zeros, (groups, doc_groups, cot_groups))
    block_out = outputs.reshape(ROWS, SEQ, D)
    grad_inputs = input_grads.reshape(ROWS, SEQ, D)
    return (block_out, grad_inputs, totals[0], totals[1], totals[2], totals[3], totals[4], totals[5], totals[6], totals[7], totals[8], totals[9], totals[10], totals[11])
```

```python
import functools

import jax
import jax.numpy as jnp
from jax import lax
from jax.experimental import pallas as pl
from jax.experimental.pallas import tpu as pltpu
from jax.sharding import PartitionSpec as P

BF = jnp.bfloat16
F32 = jnp.float32
HEAD = 64
EPS = 1e-05
GELU_C = 0.7978845608028654
GELU_A = 0.044715
BLOCK = 256
VMEM_LIMIT = 58 * 1024 * 1024


def dot(lhs, rhs, lhs_dim, rhs_dim):
    return lax.dot_general(
        lhs, rhs, (((lhs_dim,), (rhs_dim,)), ((), ())), preferred_element_type=F32
    )


def normalize(value):
    mean = jnp.mean(value, axis=-1, keepdims=True)
    centred = value - mean
    variance = jnp.mean(centred * centred, axis=-1, keepdims=True)
    rstd = lax.rsqrt(variance + EPS)
    return centred * rstd, rstd


def norm_backward(grad, xhat, rstd, gain):
    scaled = grad * gain
    mean_e = jnp.mean(scaled, axis=-1, keepdims=True)
    mean_ex = jnp.mean(scaled * xhat, axis=-1, keepdims=True)
    return rstd * (scaled - mean_e - xhat * mean_ex)


def params(limit=VMEM_LIMIT):
    return pltpu.CompilerParams(vmem_limit_bytes=limit)


def full_spec():
    return pl.BlockSpec(memory_space=pltpu.VMEM)


def norm_one_kernel(x_ref, gain_ref, bias_ref, out_ref):
    seq = x_ref.shape[0]

    @pl.loop(0, seq // BLOCK)
    def _(step):
        rows = pl.ds(pl.multiple_of(step * BLOCK, BLOCK), BLOCK)
        xhat, _ = normalize(x_ref[rows, :].astype(F32))
        normed = xhat * gain_ref[...] + bias_ref[...]
        out_ref[:, rows] = normed.T.astype(BF)


def norm_one(x, gain, bias):
    seq, width = x.shape
    return pl.pallas_call(
        norm_one_kernel,
        out_shape=jax.ShapeDtypeStruct((width, seq), BF),
        in_specs=[full_spec()] * 3,
        out_specs=full_spec(),
        compiler_params=params(),
        name="norm_one",
        cost_estimate=pl.CostEstimate(flops=20 * seq * width, bytes_accessed=4 * seq * width, transcendentals=0),
    )(x, gain, bias)


def mask_bias(docs_col_ref, docs_row_ref, mask_ref):
    seq = mask_ref.shape[0]
    for first in range(0, seq, BLOCK):
        last = first + BLOCK
        same = docs_col_ref[0:last, :] == docs_row_ref[:, first:last]
        place_k = lax.broadcasted_iota(jnp.int32, (last, BLOCK), 0)
        place_q = first + lax.broadcasted_iota(jnp.int32, (last, BLOCK), 1)
        allowed = same & (place_k <= place_q)
        mask_ref[0:last, first:last] = jnp.where(allowed, 0.0, -1e30).astype(F32)


def attend_kernel(n1t_ref, a_ref, bq_ref, bv_ref, dcol_ref, drow_ref, qkvt_ref, at_ref, lse_ref, mask_ref):
    seq = n1t_ref.shape[1]
    part = a_ref.shape[1] // 4
    mask_bias(dcol_ref, drow_ref, mask_ref)
    for c in range(3):
        w_t = a_ref[:, c * part : (c + 1) * part].T
        proj = dot(w_t, n1t_ref[...], 1, 0)
        if c == 0:
            proj = proj + bq_ref[...]
        if c == 2:
            proj = proj + bv_ref[...]
        qkvt_ref[c * part : (c + 1) * part, :] = proj.astype(BF)
    for h in range(part // HEAD):
        q_rows = slice(h * HEAD, (h + 1) * HEAD)
        k_rows = slice(part + h * HEAD, part + (h + 1) * HEAD)
        v_rows = slice(2 * part + h * HEAD, 2 * part + (h + 1) * HEAD)
        keys = qkvt_ref[k_rows, :].T
        for first in range(0, seq, BLOCK):
            last = first + BLOCK
            q_blk = qkvt_ref[q_rows, first:last] * BF(0.125)
            scores = dot(keys[0:last], q_blk, 1, 0) + mask_ref[0:last, first:last]
            top = jnp.max(scores, axis=0, keepdims=True)
            expo = jnp.exp(scores - top)
            total = jnp.sum(expo, axis=0, keepdims=True)
            out = dot(qkvt_ref[v_rows, 0:last], expo.astype(BF), 1, 0)
            at_ref[q_rows, first:last] = (out / total).astype(BF)
            lse_ref[h : h + 1, first:last] = top + jnp.log(total)


def attend(n1t, a_k, bq, bv, dcol, drow):
    width, seq = n1t.shape
    part = a_k.shape[1] // 4
    return pl.pallas_call(
        attend_kernel,
        out_shape=(
            jax.ShapeDtypeStruct((3 * part, seq), BF),
            jax.ShapeDtypeStruct((part, seq), BF),
            jax.ShapeDtypeStruct((8, seq), F32),
        ),
        in_specs=[full_spec()] * 6,
        out_specs=(full_spec(),) * 3,
        scratch_shapes=[pltpu.VMEM((seq, seq), F32)],
        compiler_params=params(),
        name="attend",
        cost_estimate=pl.CostEstimate(
            flops=2 * seq * width * 3 * part + 4 * seq * seq * part * 4, bytes_accessed=8 * seq * width, transcendentals=seq * seq
        ),
    )(n1t, a_k, bq, bv, dcol, drow)


def attend_back_kernel(
    gmt_ref, n1t_ref, a_ref, qkvt_ref, at_ref, lse_ref, dcol_ref, drow_ref,
    gpt_ref, da_ref, gb_ref, mask_ref, gat_ref, dkv_ref,
):
    seq = n1t_ref.shape[1]
    part = a_ref.shape[1] // 4
    mask_bias(dcol_ref, drow_ref, mask_ref)
    w_out = a_ref[:, 3 * part :].T
    gat_ref[...] = dot(w_out, gmt_ref[...], 1, 0).astype(BF)
    for h in range(part // HEAD):
        q_rows = slice(h * HEAD, (h + 1) * HEAD)
        k_rows = slice(part + h * HEAD, part + (h + 1) * HEAD)
        v_rows = slice(2 * part + h * HEAD, 2 * part + (h + 1) * HEAD)
        keys = qkvt_ref[k_rows, :].T
        values = qkvt_ref[v_rows, :].T
        for first in range(0, seq, BLOCK):
            last = first + BLOCK
            q_blk = qkvt_ref[q_rows, first:last] * BF(0.125)
            g_blk = gat_ref[q_rows, first:last]
            delta = jnp.sum(
                g_blk.astype(F32) * at_ref[q_rows, first:last].astype(F32), axis=0, keepdims=True
            )
            scores = dot(keys[0:last], q_blk, 1, 0) + mask_ref[0:last, first:last]
            probs = jnp.exp(scores - lse_ref[h : h + 1, first:last])
            grad_probs = dot(values[0:last], g_blk, 1, 0)
            probs_low = probs.astype(BF)
            grad_scores = (probs * (grad_probs - delta)).astype(BF)
            gpt_ref[q_rows, first:last] = (
                0.125 * dot(qkvt_ref[k_rows, 0:last], grad_scores, 1, 0)
            ).astype(BF)
            gk = dot(q_blk, grad_scores, 1, 1)
            gv = dot(g_blk, probs_low, 1, 1)
            if first > 0:
                dkv_ref[0:HEAD, 0:first] += gk[:, 0:first]
                dkv_ref[HEAD:, 0:first] += gv[:, 0:first]
            dkv_ref[0:HEAD, first:last] = gk[:, first:last]
            dkv_ref[HEAD:, first:last] = gv[:, first:last]
        gpt_ref[k_rows, :] = dkv_ref[0:HEAD, :].astype(BF)
        gpt_ref[v_rows, :] = dkv_ref[HEAD:, :].astype(BF)
    gb_ref[:, 0:1] = jnp.sum(gpt_ref[0:part, :].astype(F32), axis=1, keepdims=True)
    gb_ref[:, 1:2] = jnp.sum(gpt_ref[2 * part : 3 * part, :].astype(F32), axis=1, keepdims=True)
    da_ref[:, 0 : 3 * part] = dot(n1t_ref[...], gpt_ref[...], 1, 1).astype(BF)
    da_ref[:, 3 * part :] = dot(gmt_ref[...], at_ref[...], 1, 1).astype(BF)


def attend_back(gmt, n1t, a_k, qkvt, at, lse, dcol, drow):
    width, seq = n1t.shape
    part = a_k.shape[1] // 4
    return pl.pallas_call(
        attend_back_kernel,
        out_shape=(
            jax.ShapeDtypeStruct((3 * part, seq), BF),
            jax.ShapeDtypeStruct((width, 4 * part), BF),
            jax.ShapeDtypeStruct((part, 2), F32),
        ),
        in_specs=[full_spec()] * 8,
        out_specs=(full_spec(),) * 3,
        scratch_shapes=[
            pltpu.VMEM((seq, seq), F32),
            pltpu.VMEM((part, seq), BF),
            pltpu.VMEM((2 * HEAD, seq), F32),
        ],
        compiler_params=params(),
        name="attend_back",
        cost_estimate=pl.CostEstimate(
            flops=2 * seq * width * 5 * part + 10 * seq * seq * part * 4, bytes_accessed=12 * seq * width, transcendentals=seq * seq
        ),
    )(gmt, n1t, a_k, qkvt, at, lse, dcol, drow)


FF_BLOCK = 256


def mlp_kernel(
    x_ref, at_ref, a_ref, m_ref, bup_ref, cot_ref, vec_ref,
    out_ref, gm_ref, gmt_ref, dm_ref, gvec_ref, gbup_ref,
    mixed_ref, n2_ref, n2t_ref, cott_ref, down_ref, gn_ref, act_ref, gpre_ref,
):
    seq, width = x_ref.shape
    n_t = at_ref.shape[0]
    part = at_ref.shape[1]
    ff = m_ref.shape[2] // 2
    step_t = pl.program_id(0)
    steps = seq // BLOCK

    @pl.when(step_t == 0)
    def _():
        down_ref[...] = jnp.zeros_like(down_ref)
        gn_ref[...] = jnp.zeros_like(gn_ref)

        @pl.loop(0, steps)
        def _(step):
            rows = pl.ds(pl.multiple_of(step * BLOCK, BLOCK), BLOCK)
            total = x_ref[rows, :].astype(F32) + vec_ref[0:1, :]
            for t in range(n_t):
                total += dot(at_ref[t, :, rows].T, a_ref[t], 1, 1)
            mixed_ref[rows, :] = total
            xhat, _ = normalize(total)
            normed = (xhat * vec_ref[1:2, :] + vec_ref[2:3, :]).astype(BF)
            n2_ref[rows, :] = normed
            n2t_ref[:, rows] = normed.T
            cott_ref[:, rows] = cot_ref[rows, :].T

    for chunk in range(ff // FF_BLOCK):
        cols = slice(chunk * FF_BLOCK, (chunk + 1) * FF_BLOCK)
        down_cols = slice(ff + chunk * FF_BLOCK, ff + (chunk + 1) * FF_BLOCK)
        w_up = m_ref[0, :, cols]
        w_down = m_ref[0, :, down_cols]
        b_up = bup_ref[0, :, cols]

        def one(step, sums):
            rows = pl.ds(pl.multiple_of(step * BLOCK, BLOCK), BLOCK)
            pre = dot(n2_ref[rows, :], w_up, 1, 0) + b_up
            grad_act = dot(cot_ref[rows, :], w_down, 1, 0)
            square = pre * pre
            curve = jnp.tanh(pre * (GELU_C + (GELU_C * GELU_A) * square))
            half = 0.5 + 0.5 * curve
            act = (pre * half).astype(BF)
            slope = half + (half - half * curve) * pre * (GELU_C + (3 * GELU_C * GELU_A) * square)
            grad_pre = (slope * grad_act).astype(BF)
            act_ref[rows, :] = act
            gpre_ref[rows, :] = grad_pre
            down_ref[rows, :] += dot(act, w_down, 1, 1)
            gn_ref[rows, :] += dot(grad_pre, w_up, 1, 1)
            return sums + jnp.sum(grad_pre.astype(F32), axis=0, keepdims=True)

        gbup_ref[0, :, cols] = lax.fori_loop(0, steps, one, jnp.zeros((1, FF_BLOCK), F32))
        dm_ref[0, :, cols] = dot(n2t_ref[...], gpre_ref[...], 1, 0).astype(BF)
        dm_ref[0, :, down_cols] = dot(cott_ref[...], act_ref[...], 1, 0).astype(BF)

    @pl.when(step_t == n_t - 1)
    def _():
        gvec_ref[...] = jnp.zeros_like(gvec_ref)

        @pl.loop(0, steps)
        def _(step):
            rows = pl.ds(pl.multiple_of(step * BLOCK, BLOCK), BLOCK)
            mixed = mixed_ref[rows, :]
            out_ref[rows, :] = (mixed + down_ref[rows, :] + vec_ref[3:4, :]).astype(BF)
            xhat, rstd = normalize(mixed)
            grad_n = gn_ref[rows, :]
            cot = cot_ref[rows, :].astype(F32)
            grad_mixed = cot + norm_backward(grad_n, xhat, rstd, vec_ref[1:2, :])
            gm_ref[rows, :] = grad_mixed
            gmt_ref[:, rows] = grad_mixed.T.astype(BF)
            gvec_ref[0:1, :] += jnp.sum(grad_mixed, axis=0, keepdims=True)
            gvec_ref[1:2, :] += jnp.sum(grad_n * xhat, axis=0, keepdims=True)
            gvec_ref[2:3, :] += jnp.sum(grad_n, axis=0, keepdims=True)
            gvec_ref[3:4, :] += jnp.sum(cot, axis=0, keepdims=True)


def mlp(x, at, w_out, m_all, b_up, cot, vecs):
    seq, width = x.shape
    n_t, part, _ = at.shape
    ff2 = m_all.shape[2]
    ff = ff2 // 2

    def fixed(shape):
        return pl.BlockSpec(shape, lambda t: (0,) * len(shape), pipeline_mode=pl.Buffered(1))

    return pl.pallas_call(
        mlp_kernel,
        grid=(n_t,),
        out_shape=(
            jax.ShapeDtypeStruct((seq, width), BF),
            jax.ShapeDtypeStruct((seq, width), F32),
            jax.ShapeDtypeStruct((width, seq), BF),
            jax.ShapeDtypeStruct((n_t, width, ff2), BF),
            jax.ShapeDtypeStruct((8, width), F32),
            jax.ShapeDtypeStruct((n_t, 1, ff), F32),
        ),
        in_specs=[
            fixed((seq, width)),
            fixed((n_t, part, seq)),
            fixed((n_t, width, part)),
            pl.BlockSpec((1, width, ff2), lambda t: (t, 0, 0)),
            pl.BlockSpec((1, 1, ff), lambda t: (t, 0, 0)),
            fixed((seq, width)),
            fixed(vecs.shape),
        ],
        out_specs=(
            fixed((seq, width)),
            fixed((seq, width)),
            fixed((width, seq)),
            pl.BlockSpec((1, width, ff2), lambda t: (t, 0, 0)),
            fixed((8, width)),
            pl.BlockSpec((1, 1, ff), lambda t: (t, 0, 0)),
        ),
        scratch_shapes=[
            pltpu.VMEM((seq, width), F32),
            pltpu.VMEM((seq, width), BF),
            pltpu.VMEM((width, seq), BF),
            pltpu.VMEM((width, seq), BF),
            pltpu.VMEM((seq, width), F32),
            pltpu.VMEM((seq, width), F32),
            pltpu.VMEM((seq, FF_BLOCK), BF),
            pltpu.VMEM((seq, FF_BLOCK), BF),
        ],
        compiler_params=params(),
        name="mlp",
        cost_estimate=pl.CostEstimate(
            flops=2 * seq * width * n_t * (6 * ff + part), bytes_accessed=20 * seq * width, transcendentals=seq * n_t * ff
        ),
    )(x, at, w_out, m_all, b_up, cot, vecs)


def input_back_kernel(gpt_ref, a_ref, x_ref, gm_ref, gain_ref, out_ref, gvec_ref):
    seq = x_ref.shape[0]
    n_t = gpt_ref.shape[0]
    part3 = gpt_ref.shape[1]
    gvec_ref[...] = jnp.zeros_like(gvec_ref)

    @pl.loop(0, seq // BLOCK)
    def _(step):
        rows = pl.ds(pl.multiple_of(step * BLOCK, BLOCK), BLOCK)
        grad_n = dot(gpt_ref[0, :, rows].T, a_ref[0, :, 0:part3], 1, 1)
        for t in range(1, n_t):
            grad_n += dot(gpt_ref[t, :, rows].T, a_ref[t, :, 0:part3], 1, 1)
        xhat, rstd = normalize(x_ref[rows, :].astype(F32))
        grad_in = gm_ref[rows, :] + norm_backward(grad_n, xhat, rstd, gain_ref[...])
        out_ref[rows, :] = grad_in.astype(BF)
        gvec_ref[0:1, :] += jnp.sum(grad_n * xhat, axis=0, keepdims=True)
        gvec_ref[1:2, :] += jnp.sum(grad_n, axis=0, keepdims=True)


def input_back(gpt, a_all, x, gm, gain):
    seq, width = x.shape
    return pl.pallas_call(
        input_back_kernel,
        out_shape=(jax.ShapeDtypeStruct((seq, width), BF), jax.ShapeDtypeStruct((8, width), F32)),
        in_specs=[full_spec()] * 5,
        out_specs=(full_spec(),) * 2,
        compiler_params=params(),
        name="input_back",
        cost_estimate=pl.CostEstimate(
            flops=2 * seq * width * gpt.shape[0] * gpt.shape[1], bytes_accessed=16 * seq * width, transcendentals=0
        ),
    )(gpt, a_all, x, gm, gain)


def gather_pieces(piece, own, n_dp, n_t):
    dp = lax.axis_index("dp")
    if n_dp != 8:
        shards = [own]
        for k in range(1, n_t):
            shards.append(lax.ppermute(own, "tensor", [((z + k) % n_t, z) for z in range(n_t)]))
        return jnp.stack(shards)
    moved = [
        lax.ppermute(piece, "tensor", [((z + k) % n_t, z) for z in range(n_t)]) for k in range(1, n_t)
    ]
    held = {0: jnp.stack(moved)}
    for mask in (2, 4, 6):
        held[mask] = lax.ppermute(held[0], "dp", [(i, i ^ mask) for i in range(n_dp)])
    for mask in (0, 2, 4, 6):
        held[mask + 1] = lax.ppermute(held[mask], "dp", [(i, i ^ 1) for i in range(n_dp)])
    rows = piece.shape[0]
    whole = jnp.zeros((n_t - 1,) + own.shape, own.dtype)
    for mask, part in held.items():
        whole = lax.dynamic_update_slice(whole, part, (0, (dp ^ mask) * rows, 0))
    return jnp.concatenate([own[None], whole])


def scatter_sum(grads, n_dp, n_t):
    dp = lax.axis_index("dp")
    rows = grads.shape[1] // n_dp
    cols = grads.shape[2]
    if n_dp != 8:
        summed = lax.psum_scatter(grads, "dp", scatter_dimension=1, tiled=True)
    else:
        split = grads.reshape(n_t, n_dp // 2, 2, rows, cols)
        core = dp % 2
        keep = lax.dynamic_index_in_dim(split, core, 2, keepdims=False)
        send = lax.dynamic_index_in_dim(split, 1 - core, 2, keepdims=False)
        got = lax.ppermute(send, "dp", [(i, i ^ 1) for i in range(n_dp)])
        half = (keep.astype(F32) + got.astype(F32)).astype(BF)
        total = lax.dynamic_index_in_dim(half, dp // 2, 1, keepdims=False).astype(F32)
        for mask in (2, 4, 6):
            part = lax.dynamic_index_in_dim(half, (dp ^ mask) // 2, 1, keepdims=False)
            total += lax.ppermute(part, "dp", [(i, i ^ mask) for i in range(n_dp)]).astype(F32)
        summed = total.astype(BF)
    result = summed[0].astype(F32)
    for k in range(1, n_t):
        result += lax.ppermute(
            summed[k], "tensor", [(z, (z + k) % n_t) for z in range(n_t)]
        ).astype(F32)
    return result


def to_rows(blocks, n_t):
    return lax.all_to_all(blocks, "tensor", 0, 1, tiled=True)


def to_positions(rows, n_t):
    return lax.all_to_all(rows, "tensor", 1, 0, tiled=True)


def local(n_dp, n_t, inputs, doc_ids, ln1_gain, ln1_bias, w_qkv, b_qv, w_out, out_bias, ln2_gain, ln2_bias,
          w_up, b_up, w_down, down_bias, cotangent):
    width = inputs.shape[2]
    part = w_out.shape[0]
    dp = lax.axis_index("dp")
    tensor = lax.axis_index("tensor")
    own_rows = inputs.shape[0] // n_t

    own_a = jnp.concatenate([w_qkv.reshape(width, 3 * part), w_out.T], axis=1)
    own_m = jnp.concatenate([w_up, w_down.T], axis=1)
    rows = width // n_dp
    piece_a = lax.dynamic_slice_in_dim(own_a, dp * rows, rows, 0)
    piece_m = lax.dynamic_slice_in_dim(own_m, dp * rows, rows, 0)
    a_all = gather_pieces(piece_a, own_a, n_dp, n_t)
    x_rows = to_rows(inputs, n_t)
    cot_rows = to_rows(cotangent, n_t)
    m_all = gather_pieces(piece_m, own_m, n_dp, n_t)

    small = jnp.concatenate([b_qv.reshape(-1), b_up])
    smalls = [small]
    for k in range(1, n_t):
        smalls.append(lax.ppermute(small, "tensor", [((z + k) % n_t, z) for z in range(n_t)]))
    smalls = jnp.stack(smalls)
    bq = smalls[:, 0:part, None]
    bv = smalls[:, part : 2 * part, None]
    bup = smalls[:, None, 2 * part :]
    vecs = jnp.stack([out_bias, ln2_gain, ln2_bias, down_bias])
    doc_rows = lax.dynamic_slice_in_dim(doc_ids, tensor * own_rows, own_rows, 0)

    outs, grads_in, das, dms, gvecs, gins, gbs, gbups = [], [], [], [], [], [], [], []
    for r in range(own_rows):
        x = x_rows[r]
        drow = doc_rows[r][None, :]
        dcol = doc_rows[r][:, None]
        n1t = norm_one(x, ln1_gain[None], ln1_bias[None])
        fwd = [attend(n1t, a_all[k], bq[k], bv[k], dcol, drow) for k in range(n_t)]
        at = jnp.stack([f[1] for f in fwd])
        out, gm, gmt, dm, gvec, gbup = mlp(x, at, a_all[:, :, 3 * part :], m_all, bup, cot_rows[r], vecs)
        back = [
            attend_back(gmt, n1t, a_all[k], fwd[k][0], fwd[k][1], fwd[k][2], dcol, drow) for k in range(n_t)
        ]
        gpt = jnp.stack([b[0] for b in back])
        grad_in, gin = input_back(gpt, a_all, x, gm, ln1_gain[None])
        outs.append(out)
        grads_in.append(grad_in)
        das.append(jnp.stack([b[1] for b in back]))
        gbs.append(jnp.stack([b[2] for b in back]))
        dms.append(dm)
        gvecs.append(gvec)
        gins.append(gin)
        gbups.append(gbup)

    def total(items):
        if len(items) == 1:
            return items[0]
        return sum(item.astype(F32) for item in items).astype(items[0].dtype)

    block_out = to_positions(jnp.stack(outs), n_t)
    grad_inputs = to_positions(jnp.stack(grads_in), n_t)
    share_m = scatter_sum(total(dms), n_dp, n_t)
    share_a = scatter_sum(total(das), n_dp, n_t)
    gvec, gin, gb, gbup = total(gvecs), total(gins), total(gbs), total(gbups)

    ff = w_up.shape[1]
    spread = jnp.concatenate([gin[0:2], gvec[0:4]])
    spread = spread.reshape(6, n_dp * n_t, width // (n_dp * n_t)).transpose(1, 0, 2).reshape(n_dp, n_t, -1)
    shard = jnp.concatenate(
        [
            gb.transpose(0, 2, 1).reshape(n_t, 2, n_dp, part // n_dp).transpose(2, 0, 1, 3).reshape(n_dp, n_t, -1),
            gbup.reshape(n_t, n_dp, ff // n_dp).transpose(1, 0, 2),
        ],
        axis=2,
    )
    shard = jnp.roll(shard, tensor, axis=1)
    both = jnp.concatenate([spread, shard], axis=2).reshape(n_dp * n_t, -1)
    mine = lax.psum_scatter(both, ("dp", "tensor"), scatter_dimension=0, tiled=True)[0]
    each = width // (n_dp * n_t)
    vec = mine[0 : 6 * each].reshape(6, each)
    share_b_qv = mine[6 * each : 6 * each + 2 * (part // n_dp)].reshape(2, part // n_dp)
    share_b_up = mine[6 * each + 2 * (part // n_dp) :]
    share_w_qkv = share_a[:, 0 : 3 * part].reshape(rows, 3, part)
    share_w_out = share_a[:, 3 * part :].T
    share_w_up = share_m[:, 0:ff]
    share_w_down = share_m[:, ff:].T
    return (
        block_out,
        grad_inputs,
        vec[0],
        vec[1],
        share_w_qkv,
        share_b_qv,
        share_w_out,
        vec[2],
        vec[3],
        vec[4],
        share_w_up,
        share_b_up,
        share_w_down,
        vec[5],
    )


def solution(mesh):
    return jax.shard_map(
        functools.partial(local, mesh.shape["dp"], mesh.shape["tensor"]),
        mesh=mesh,
        in_specs=(
            P("dp", "tensor", None),
            P("dp", None),
            P(),
            P(),
            P(None, None, "tensor"),
            P(None, "tensor"),
            P("tensor", None),
            P(),
            P(),
            P(),
            P(None, "tensor"),
            P("tensor"),
            P("tensor", None),
            P(),
            P("dp", "tensor", None),
        ),
        out_specs=(
            P("dp", "tensor", None),
            P("dp", "tensor", None),
            P(("dp", "tensor")),
            P(("dp", "tensor")),
            P("dp", None, "tensor"),
            P(None, ("tensor", "dp")),
            P("tensor", "dp"),
            P(("dp", "tensor")),
            P(("dp", "tensor")),
            P(("dp", "tensor")),
            P("dp", "tensor"),
            P(("tensor", "dp")),
            P("tensor", "dp"),
            P(("dp", "tensor")),
        ),
        check_vma=False,
    )
```

```python
import functools

import jax
import jax.numpy as jnp
from jax import lax
from jax.experimental import pallas as pl
from jax.experimental.pallas import tpu as pltpu
from jax.sharding import PartitionSpec as P

BF = jnp.bfloat16
F32 = jnp.float32
HEAD = 64
EPS = 1e-05
GELU_C = 0.7978845608028654
GELU_A = 0.044715
BLOCK = 256
MIB = 1024 * 1024
KEEP = (0, 2, 4, 6)
PAIR = 1


def dot(lhs, rhs, lhs_dim, rhs_dim):
    return lax.dot_general(
        lhs, rhs, (((lhs_dim,), (rhs_dim,)), ((), ())), preferred_element_type=F32
    )


def normalize(value):
    mean = jnp.mean(value, axis=-1, keepdims=True)
    centred = value - mean
    variance = jnp.mean(centred * centred, axis=-1, keepdims=True)
    rstd = lax.rsqrt(variance + EPS)
    return centred * rstd, rstd


def norm_backward(grad, xhat, rstd, gain):
    scaled = grad * gain
    mean_e = jnp.mean(scaled, axis=-1, keepdims=True)
    mean_ex = jnp.mean(scaled * xhat, axis=-1, keepdims=True)
    return rstd * (scaled - mean_e - xhat * mean_ex)


def column(line):
    return jnp.broadcast_to(line, (8, line.shape[1])).T[:, 0:1]


def block_rows(index, size=BLOCK):
    return pl.ds(pl.multiple_of(index * size, size), size)


VMEM = pl.BlockSpec(memory_space=pltpu.VMEM)
SMEM = pl.BlockSpec(memory_space=pltpu.SMEM)
HBM = pl.BlockSpec(memory_space=pl.ANY)


def call(kernel, name, outs, specs, args, out_specs=None, vmem=60, scratch=(), grid=()):
    shapes = tuple(jax.ShapeDtypeStruct(*o) for o in outs)
    return pl.pallas_call(
        kernel,
        grid=grid,
        out_shape=shapes,
        in_specs=specs,
        out_specs=out_specs or (VMEM,) * len(outs),
        scratch_shapes=list(scratch),
        compiler_params=pltpu.CompilerParams(vmem_limit_bytes=vmem * MIB),
        name=name,
        cost_estimate=pl.CostEstimate(flops=1, bytes_accessed=1, transcendentals=0),
    )(*args)


def fixed(shape):
    return pl.BlockSpec(shape, lambda *_: (0,) * len(shape), pipeline_mode=pl.Buffered(1))


def nth(shape, base=0):
    return pl.BlockSpec((1,) + tuple(shape[1:]), lambda t: (lax.rem(t + base, shape[0]),) + (0,) * (len(shape) - 1))


def own_copies(owns, wholes, sems):
    return [
        pltpu.make_async_copy(own, whole.at[0], sems.at[0, i]) for i, (own, whole) in enumerate(zip(owns, wholes))
    ]


def piece_copies(ids_ref, sources, plan, wholes, sems, k, slot):
    copies = []
    for src, (place, arrays) in zip(sources, plan):
        rows = src.shape[3]
        for m in range(src.shape[0]):
            at = pl.multiple_of(ids_ref[place + m] * rows, rows)
            for u, array in enumerate(arrays):
                copies.append(
                    pltpu.make_async_copy(
                        src.at[m, k - 1, u], wholes[array].at[slot, pl.ds(at, rows), :], sems.at[slot, len(copies)]
                    )
                )
    return copies


def piece_count(sources):
    return sum(src.shape[0] * src.shape[2] for src in sources)


def fetch(base, count, step, ids_ref, owns, sources, plan, wholes, sems):
    slot = lax.rem(step, 2)
    begins_own = base == 0

    def start():
        @pl.when(step == 0)
        def _():
            for copy in own_copies(owns, wholes, sems) if begins_own else piece_copies(
                ids_ref, sources, plan, wholes, sems, base, 0
            ):
                copy.start()

        @pl.when(step < count - 1)
        def _():
            for copy in piece_copies(ids_ref, sources, plan, wholes, sems, base + step + 1, lax.rem(step + 1, 2)):
                copy.start()

    def wait():
        if begins_own:
            @pl.when(step == 0)
            def _():
                for copy in own_copies(owns, wholes, sems):
                    copy.wait()

        @pl.when(step > 0 if begins_own else step >= 0)
        def _():
            for copy in piece_copies(ids_ref, sources, plan, wholes, sems, base + step, slot):
                copy.wait()

    return start, wait


def first_kernel(gain_ref, bias_ref, x_ref, n1t_ref):
    xhat, _ = normalize(x_ref[...].astype(F32))
    n1t_ref[...] = (xhat * gain_ref[...] + bias_ref[...]).T.astype(BF)


def first(gain, bias, x):
    seq, width = x.shape
    return call(
        first_kernel,
        "first",
        [((width, seq), BF)],
        [fixed(gain.shape), fixed(bias.shape), pl.BlockSpec((BLOCK, width), lambda i: (i, 0))],
        (gain, bias, x),
        out_specs=(pl.BlockSpec((width, BLOCK), lambda i: (0, i)),),
        grid=(seq // BLOCK,),
    )[0]


def mask_bias(docs_ref, mask_ref):
    seq = mask_ref.shape[0]
    docs = docs_ref[...]
    docs_col = column(docs)
    for begin in range(0, seq, BLOCK):
        end = begin + BLOCK
        same = docs_col[0:end] == docs[:, begin:end]
        place_k = lax.broadcasted_iota(jnp.int32, (end, BLOCK), 0)
        place_q = begin + lax.broadcasted_iota(jnp.int32, (end, BLOCK), 1)
        allowed = same & (place_k <= place_q)
        mask_ref[0:end, begin:end] = jnp.where(allowed, 0.0, -1e30).astype(F32)


def attend_kernel(base, plan, ids_ref, n1t_ref, small_ref, docs_ref, own_ref, *refs):
    sources, (qkvt_ref, at_ref, lse_ref, a_ref, mask_ref, held_ref, sems) = refs[: len(plan)], refs[len(plan) :]
    step = pl.program_id(0)
    start, wait = fetch(base, pl.num_programs(0), step, ids_ref, [own_ref], sources, plan, [held_ref], sems)
    start()
    seq = n1t_ref.shape[1]
    part = at_ref.shape[1]

    @pl.when(pl.program_id(0) == 0)
    def _():
        mask_bias(docs_ref, mask_ref)

    wait()
    a_ref[0] = held_ref[lax.rem(step, 2)]
    proj = dot(a_ref[0, 0 : 3 * part, :], n1t_ref[...], 1, 0)
    qkvt_ref[0, 0:part, :] = (proj[0:part] + column(small_ref[0, 0:1, 0:part])).astype(BF)
    qkvt_ref[0, part : 2 * part, :] = proj[part : 2 * part].astype(BF)
    qkvt_ref[0, 2 * part :, :] = (proj[2 * part :] + column(small_ref[0, 1:2, 0:part])).astype(BF)
    for h in range(part // HEAD):
        q_rows = slice(h * HEAD, (h + 1) * HEAD)
        k_rows = slice(part + h * HEAD, part + (h + 1) * HEAD)
        v_rows = slice(2 * part + h * HEAD, 2 * part + (h + 1) * HEAD)
        keys = qkvt_ref[0, k_rows, :].T
        for begin in range(0, seq, BLOCK):
            end = begin + BLOCK
            q_blk = qkvt_ref[0, q_rows, begin:end] * BF(0.125)
            scores = dot(keys[0:end], q_blk, 1, 0) + mask_ref[0:end, begin:end]
            top = jnp.max(scores, axis=0, keepdims=True)
            expo = jnp.exp(scores - top)
            total = jnp.sum(expo, axis=0, keepdims=True)
            out = dot(qkvt_ref[0, v_rows, 0:end], expo.astype(BF), 1, 0)
            at_ref[0, q_rows, begin:end] = (out / total).astype(BF)
            lse_ref[0, h : h + 1, begin:end] = top + jnp.log(total)


def attend(group, ids, n1t, own_a, sources, plan, smalls, docs):
    width, seq = n1t.shape
    base, count, part = group[0], len(group), own_a.shape[0] // 4
    shapes = [(count, 3 * part, seq), (count, part, seq), (count, 8, seq), (count,) + own_a.shape]
    return call(
        functools.partial(attend_kernel, base, plan),
        "attend",
        [(shapes[0], BF), (shapes[1], BF), (shapes[2], F32), (shapes[3], BF)],
        [SMEM, fixed(n1t.shape), nth(smalls.shape, base), fixed(docs.shape)] + [HBM] * (1 + len(sources)),
        (ids, n1t, smalls, docs, own_a) + tuple(sources),
        out_specs=tuple(nth(s) for s in shapes),
        grid=(count,),
        scratch=[
            pltpu.VMEM((seq, seq), F32),
            pltpu.VMEM((2,) + own_a.shape, BF),
            pltpu.SemaphoreType.DMA((2, piece_count(sources))),
        ],
    )


def split_rows(whole_ref, ids_ref, outs, array=0):
    for g, out in enumerate(outs):
        count, rows = out.shape[0], out.shape[3]
        for m in range(count):
            at = pl.multiple_of(ids_ref[g * count + m] * rows, rows)
            out[m, 0, array] = whole_ref[pl.ds(at, rows), :]


def attend_back_kernel(
    n_split, ids_ref, gmt_ref, n1t_ref, a_ref, qkvt_ref, at_ref, lse_ref, docs_ref, gpt_ref, gb_ref, *refs
):
    splits, (mask_ref, gat_ref, dkv_ref, da_ref) = refs[:n_split], refs[n_split:]
    seq = n1t_ref.shape[1]
    part = at_ref.shape[1]

    @pl.when(pl.program_id(0) == 0)
    def _():
        mask_bias(docs_ref, mask_ref)

    gat_ref[...] = dot(a_ref[0, 3 * part :, :], gmt_ref[...], 1, 0).astype(BF)
    for h in range(part // HEAD):
        q_rows = slice(h * HEAD, (h + 1) * HEAD)
        k_rows = slice(part + h * HEAD, part + (h + 1) * HEAD)
        v_rows = slice(2 * part + h * HEAD, 2 * part + (h + 1) * HEAD)
        keys = qkvt_ref[0, k_rows, :].T
        values = qkvt_ref[0, v_rows, :].T
        for begin in range(0, seq, BLOCK):
            end = begin + BLOCK
            q_blk = qkvt_ref[0, q_rows, begin:end] * BF(0.125)
            g_blk = gat_ref[q_rows, begin:end]
            delta = jnp.sum(
                g_blk.astype(F32) * at_ref[0, q_rows, begin:end].astype(F32), axis=0, keepdims=True
            )
            scores = dot(keys[0:end], q_blk, 1, 0) + mask_ref[0:end, begin:end]
            probs = jnp.exp(scores - lse_ref[0, h : h + 1, begin:end])
            grad_probs = dot(values[0:end], g_blk, 1, 0)
            probs_low = probs.astype(BF)
            grad_scores = (probs * (grad_probs - delta)).astype(BF)
            gpt_ref[0, q_rows, begin:end] = (
                0.125 * dot(qkvt_ref[0, k_rows, 0:end], grad_scores, 1, 0)
            ).astype(BF)
            gk = dot(q_blk, grad_scores, 1, 1)
            gv = dot(g_blk, probs_low, 1, 1)
            if begin > 0:
                dkv_ref[0:HEAD, 0:begin] += gk[:, 0:begin]
                dkv_ref[HEAD:, 0:begin] += gv[:, 0:begin]
            dkv_ref[0:HEAD, begin:end] = gk[:, begin:end]
            dkv_ref[HEAD:, begin:end] = gv[:, begin:end]
        gpt_ref[0, k_rows, :] = dkv_ref[0:HEAD, :].astype(BF)
        gpt_ref[0, v_rows, :] = dkv_ref[HEAD:, :].astype(BF)
    ones = jnp.ones((8, seq), BF)
    gb_ref[0, 0:1, :] = dot(ones, gpt_ref[0, 0:part, :], 1, 1)[0:1]
    gb_ref[0, 1:2, :] = dot(ones, gpt_ref[0, 2 * part : 3 * part, :], 1, 1)[0:1]
    da_ref[:, 0 : 3 * part] = dot(n1t_ref[...], gpt_ref[0], 1, 1).astype(BF)
    da_ref[:, 3 * part :] = dot(gmt_ref[...], at_ref[0], 1, 1).astype(BF)
    split_rows(da_ref, ids_ref, splits)


def attend_back(splits, ids, gmt, n1t, qkvt, at, lse, a_part, docs):
    width, seq = n1t.shape
    part = at.shape[1]
    n_split, blocks = splits
    count = at.shape[0]
    cut = (blocks, count, 1, width // (n_split * blocks), 4 * part)
    cut_spec = pl.BlockSpec((blocks, 1) + cut[2:], lambda t: (0, t, 0, 0, 0))
    return call(
        functools.partial(attend_back_kernel, n_split),
        "attend_back",
        [((count, 3 * part, seq), BF), ((count, 2, part), F32)] + [(cut, BF)] * n_split,
        [SMEM, fixed(gmt.shape), fixed(n1t.shape), nth(a_part.shape), nth(qkvt.shape), nth(at.shape),
         nth(lse.shape), fixed(docs.shape)],
        (ids, gmt, n1t, a_part, qkvt, at, lse, docs),
        out_specs=(nth((count, 3 * part, seq)), nth((count, 2, part))) + (cut_spec,) * n_split,
        grid=(count,),
        scratch=[
            pltpu.VMEM((seq, seq), F32),
            pltpu.VMEM((part, seq), BF),
            pltpu.VMEM((2 * HEAD, seq), F32),
            pltpu.VMEM((width, 4 * part), BF),
        ],
    )


def mlp_kernel(
    n_t, n_split, plan, ids_ref, x_ref, at_one_ref, at_two_ref, out_one_ref, out_two_ref, small_ref,
    out_bias_ref, gain_ref, bias_ref, down_bias_ref, own_up_ref, own_down_ref, *refs
):
    sources, refs = refs[: len(plan)], refs[len(plan) :]
    cot_ref, out_ref, *refs = refs
    gm_ref, gmt_ref, gvec_ref, gbup_ref = refs[:4]
    splits = refs[4 : 4 + n_split]
    (mixed_ref, n2_ref, n2t_ref, cott_ref, total_ref, grad_ref, act_ref, gpre_ref, dm_ref,
     up_all_ref, down_all_ref, sems) = refs[4 + n_split :]
    seq, width = x_ref.shape
    step_t = pl.program_id(0)
    blocks = seq // BLOCK
    slot = lax.rem(step_t, 2)
    wholes = [up_all_ref, down_all_ref]
    start, wait = fetch(0, n_t, step_t, ids_ref, [own_up_ref, own_down_ref], sources, plan, wholes, sems)
    up_ref, down_ref = up_all_ref.at[slot], down_all_ref.at[slot]
    start()

    @pl.when(step_t == 0)
    def _():
        gvec_ref[...] = jnp.zeros_like(gvec_ref)

        @pl.loop(0, blocks)
        def _(step):
            rows = block_rows(step)
            total = x_ref[rows, :].astype(F32) + out_bias_ref[...]
            for at_ref, w_out_ref in ((at_one_ref, out_one_ref), (at_two_ref, out_two_ref)):
                for t in range(at_ref.shape[0]):
                    total += dot(at_ref[t, :, rows].T, w_out_ref[t], 1, 0)
            mixed_ref[rows, :] = total
            xhat, _ = normalize(total)
            normed = (xhat * gain_ref[...] + bias_ref[...]).astype(BF)
            n2_ref[rows, :] = normed
            n2t_ref[:, rows] = normed.T
            held = cot_ref[rows, :]
            cott_ref[:, rows] = held.T
            gvec_ref[3:4, :] += jnp.sum(held.astype(F32), axis=0, keepdims=True)
            total_ref[rows, :] = jnp.zeros((BLOCK, width), F32)
            grad_ref[rows, :] = jnp.zeros((BLOCK, width), F32)

    wait()
    bias = small_ref[0, 2:3, :]

    def one(step, sums):
        rows = block_rows(step)
        pre = dot(n2_ref[rows, :], up_ref[...], 1, 0) + bias
        grad_act = dot(cot_ref[rows, :], down_ref[...], 1, 1)
        square = pre * pre
        curve = jnp.tanh(pre * (GELU_C + (GELU_C * GELU_A) * square))
        half = 0.5 + 0.5 * curve
        act = (pre * half).astype(BF)
        slope = half + (half - half * curve) * pre * (GELU_C + (3 * GELU_C * GELU_A) * square)
        grad_pre = (slope * grad_act).astype(BF)
        act_ref[rows, :] = act
        gpre_ref[rows, :] = grad_pre
        total_ref[rows, :] += dot(act, down_ref[...], 1, 0)
        grad_ref[rows, :] += dot(grad_pre, up_ref[...], 1, 1)
        return sums + jnp.sum(grad_pre.astype(F32), axis=0, keepdims=True)

    gbup_ref[0] = lax.fori_loop(0, blocks, one, jnp.zeros(bias.shape, F32), unroll=True)
    dm_ref[...] = dot(n2t_ref[...], gpre_ref[...], 1, 0).astype(BF)
    split_rows(dm_ref, ids_ref, splits, 0)
    dm_ref[...] = dot(cott_ref[...], act_ref[...], 1, 0).astype(BF)
    split_rows(dm_ref, ids_ref, splits, 1)

    @pl.when(step_t == n_t - 1)
    def _():
        @pl.loop(0, blocks)
        def _(step):
            rows = block_rows(step)
            xhat, rstd = normalize(mixed_ref[rows, :])
            grad_n = grad_ref[rows, :]
            grad_mixed = cot_ref[rows, :].astype(F32) + norm_backward(grad_n, xhat, rstd, gain_ref[...])
            gm_ref[rows, :] = grad_mixed
            gmt_ref[:, rows] = grad_mixed.T.astype(BF)
            gvec_ref[0:1, :] += jnp.sum(grad_mixed, axis=0, keepdims=True)
            gvec_ref[1:2, :] += jnp.sum(grad_n * xhat, axis=0, keepdims=True)
            gvec_ref[2:3, :] += jnp.sum(grad_n, axis=0, keepdims=True)
            out_ref[rows, :] = (mixed_ref[rows, :] + total_ref[rows, :] + down_bias_ref[...]).astype(BF)


def mlp(splits, ids, x, at_one, at_two, a_one, a_two, w_up, w_down, sources, plan, smalls, vecs, cot):
    seq, width = x.shape
    n_t, part = at_one.shape[0] + at_two.shape[0], at_one.shape[1]
    ff = w_up.shape[1]
    n_split, blocks = splits
    cut = (blocks, n_t, 2, width // (n_split * blocks), ff)
    cut_spec = pl.BlockSpec((blocks, 1) + cut[2:], lambda t: (0, t, 0, 0, 0))
    gbup = (n_t, 1, ff)
    return call(
        functools.partial(mlp_kernel, n_t, n_split, plan),
        "mlp",
        [((seq, width), BF), ((seq, width), F32), ((width, seq), BF), ((8, width), F32), (gbup, F32)]
        + [(cut, BF)] * n_split,
        [SMEM, fixed(x.shape), fixed(at_one.shape), fixed(at_two.shape),
         *[pl.BlockSpec((a.shape[0], part, width), lambda t: (0, 3, 0), pipeline_mode=pl.Buffered(1)) for a in (a_one, a_two)],
         nth(smalls.shape)] + [fixed((1, width))] * 4 + [HBM] * (2 + len(sources)) + [fixed(cot.shape)],
        (ids, x, at_one, at_two, a_one, a_two, smalls) + tuple(vecs) + (w_up, w_down) + tuple(sources) + (cot,),
        out_specs=(fixed((seq, width)), fixed((seq, width)), fixed((width, seq)), fixed((8, width)), nth(gbup))
        + (cut_spec,) * n_split,
        grid=(n_t,),
        scratch=[
            pltpu.VMEM((seq, width), F32),
            pltpu.VMEM((seq, width), BF),
            pltpu.VMEM((width, seq), BF),
            pltpu.VMEM((width, seq), BF),
            pltpu.VMEM((seq, width), F32),
            pltpu.VMEM((seq, width), F32),
            pltpu.VMEM((seq, ff), BF),
            pltpu.VMEM((seq, ff), BF),
            pltpu.VMEM((width, ff), BF),
            pltpu.VMEM((2, width, ff), BF),
            pltpu.VMEM((2, ff, width), BF),
            pltpu.SemaphoreType.DMA((2, max(2, piece_count(sources)))),
        ],
    )


def input_back_kernel(x_ref, gm_ref, gain_ref, a_one_ref, a_two_ref, one_ref, two_ref, out_ref, gvec_ref):

    @pl.when(pl.program_id(0) == 0)
    def _():
        gvec_ref[...] = jnp.zeros_like(gvec_ref)

    grad_n = None
    for gpt_ref, a_ref in ((one_ref, a_one_ref), (two_ref, a_two_ref)):
        for t in range(gpt_ref.shape[0]):
            share = dot(gpt_ref[t].T, a_ref[t], 1, 0)
            grad_n = share if grad_n is None else grad_n + share
    xhat, rstd = normalize(x_ref[...].astype(F32))
    out_ref[...] = (gm_ref[...] + norm_backward(grad_n, xhat, rstd, gain_ref[...])).astype(BF)
    gvec_ref[0:1, :] += jnp.sum(grad_n * xhat, axis=0, keepdims=True)
    gvec_ref[1:2, :] += jnp.sum(grad_n, axis=0, keepdims=True)


def input_back(x, gm, gain, a_one, a_two, one, two):
    seq, width = x.shape
    part3 = one.shape[1]
    by_rows = pl.BlockSpec((BLOCK, width), lambda i: (i, 0))

    def by_columns(gpt):
        return pl.BlockSpec(gpt.shape[:2] + (BLOCK,), lambda i: (0, 0, i))

    return call(
        input_back_kernel,
        "input_back",
        [((seq, width), BF), ((8, width), F32)],
        [by_rows, by_rows, fixed(gain.shape), fixed((one.shape[0], part3, width)), fixed((two.shape[0], part3, width)),
         by_columns(one), by_columns(two)],
        (x, gm, gain, a_one, a_two, one, two),
        out_specs=(by_rows, fixed((8, width))),
        grid=(seq // BLOCK,),
    )


def trade(value):
    return lax.all_to_all(value, "tensor", 0, 0, tiled=True)


def turn(value, by):
    return jnp.roll(value, -by, axis=0)


def swap(value, n_dp, mask):
    return lax.ppermute(value, "dp", [(i, i ^ mask) for i in range(n_dp)])


def after(value, *others):
    return lax.optimization_barrier((value,) + others)[0]


def chip_pieces(pieces, n_dp):
    if n_dp != 8:
        return [(lax.all_gather(pieces, "dp", axis=2, tiled=True), 0, tuple(range(pieces.shape[1])))]
    arrays = tuple(range(pieces.shape[1]))
    if len(arrays) == 1:
        return [(pieces, 0, arrays)] + [(swap(pieces, n_dp, mask), m + 1, arrays) for m, mask in enumerate(KEEP[1:])]
    by_x, by_y = swap(pieces, n_dp, KEEP[1]), swap(pieces, n_dp, KEEP[2])
    first_far = swap(by_y[:, 0:1], n_dp, KEEP[1])
    second_far = swap(by_x[:, 1:2], n_dp, KEEP[2])
    return [(pieces, 0, arrays), (by_x, 1, arrays), (by_y, 2, arrays), (first_far, 3, (0,)), (second_far, 3, (1,))]


def pair_pieces(mine, n_dp):
    if n_dp != 8:
        return [value[None] for value, _, _ in mine], tuple((place, arrays) for _, place, arrays in mine)
    both = mine + [(swap(value, n_dp, PAIR), place + len(KEEP), arrays) for value, place, arrays in mine]
    return [value[None] for value, _, _ in both], tuple((place, arrays) for _, place, arrays in both)


def pair_swap(parts, n_dp):
    return [swap(parts[1], n_dp, PAIR)] if n_dp == 8 else []


def pair_sum(parts, got, places, select):
    return [parts[0][p][select].astype(F32) + got[0][p][select].astype(F32) for p in places]


def chip_send(parts, got, n_dp, near, far, select):
    if n_dp != 8:
        whole = parts[0][0][select]
        return lax.psum_scatter(whole, "dp", scatter_dimension=whole.ndim - 2, tiled=True)
    return swap(jnp.stack(pair_sum(parts, got, (near, 3), select)).astype(BF), n_dp, KEEP[near])


def chip_pass(parts, got, sent, n_dp, near, far, select):
    if n_dp != 8:
        return [sent]
    here, there = pair_sum(parts, got, (0, far), select)
    here = here + sent[0].astype(F32)
    there = (there + sent[1].astype(F32)).astype(BF)
    return [here, swap(there, n_dp, KEEP[far])]


def chip_sum(terms):
    total = terms[0].astype(F32)
    for item in terms[1:]:
        total += item.astype(F32)
    return total


def in_parts(value):
    high = value.astype(BF)
    rest = value - high.astype(F32)
    middle = rest.astype(BF)
    return [high, middle, (rest - middle.astype(F32)).astype(BF)]


def small_vectors(b_qv, b_up):
    value = jnp.concatenate([jnp.pad(b_qv, ((0, 0), (0, b_up.shape[0] - b_qv.shape[1]))), b_up[None]])
    return jnp.concatenate(in_parts(value) + [jnp.zeros((7,) + b_up.shape, BF)])


def local(n_dp, n_t, inputs, doc_ids, ln1_gain, ln1_bias, w_qkv, b_qv, w_out, out_bias, ln2_gain, ln2_bias,
          w_up, b_up, w_down, down_bias, cotangent):
    width = inputs.shape[2]
    part, ff = w_out.shape[0], w_up.shape[1]
    dp = lax.axis_index("dp")
    tensor = lax.axis_index("tensor")
    own_rows = inputs.shape[0] // n_t
    rows = width // n_dp
    each_row = range(own_rows)
    splits = (2, 4) if n_dp == 8 else (1, 1)
    order = jnp.array(KEEP + tuple(m ^ PAIR for m in KEEP), jnp.int32)
    ids = order ^ dp if n_dp == 8 else jnp.zeros_like(order)
    half = n_t // 2
    groups = (tuple(range(half)), tuple(range(half, n_t)))

    def own_piece(whole):
        return lax.dynamic_slice_in_dim(whole, dp * rows, rows, 0)

    def others(gathered):
        return turn(gathered, tensor + 1)[: n_t - 1]

    def split_row(values):
        values = values.reshape((n_t, own_rows) + values.shape[1:])
        return [values[:, r].reshape(-1, width) for r in each_row]

    def join_row(values):
        blocks = jnp.stack([v.reshape(n_t, -1, width) for v in values], axis=1)
        return blocks.reshape((n_t * own_rows,) + blocks.shape[2:])

    own_a = jnp.concatenate([w_qkv.transpose(1, 2, 0).reshape(3 * part, width), w_out])
    pieces = jnp.concatenate([own_piece(own_a), own_piece(w_up), own_piece(w_down), small_vectors(b_qv, b_up)])
    gathered = trade(jnp.broadcast_to(pieces[None], (n_t,) + pieces.shape))
    smalls = turn(gathered[:, 3 * rows :].astype(F32), tensor)
    smalls = smalls[:, 0:3] + smalls[:, 3:6] + smalls[:, 6:9]
    stack_a, stack_m = others(gathered[:, :rows])[:, None], others(gathered[:, rows : 3 * rows])
    stack_m = stack_m.reshape(n_t - 1, 2, rows, width)
    mine_a = chip_pieces(stack_a, n_dp)
    x_rows = split_row(trade(after(inputs, gathered)))
    mine_m = chip_pieces(after(stack_m, [m[0] for m in mine_a]), n_dp)
    sources_a, plan_a = pair_pieces(mine_a, n_dp)
    cot_rows = split_row(trade(after(cotangent, x_rows)))
    vecs = [v[None] for v in (out_bias, ln2_gain, ln2_bias, down_bias)]
    doc_rows = lax.dynamic_slice_in_dim(doc_ids, tensor * own_rows, own_rows, 0)
    docs = [doc_rows[r : r + 1] for r in each_row]

    def total_of(*items):
        if len(items) == 1:
            return items[0]
        return sum(item.astype(F32) for item in items).astype(items[0].dtype)

    def together(results):
        return [jax.tree.map(total_of, *items) for items in zip(*results)]

    n1ts = [first(ln1_gain[None], ln1_bias[None], x) for x in x_rows]
    seen_one = [attend(groups[0], ids, n1ts[r], own_a, sources_a, plan_a, smalls, docs[r]) for r in each_row]
    n1ts, values_m = lax.optimization_barrier((n1ts, [m[0] for m in mine_m], seen_one))[:2]
    mine_m = [(value,) + m[1:] for value, m in zip(values_m, mine_m)]
    sources_m, plan_m = pair_pieces(mine_m, n_dp)
    seen_two = [attend(groups[1], ids, n1ts[r], own_a, sources_a, plan_a, smalls, docs[r]) for r in each_row]
    sources_m, cot_rows = lax.optimization_barrier((sources_m, cot_rows, seen_two))[:2]
    made = [
        mlp(splits, ids, x_rows[r], seen_one[r][1], seen_two[r][1], seen_one[r][3], seen_two[r][3], w_up, w_down,
            sources_m, plan_m, smalls, vecs, cot_rows[r])
        for r in each_row
    ]
    gvec, gbup, *dms = together([m[3:] for m in made])
    got_m = pair_swap(dms, n_dp)
    block_out = trade(join_row([m[0] for m in made]))

    def back(gmts, seen):
        items = [attend_back(splits, ids, gmts[r], n1ts[r], *seen[r], docs[r]) for r in each_row]
        return [i[0] for i in items], together([i[1:] for i in items])

    up_way, down_way = (1, 2, (slice(None), 0)), (2, 1, (slice(None), 1))
    one_way, two_way = (1, 2, ()), (2, 1, ())
    gmts = [m[2] for m in made]
    gpt_two, (gb_two, *da_two) = back(gmts, seen_two)
    got_m, dms = lax.optimization_barrier((got_m, dms, gpt_two))[:2]
    sent_m = [chip_send(dms, got_m, n_dp, *way) for way in (up_way, down_way)]
    got_two = pair_swap(da_two, n_dp)
    gmts, dms, got_m = lax.optimization_barrier((gmts, dms, got_m, gpt_two))[:3]
    gpt_one, (gb_one, *da_one) = back(gmts, seen_one)
    got_one = pair_swap(da_one, n_dp)
    block_out, got_two, sent_m, dms, got_m = lax.optimization_barrier(
        (block_out, got_two, sent_m, dms, got_m, gpt_one)
    )[:5]
    passed_m = [chip_pass(dms, got_m, sent, n_dp, *way) for sent, way in zip(sent_m, (up_way, down_way))]
    gms = lax.optimization_barrier(([m[1] for m in made], gpt_one, block_out, sent_m))[0]
    ends = [
        input_back(x_rows[r], gms[r], ln1_gain[None], seen_two[r][3], seen_one[r][3], gpt_two[r], gpt_one[r])
        for r in each_row
    ]
    (gin,) = together([e[1:] for e in ends])
    grad_inputs = trade(join_row([e[0] for e in ends]))
    got_one, got_two, passed_m = lax.optimization_barrier((got_one, got_two, passed_m, ends))[:3]
    sent_one = chip_send(da_one, got_one, n_dp, *one_way)
    sent_two = chip_send(da_two, got_two, n_dp, *two_way)
    passed_one = chip_pass(da_one, got_one, sent_one, n_dp, *one_way)
    passed_two = chip_pass(da_two, got_two, sent_two, n_dp, *two_way)

    def shard_sum(summed):
        return jnp.sum(trade(turn(summed.astype(BF), -tensor)).astype(F32), axis=0)

    sums_m = jnp.concatenate([chip_sum(passed) for passed in passed_m], axis=1)
    sums_a = jnp.concatenate([chip_sum(passed_one), chip_sum(passed_two)])[:, 0]
    gbs = jnp.concatenate([gb_one, gb_two])

    each = width // (n_dp * n_t)
    vectors = jnp.concatenate([gin[0:2], gvec[0:4]])
    vectors = vectors.reshape(6, n_dp, n_t, each).transpose(1, 2, 0, 3).reshape(n_dp, n_t, 6 * each)
    shard = jnp.concatenate(
        [
            gbs.reshape(n_t, 2, n_dp, part // n_dp).transpose(2, 0, 1, 3).reshape(n_dp, n_t, -1),
            gbup.reshape(n_t, n_dp, ff // n_dp).transpose(1, 0, 2),
        ],
        axis=2,
    )
    both = jnp.concatenate([vectors, jnp.roll(shard, tensor, axis=1)], axis=2)
    if n_dp == 8:
        for mask in (1, 2, 4):
            bit = (dp // mask) % 2
            split = both.reshape((both.shape[0] // 2, 2) + both.shape[1:])
            kept = lax.dynamic_index_in_dim(split, bit, 1, keepdims=False)
            sent = lax.dynamic_index_in_dim(split, 1 - bit, 1, keepdims=False)
            both = kept + swap(sent, n_dp, mask)
        both = both[0]
    else:
        both = lax.psum_scatter(both, "dp", scatter_dimension=0, tiled=False)
    parts = turn(jnp.concatenate([p[:, None] for p in in_parts(both)], axis=1), tensor)
    parts = jnp.pad(parts, ((0, 0), (0, 13), (0, width - parts.shape[2])))
    share = shard_sum(after(jnp.concatenate([sums_a.astype(BF), sums_m.astype(BF), parts], axis=1), grad_inputs))
    share_a, share_up, share_down = (share[i * rows : (i + 1) * rows] for i in range(3))
    mine = jnp.sum(share[3 * rows : 3 * rows + 3, 0 : both.shape[1]], axis=0)
    vec_out = mine[0 : 6 * each].reshape(6, each)
    share_b_qv = mine[6 * each : 6 * each + 2 * (part // n_dp)].reshape(2, part // n_dp)
    share_b_up = mine[6 * each + 2 * (part // n_dp) :]
    share_w_qkv = share_a[:, 0 : 3 * part].reshape(rows, 3, part)
    share_w_out = share_a[:, 3 * part :].T
    return (
        block_out,
        grad_inputs,
        vec_out[0],
        vec_out[1],
        share_w_qkv,
        share_b_qv,
        share_w_out,
        vec_out[2],
        vec_out[3],
        vec_out[4],
        share_up,
        share_b_up,
        share_down.T,
        vec_out[5],
    )


def solution(mesh):
    return jax.shard_map(
        functools.partial(local, mesh.shape["dp"], mesh.shape["tensor"]),
        mesh=mesh,
        in_specs=(
            P("dp", "tensor", None),
            P("dp", None),
            P(),
            P(),
            P(None, None, "tensor"),
            P(None, "tensor"),
            P("tensor", None),
            P(),
            P(),
            P(),
            P(None, "tensor"),
            P("tensor"),
            P("tensor", None),
            P(),
            P("dp", "tensor", None),
        ),
        out_specs=(
            P("dp", "tensor", None),
            P("dp", "tensor", None),
            P(("dp", "tensor")),
            P(("dp", "tensor")),
            P("dp", None, "tensor"),
            P(None, ("tensor", "dp")),
            P("tensor", "dp"),
            P(("dp", "tensor")),
            P(("dp", "tensor")),
            P(("dp", "tensor")),
            P("dp", "tensor"),
            P(("tensor", "dp")),
            P("tensor", "dp"),
            P(("dp", "tensor")),
        ),
        check_vma=False,
    )
```

```python
import functools

import jax
import jax.numpy as jnp
from jax import lax
from jax.experimental import pallas as pl
from jax.experimental.pallas import tpu as pltpu
from jax.sharding import PartitionSpec as P

BF = jnp.bfloat16
F32 = jnp.float32
HEAD = 64
EPS = 1e-05
GELU_C = 0.7978845608028654
GELU_A = 0.044715
BLOCK = 256
MIB = 1024 * 1024
KEEP = (0, 2, 4, 6)
PAIR = 1


def dot(lhs, rhs, lhs_dim, rhs_dim):
    return lax.dot_general(
        lhs, rhs, (((lhs_dim,), (rhs_dim,)), ((), ())), preferred_element_type=F32
    )


def normalize(value):
    mean = jnp.mean(value, axis=-1, keepdims=True)
    centred = value - mean
    variance = jnp.mean(centred * centred, axis=-1, keepdims=True)
    rstd = lax.rsqrt(variance + EPS)
    return centred * rstd, rstd


def norm_backward(grad, xhat, rstd, gain):
    scaled = grad * gain
    mean_e = jnp.mean(scaled, axis=-1, keepdims=True)
    mean_ex = jnp.mean(scaled * xhat, axis=-1, keepdims=True)
    return rstd * (scaled - mean_e - xhat * mean_ex)


def column(line):
    return jnp.broadcast_to(line, (8, line.shape[1])).T[:, 0:1]


def block_rows(index, size=BLOCK):
    return pl.ds(pl.multiple_of(index * size, size), size)


VMEM = pl.BlockSpec(memory_space=pltpu.VMEM)
SMEM = pl.BlockSpec(memory_space=pltpu.SMEM)
HBM = pl.BlockSpec(memory_space=pl.ANY)


def call(kernel, name, outs, specs, args, out_specs=None, vmem=60, scratch=(), grid=()):
    shapes = tuple(jax.ShapeDtypeStruct(*o) for o in outs)
    return pl.pallas_call(
        kernel,
        grid=grid,
        out_shape=shapes,
        in_specs=specs,
        out_specs=out_specs or (VMEM,) * len(outs),
        scratch_shapes=list(scratch),
        compiler_params=pltpu.CompilerParams(vmem_limit_bytes=vmem * MIB),
        name=name,
        cost_estimate=pl.CostEstimate(flops=1, bytes_accessed=1, transcendentals=0),
    )(*args)


def fixed(shape):
    return pl.BlockSpec(shape, lambda *_: (0,) * len(shape), pipeline_mode=pl.Buffered(1))


def nth(shape, base=0):
    return pl.BlockSpec((1,) + tuple(shape[1:]), lambda t: (lax.rem(t + base, shape[0]),) + (0,) * (len(shape) - 1))


def own_copies(owns, wholes, sems):
    return [
        pltpu.make_async_copy(own, whole.at[0], sems.at[0, i]) for i, (own, whole) in enumerate(zip(owns, wholes))
    ]


def piece_copies(ids_ref, sources, plan, wholes, sems, k, slot):
    copies = []
    for src, (place, arrays) in zip(sources, plan):
        rows = src.shape[3]
        for m in range(src.shape[0]):
            at = pl.multiple_of(ids_ref[place + m] * rows, rows)
            for u, array in enumerate(arrays):
                copies.append(
                    pltpu.make_async_copy(
                        src.at[m, u, k - 1], wholes[array].at[slot, pl.ds(at, rows), :], sems.at[slot, len(copies)]
                    )
                )
    return copies


def piece_count(sources):
    return sum(src.shape[0] * src.shape[1] for src in sources)


def fetch(base, count, step, ids_ref, owns, sources, plan, wholes, sems):
    slot = lax.rem(step, 2)
    begins_own = base == 0

    def start():
        @pl.when(step == 0)
        def _():
            for copy in own_copies(owns, wholes, sems) if begins_own else piece_copies(
                ids_ref, sources, plan, wholes, sems, base, 0
            ):
                copy.start()

        @pl.when(step < count - 1)
        def _():
            for copy in piece_copies(ids_ref, sources, plan, wholes, sems, base + step + 1, lax.rem(step + 1, 2)):
                copy.start()

    def wait():
        if begins_own:
            @pl.when(step == 0)
            def _():
                for copy in own_copies(owns, wholes, sems):
                    copy.wait()

        @pl.when(step > 0 if begins_own else step >= 0)
        def _():
            for copy in piece_copies(ids_ref, sources, plan, wholes, sems, base + step, slot):
                copy.wait()

    return start, wait


def first_kernel(gain_ref, bias_ref, x_ref, n1t_ref):
    xhat, _ = normalize(x_ref[...].astype(F32))
    n1t_ref[...] = (xhat * gain_ref[...] + bias_ref[...]).astype(BF).T


def first(gain, bias, x):
    seq, width = x.shape
    return call(
        first_kernel,
        "first",
        [((width, seq), BF)],
        [fixed(gain.shape), fixed(bias.shape), pl.BlockSpec((BLOCK, width), lambda i: (i, 0))],
        (gain, bias, x),
        out_specs=(pl.BlockSpec((width, BLOCK), lambda i: (0, i)),),
        grid=(seq // BLOCK,),
    )[0]


def mask_bias(docs_ref, mask_ref):
    seq = mask_ref.shape[0]
    docs = docs_ref[...]
    docs_col = column(docs)
    for begin in range(0, seq, BLOCK):
        end = begin + BLOCK
        same = docs_col[0:end] == docs[:, begin:end]
        place_k = lax.broadcasted_iota(jnp.int32, (end, BLOCK), 0)
        place_q = begin + lax.broadcasted_iota(jnp.int32, (end, BLOCK), 1)
        allowed = same & (place_k <= place_q)
        mask_ref[0:end, begin:end] = jnp.where(allowed, 0.0, -1e30).astype(F32)


def attend_kernel(base, plan, ids_ref, n1t_ref, small_ref, docs_ref, own_ref, *refs):
    sources, (qkvt_ref, at_ref, lse_ref, a_ref, mask_ref, held_ref, sems) = refs[: len(plan)], refs[len(plan) :]
    step = pl.program_id(0)
    start, wait = fetch(base, pl.num_programs(0), step, ids_ref, [own_ref], sources, plan, [held_ref], sems)
    start()
    seq = n1t_ref.shape[1]
    part = at_ref.shape[1]

    @pl.when(pl.program_id(0) == 0)
    def _():
        mask_bias(docs_ref, mask_ref)

    wait()
    a_ref[0] = held_ref[lax.rem(step, 2)]
    proj = dot(a_ref[0, 0 : 3 * part, :], n1t_ref[...], 1, 0)
    qkvt_ref[0, 0:part, :] = (proj[0:part] + column(small_ref[0, 0:1, 0:part])).astype(BF)
    qkvt_ref[0, part : 2 * part, :] = proj[part : 2 * part].astype(BF)
    qkvt_ref[0, 2 * part :, :] = (proj[2 * part :] + column(small_ref[0, 1:2, 0:part])).astype(BF)
    heads = range(part // HEAD)

    def rows_of(which, h):
        return slice(which * part + h * HEAD, which * part + (h + 1) * HEAD)

    keys = [qkvt_ref[0, rows_of(1, h), :].T for h in heads]
    values = [jnp.concatenate([qkvt_ref[0, rows_of(2, h), :], jnp.ones((16, seq), BF)]) for h in heads]

    def scores_of(begin):
        end = begin + BLOCK
        mask = mask_ref[0:end, begin:end]
        return [dot(keys[h][0:end], qkvt_ref[0, rows_of(0, h), begin:end] * BF(0.125), 1, 0) + mask for h in heads]

    scores = scores_of(0)
    for begin in range(0, seq, BLOCK):
        end = begin + BLOCK
        now = scores
        top = [jnp.max(s, axis=0, keepdims=True) for s in now]
        if end < seq:
            scores = scores_of(end)
        expo = [jnp.exp(s - t).astype(BF) for s, t in zip(now, top)]
        out = [dot(values[h][:, 0:end], expo[h], 1, 0) for h in heads]
        for h in heads:
            total = out[h][HEAD : HEAD + 1]
            at_ref[0, h * HEAD : (h + 1) * HEAD, begin:end] = (out[h][0:HEAD] / total).astype(BF)
            lse_ref[0, h : h + 1, begin:end] = top[h] + jnp.log(total)


def attend(group, ids, n1t, own_a, sources, plan, smalls, docs):
    width, seq = n1t.shape
    base, count, part = group[0], len(group), own_a.shape[0] // 4
    shapes = [(count, 3 * part, seq), (count, part, seq), (count, 8, seq), (count,) + own_a.shape]
    return call(
        functools.partial(attend_kernel, base, plan),
        "attend",
        [(shapes[0], BF), (shapes[1], BF), (shapes[2], F32), (shapes[3], BF)],
        [SMEM, fixed(n1t.shape), nth(smalls.shape, base), fixed(docs.shape)] + [HBM] * (1 + len(sources)),
        (ids, n1t, smalls, docs, own_a) + tuple(sources),
        out_specs=tuple(nth(s) for s in shapes),
        grid=(count,),
        scratch=[
            pltpu.VMEM((seq, seq), F32),
            pltpu.VMEM((2,) + own_a.shape, BF),
            pltpu.SemaphoreType.DMA((2, piece_count(sources))),
        ],
    )


def split_rows(whole_ref, ids_ref, outs, array=0):
    for g, out in enumerate(outs):
        count, rows = out.shape[1], out.shape[3]
        for m in range(count):
            at = pl.multiple_of(ids_ref[g * count + m] * rows, rows)
            out[array, m, 0] = whole_ref[pl.ds(at, rows), :]


def attend_back_kernel(
    n_split, ids_ref, gmt_ref, n1t_ref, a_ref, qkvt_ref, at_ref, lse_ref, docs_ref, gpt_ref, gb_ref, *refs
):
    splits, (mask_ref, gat_ref, dkv_ref, da_ref) = refs[:n_split], refs[n_split:]
    seq = n1t_ref.shape[1]
    part = at_ref.shape[1]

    @pl.when(pl.program_id(0) == 0)
    def _():
        mask_bias(docs_ref, mask_ref)

    gat_ref[...] = dot(a_ref[0, 3 * part :, :], gmt_ref[...], 1, 0).astype(BF)
    heads = range(part // HEAD)

    def rows_of(which, h):
        return slice(which * part + h * HEAD, which * part + (h + 1) * HEAD)

    keys = [qkvt_ref[0, rows_of(1, h), :].T for h in heads]
    values = [qkvt_ref[0, rows_of(2, h), :].T for h in heads]
    items = [(begin, h) for begin in range(0, seq, BLOCK) for h in heads]

    def begin_item(begin, h):
        end = begin + BLOCK
        query = qkvt_ref[0, rows_of(0, h), begin:end] * BF(0.125)
        grad = gat_ref[rows_of(0, h), begin:end]
        scores = dot(keys[h][0:end], query, 1, 0) + mask_ref[0:end, begin:end]
        return query, grad, scores, dot(values[h][0:end], grad, 1, 0)

    ahead = begin_item(*items[0])
    for i, (begin, h) in enumerate(items):
        end = begin + BLOCK
        query, grad, scores, grad_probs = ahead
        if i + 1 < len(items):
            ahead = begin_item(*items[i + 1])
        delta = jnp.sum(
            grad.astype(F32) * at_ref[0, rows_of(0, h), begin:end].astype(F32), axis=0, keepdims=True
        )
        probs = jnp.exp(scores - lse_ref[0, h : h + 1, begin:end])
        grad_scores = (probs * (grad_probs - delta)).astype(BF)
        gpt_ref[0, rows_of(0, h), begin:end] = (
            0.125 * dot(qkvt_ref[0, rows_of(1, h), 0:end], grad_scores, 1, 0)
        ).astype(BF)
        for which, share in ((0, dot(query, grad_scores, 1, 1)), (1, dot(grad, probs.astype(BF), 1, 1))):
            if begin > 0:
                dkv_ref[h, which, :, 0:begin] += share[:, 0:begin]
            dkv_ref[h, which, :, begin:end] = share[:, begin:end]
    for h in heads:
        for which in range(2):
            gpt_ref[0, rows_of(1 + which, h), :] = dkv_ref[h, which].astype(BF)
    ones = jnp.ones((8, seq), BF)
    gb_ref[0, 0:1, :] = dot(ones, gpt_ref[0, 0:part, :], 1, 1)[0:1]
    gb_ref[0, 1:2, :] = dot(ones, gpt_ref[0, 2 * part : 3 * part, :], 1, 1)[0:1]
    da_ref[:, 0 : 3 * part] = dot(n1t_ref[...], gpt_ref[0], 1, 1).astype(BF)
    da_ref[:, 3 * part :] = dot(gmt_ref[...], at_ref[0], 1, 1).astype(BF)
    split_rows(da_ref, ids_ref, splits)


def attend_back(splits, ids, gmt, n1t, qkvt, at, lse, a_part, docs):
    width, seq = n1t.shape
    part = at.shape[1]
    n_split, blocks = splits
    count = at.shape[0]
    cut = (1, blocks, count, width // (n_split * blocks), 4 * part)
    cut_spec = pl.BlockSpec((1, blocks, 1) + cut[3:], lambda t: (0, 0, t, 0, 0))
    return call(
        functools.partial(attend_back_kernel, n_split),
        "attend_back",
        [((count, 3 * part, seq), BF), ((count, 2, part), F32)] + [(cut, BF)] * n_split,
        [SMEM, fixed(gmt.shape), fixed(n1t.shape), nth(a_part.shape), nth(qkvt.shape), nth(at.shape),
         nth(lse.shape), fixed(docs.shape)],
        (ids, gmt, n1t, a_part, qkvt, at, lse, docs),
        out_specs=(nth((count, 3 * part, seq)), nth((count, 2, part))) + (cut_spec,) * n_split,
        grid=(count,),
        scratch=[
            pltpu.VMEM((seq, seq), F32),
            pltpu.VMEM((part, seq), BF),
            pltpu.VMEM((part // HEAD, 2, HEAD, seq), F32),
            pltpu.VMEM((width, 4 * part), BF),
        ],
    )


def mlp_kernel(
    n_t, n_split, plan, ids_ref, x_ref, at_one_ref, at_two_ref, out_one_ref, out_two_ref, small_ref,
    out_bias_ref, gain_ref, bias_ref, down_bias_ref, own_up_ref, own_down_ref, *refs
):
    sources, refs = refs[: len(plan)], refs[len(plan) :]
    cot_ref, out_ref, *refs = refs
    gm_ref, gmt_ref, gvec_ref, gbup_ref = refs[:4]
    splits = refs[4 : 4 + n_split]
    (mixed_ref, n2_ref, n2t_ref, cott_ref, total_ref, grad_ref, act_ref, gpre_ref, dm_ref,
     up_all_ref, down_all_ref, sems) = refs[4 + n_split :]
    seq, width = x_ref.shape
    step_t = pl.program_id(0)
    blocks = seq // BLOCK
    slot = lax.rem(step_t, 2)
    wholes = [up_all_ref, down_all_ref]
    start, wait = fetch(0, n_t, step_t, ids_ref, [own_up_ref, own_down_ref], sources, plan, wholes, sems)
    up_ref, down_ref = up_all_ref.at[slot], down_all_ref.at[slot]
    start()

    @pl.when(step_t == 0)
    def _():
        gvec_ref[...] = jnp.zeros_like(gvec_ref)

        for step in range(blocks):
            rows = slice(step * BLOCK, (step + 1) * BLOCK)
            total = x_ref[rows, :].astype(F32) + out_bias_ref[...]
            for at_ref, w_out_ref in ((at_one_ref, out_one_ref), (at_two_ref, out_two_ref)):
                for t in range(at_ref.shape[0]):
                    total += dot(at_ref[t, :, rows].T, w_out_ref[t], 1, 0)
            mixed_ref[rows, :] = total
            xhat, _ = normalize(total)
            normed = (xhat * gain_ref[...] + bias_ref[...]).astype(BF)
            n2_ref[rows, :] = normed
            n2t_ref[:, rows] = normed.T
            held = cot_ref[rows, :]
            cott_ref[:, rows] = held.T
            gvec_ref[3:4, :] += jnp.sum(held.astype(F32), axis=0, keepdims=True)
            total_ref[rows, :] = jnp.zeros((BLOCK, width), F32)
            grad_ref[rows, :] = jnp.zeros((BLOCK, width), F32)

    wait()
    bias = small_ref[0, 2:3, :]

    def begin_block(step):
        rows = slice(step * BLOCK, (step + 1) * BLOCK)
        pre = dot(n2_ref[rows, :], up_ref[...], 1, 0) + bias
        return pre, dot(cot_ref[rows, :], down_ref[...], 1, 1)

    sums = jnp.zeros(bias.shape, F32)
    ahead = begin_block(0)
    for step in range(blocks):
        rows = slice(step * BLOCK, (step + 1) * BLOCK)
        pre, grad_act = ahead
        if step + 1 < blocks:
            ahead = begin_block(step + 1)
        square = pre * pre
        curve = jnp.tanh(pre * (GELU_C + (GELU_C * GELU_A) * square))
        half = 0.5 + 0.5 * curve
        act = (pre * half).astype(BF)
        slope = half + (half - half * curve) * pre * (GELU_C + (3 * GELU_C * GELU_A) * square)
        grad_pre = (slope * grad_act).astype(BF)
        act_ref[rows, :] = act
        gpre_ref[rows, :] = grad_pre
        total_ref[rows, :] += dot(act, down_ref[...], 1, 0)
        grad_ref[rows, :] += dot(grad_pre, up_ref[...], 1, 1)
        sums += jnp.sum(grad_pre.astype(F32), axis=0, keepdims=True)
    gbup_ref[0] = sums
    dm_ref[...] = dot(n2t_ref[...], gpre_ref[...], 1, 0).astype(BF)
    split_rows(dm_ref, ids_ref, splits, 0)
    dm_ref[...] = dot(cott_ref[...], act_ref[...], 1, 0).astype(BF)
    split_rows(dm_ref, ids_ref, splits, 1)

    @pl.when(step_t == n_t - 1)
    def _():
        for step in range(blocks):
            rows = slice(step * BLOCK, (step + 1) * BLOCK)
            xhat, rstd = normalize(mixed_ref[rows, :])
            grad_n = grad_ref[rows, :]
            grad_mixed = cot_ref[rows, :].astype(F32) + norm_backward(grad_n, xhat, rstd, gain_ref[...])
            gm_ref[rows, :] = grad_mixed.astype(BF)
            gmt_ref[:, rows] = grad_mixed.astype(BF).T
            gvec_ref[0:1, :] += jnp.sum(grad_mixed, axis=0, keepdims=True)
            gvec_ref[1:2, :] += jnp.sum(grad_n * xhat, axis=0, keepdims=True)
            gvec_ref[2:3, :] += jnp.sum(grad_n, axis=0, keepdims=True)
            out_ref[rows, :] = (mixed_ref[rows, :] + total_ref[rows, :] + down_bias_ref[...]).astype(BF)


def mlp(splits, ids, x, at_one, at_two, a_one, a_two, w_up, w_down, sources, plan, smalls, vecs, cot):
    seq, width = x.shape
    n_t, part = at_one.shape[0] + at_two.shape[0], at_one.shape[1]
    ff = w_up.shape[1]
    n_split, blocks = splits
    cut = (2, blocks, n_t, width // (n_split * blocks), ff)
    cut_spec = pl.BlockSpec((2, blocks, 1) + cut[3:], lambda t: (0, 0, t, 0, 0))
    gbup = (n_t, 1, ff)
    return call(
        functools.partial(mlp_kernel, n_t, n_split, plan),
        "mlp",
        [((seq, width), BF), ((seq, width), BF), ((width, seq), BF), ((8, width), F32), (gbup, F32)]
        + [(cut, BF)] * n_split,
        [SMEM, fixed(x.shape), fixed(at_one.shape), fixed(at_two.shape),
         *[pl.BlockSpec((a.shape[0], part, width), lambda t: (0, 3, 0), pipeline_mode=pl.Buffered(1)) for a in (a_one, a_two)],
         nth(smalls.shape)] + [fixed((1, width))] * 4 + [HBM] * (2 + len(sources)) + [fixed(cot.shape)],
        (ids, x, at_one, at_two, a_one, a_two, smalls) + tuple(vecs) + (w_up, w_down) + tuple(sources) + (cot,),
        out_specs=(fixed((seq, width)), fixed((seq, width)), fixed((width, seq)), fixed((8, width)), nth(gbup))
        + (cut_spec,) * n_split,
        grid=(n_t,),
        scratch=[
            pltpu.VMEM((seq, width), F32),
            pltpu.VMEM((seq, width), BF),
            pltpu.VMEM((width, seq), BF),
            pltpu.VMEM((width, seq), BF),
            pltpu.VMEM((seq, width), F32),
            pltpu.VMEM((seq, width), F32),
            pltpu.VMEM((seq, ff), BF),
            pltpu.VMEM((seq, ff), BF),
            pltpu.VMEM((width, ff), BF),
            pltpu.VMEM((2, width, ff), BF),
            pltpu.VMEM((2, ff, width), BF),
            pltpu.SemaphoreType.DMA((2, max(2, piece_count(sources)))),
        ],
    )


def input_back_kernel(x_ref, gm_ref, gain_ref, a_one_ref, a_two_ref, one_ref, two_ref, out_ref, gvec_ref):

    @pl.when(pl.program_id(0) == 0)
    def _():
        gvec_ref[...] = jnp.zeros_like(gvec_ref)

    gp = jnp.concatenate([ref[t] for ref in (one_ref, two_ref) for t in range(ref.shape[0])]).T
    weights = jnp.concatenate([ref[t] for ref in (a_one_ref, a_two_ref) for t in range(ref.shape[0])])
    grad_n = dot(gp, weights, 1, 0)
    xhat, rstd = normalize(x_ref[...].astype(F32))
    out_ref[...] = (gm_ref[...].astype(F32) + norm_backward(grad_n, xhat, rstd, gain_ref[...])).astype(BF)
    gvec_ref[0:1, :] += jnp.sum(grad_n * xhat, axis=0, keepdims=True)
    gvec_ref[1:2, :] += jnp.sum(grad_n, axis=0, keepdims=True)


def input_back(x, gm, gain, a_one, a_two, one, two):
    seq, width = x.shape
    part3 = one.shape[1]
    by_rows = pl.BlockSpec((BLOCK, width), lambda i: (i, 0))

    def by_columns(gpt):
        return pl.BlockSpec(gpt.shape[:2] + (BLOCK,), lambda i: (0, 0, i))

    return call(
        input_back_kernel,
        "input_back",
        [((seq, width), BF), ((8, width), F32)],
        [by_rows, by_rows, fixed(gain.shape), fixed((one.shape[0], part3, width)), fixed((two.shape[0], part3, width)),
         by_columns(one), by_columns(two)],
        (x, gm, gain, a_one, a_two, one, two),
        out_specs=(by_rows, fixed((8, width))),
        grid=(seq // BLOCK,),
    )


def trade(value):
    return lax.all_to_all(value, "tensor", 0, 0, tiled=True)


def turn(value, by):
    return jnp.roll(value, -by, axis=0)


def swap(value, n_dp, mask):
    return lax.ppermute(value, "dp", [(i, i ^ mask) for i in range(n_dp)])


def after(value, *others):
    return lax.optimization_barrier((value,) + others)[0]


def gather_others(value, tensor, n_t):
    if n_t != 4:
        gathered = trade(jnp.broadcast_to(value[None], (n_t,) + value.shape))
        return turn(gathered, tensor + 1)[: n_t - 1], gathered

    def line(item, pairs):
        return lax.ppermute(item, "tensor", pairs)

    two = line(value, [(0, 2), (1, 3), (2, 0), (3, 1)])
    up = line(value, [(0, 1), (1, 2), (2, 3)])
    down = line(value, [(1, 0), (2, 1), (3, 2)])
    far = line(two, [(2, 3), (1, 0)])
    return jnp.stack([jnp.where(tensor == 3, far, down), two, jnp.where(tensor == 0, far, up)]), (up, down, far)


def chip_pieces(pieces, n_dp):
    if n_dp != 8:
        return [(lax.all_gather(pieces, "dp", axis=2, tiled=True), 0, tuple(range(pieces.shape[0])))]
    arrays = tuple(range(pieces.shape[0]))
    if len(arrays) == 1:
        return [(pieces, 0, arrays)] + [(swap(pieces, n_dp, mask), m + 1, arrays) for m, mask in enumerate(KEEP[1:])]
    by_x, by_y = swap(pieces, n_dp, KEEP[1]), swap(pieces, n_dp, KEEP[2])
    return [(pieces, 0, arrays), (by_x, 1, arrays), (by_y, 2, arrays)]


def chip_forward(mine, n_dp, *others):
    if n_dp != 8:
        return mine
    pieces, by_x, by_y = mine
    from_x, from_y = lax.optimization_barrier((by_x[0], by_y[0]) + others)[:2]
    first_far = swap(from_y[0:1], n_dp, KEEP[1])
    second_far = swap(from_x[1:2], n_dp, KEEP[2])
    return [pieces, (from_x,) + by_x[1:], (from_y,) + by_y[1:], (first_far, 3, (0,)), (second_far, 3, (1,))]


def pair_pieces(mine, n_dp):
    if n_dp != 8:
        return [value[None] for value, _, _ in mine], tuple((place, arrays) for _, place, arrays in mine)
    both = mine + [(swap(value, n_dp, PAIR), place + len(KEEP), arrays) for value, place, arrays in mine]
    return [value[None] for value, _, _ in both], tuple((place, arrays) for _, place, arrays in both)


def pair_swap(parts, n_dp):
    return [swap(parts[1], n_dp, PAIR)] if n_dp == 8 else []


def pair_sum(parts, got, places, select):
    return [parts[0][select, p].astype(F32) + got[0][select, p].astype(F32) for p in places]


def chip_send(parts, got, n_dp, near, far, select):
    if n_dp != 8:
        whole = parts[0][select, 0]
        return lax.psum_scatter(whole, "dp", scatter_dimension=whole.ndim - 2, tiled=True)
    return swap(jnp.stack(pair_sum(parts, got, (near, 3), select)).astype(BF), n_dp, KEEP[near])


def chip_pass(parts, got, sent, n_dp, near, far, select):
    if n_dp != 8:
        return [sent]
    here, there = pair_sum(parts, got, (0, far), select)
    here = here + sent[0].astype(F32)
    there = (there + sent[1].astype(F32)).astype(BF)
    return [here, swap(there, n_dp, KEEP[far])]


def chip_sum(terms):
    total = terms[0].astype(F32)
    for item in terms[1:]:
        total += item.astype(F32)
    return total


def in_parts(value):
    high = value.astype(BF)
    rest = value - high.astype(F32)
    middle = rest.astype(BF)
    return [high, middle, (rest - middle.astype(F32)).astype(BF)]


def small_vectors(b_qv, b_up):
    value = jnp.concatenate([jnp.pad(b_qv, ((0, 0), (0, b_up.shape[0] - b_qv.shape[1]))), b_up[None]])
    return jnp.concatenate(in_parts(value) + [jnp.zeros((7,) + b_up.shape, BF)])


def local(n_dp, n_t, inputs, doc_ids, ln1_gain, ln1_bias, w_qkv, b_qv, w_out, out_bias, ln2_gain, ln2_bias,
          w_up, b_up, w_down, down_bias, cotangent):
    width = inputs.shape[2]
    part, ff = w_out.shape[0], w_up.shape[1]
    dp = lax.axis_index("dp")
    tensor = lax.axis_index("tensor")
    own_rows = inputs.shape[0] // n_t
    rows = width // n_dp
    each_row = range(own_rows)
    splits = (2, 4) if n_dp == 8 else (1, 1)
    order = jnp.array(KEEP + tuple(m ^ PAIR for m in KEEP), jnp.int32)
    ids = order ^ dp if n_dp == 8 else jnp.zeros_like(order)
    half = n_t // 2
    groups = (tuple(range(half)), tuple(range(half, n_t)))

    def own_piece(whole):
        return lax.dynamic_slice_in_dim(whole, dp * rows, rows, 0)

    def split_row(values):
        values = values.reshape((n_t, own_rows) + values.shape[1:])
        return [values[:, r].reshape(-1, width) for r in each_row]

    def join_row(values):
        blocks = jnp.stack([v.reshape(n_t, -1, width) for v in values], axis=1)
        return blocks.reshape((n_t * own_rows,) + blocks.shape[2:])

    own_a = jnp.concatenate([w_qkv.transpose(1, 2, 0).reshape(3 * part, width), w_out])
    pieces = jnp.concatenate([own_piece(own_a), own_piece(w_up), own_piece(w_down), small_vectors(b_qv, b_up)])
    gathered, moved = gather_others(pieces, tensor, n_t)
    smalls = jnp.concatenate([pieces[None, 3 * rows :], gathered[:, 3 * rows :]]).astype(F32)
    smalls = smalls[:, 0:3] + smalls[:, 3:6] + smalls[:, 6:9]
    stack_a = gathered[None, :, :rows]
    stack_m = jnp.stack([gathered[:, rows : 2 * rows], gathered[:, 2 * rows : 3 * rows]])
    mine_a = chip_pieces(stack_a, n_dp)
    x_rows = trade(after(inputs, *moved))
    mine_m = chip_pieces(stack_m, n_dp)
    sources_a, plan_a = pair_pieces(mine_a, n_dp)
    values_m = [m[0] for m in mine_m]
    values_m, sources_a, x_rows = lax.optimization_barrier((values_m, sources_a, x_rows))
    mine_m = [(value,) + m[1:] for value, m in zip(values_m, mine_m)]
    x_rows = split_row(x_rows)
    cot_rows = split_row(trade(after(cotangent, x_rows)))
    vecs = [v[None] for v in (out_bias, ln2_gain, ln2_bias, down_bias)]
    doc_rows = lax.dynamic_slice_in_dim(doc_ids, tensor * own_rows, own_rows, 0)
    docs = [doc_rows[r : r + 1] for r in each_row]

    def total_of(*items):
        if len(items) == 1:
            return items[0]
        return sum(item.astype(F32) for item in items).astype(items[0].dtype)

    def together(results):
        return [jax.tree.map(total_of, *items) for items in zip(*results)]

    n1ts = [first(ln1_gain[None], ln1_bias[None], x) for x in x_rows]
    seen_one = [attend(groups[0], ids, n1ts[r], own_a, sources_a, plan_a, smalls, docs[r]) for r in each_row]
    mine_m = chip_forward(mine_m, n_dp, n1ts)
    n1ts, values_m = lax.optimization_barrier((n1ts, [m[0] for m in mine_m], seen_one))[:2]
    mine_m = [(value,) + m[1:] for value, m in zip(values_m, mine_m)]
    sources_m, plan_m = pair_pieces(mine_m, n_dp)
    seen_two = [attend(groups[1], ids, n1ts[r], own_a, sources_a, plan_a, smalls, docs[r]) for r in each_row]
    sources_m, cot_rows = lax.optimization_barrier((sources_m, cot_rows, seen_two))[:2]
    made = [
        mlp(splits, ids, x_rows[r], seen_one[r][1], seen_two[r][1], seen_one[r][3], seen_two[r][3], w_up, w_down,
            sources_m, plan_m, smalls, vecs, cot_rows[r])
        for r in each_row
    ]
    gvec, gbup, *dms = together([m[3:] for m in made])
    got_m = pair_swap(dms, n_dp)
    block_out = trade(join_row([m[0] for m in made]))

    def back(gmts, seen):
        items = [attend_back(splits, ids, gmts[r], n1ts[r], *seen[r], docs[r]) for r in each_row]
        return [i[0] for i in items], together([i[1:] for i in items])

    up_way, down_way = (1, 2, 0), (2, 1, 1)
    one_way, two_way = (1, 2, 0), (2, 1, 0)
    gmts = [m[2] for m in made]
    gpt_two, (gb_two, *da_two) = back(gmts, seen_two)
    got_m, keep_m = lax.optimization_barrier((got_m, dms[0], gpt_two))[:2]
    dms = [keep_m]
    sent_m = [chip_send(dms, got_m, n_dp, *way) for way in (up_way, down_way)]
    got_two = pair_swap(da_two, n_dp)
    gmts = lax.optimization_barrier((gmts, gpt_two))[0]
    gpt_one, (gb_one, *da_one) = back(gmts, seen_one)
    got_one = pair_swap(da_one, n_dp)
    block_out, got_two, sent_m = lax.optimization_barrier((block_out, got_two, sent_m, gpt_one))[:3]
    passed_m = [chip_pass(dms, got_m, sent, n_dp, *way) for sent, way in zip(sent_m, (up_way, down_way))]
    gms = lax.optimization_barrier(([m[1] for m in made], gpt_one, block_out, sent_m))[0]
    ends = [
        input_back(x_rows[r], gms[r], ln1_gain[None], seen_two[r][3], seen_one[r][3], gpt_two[r], gpt_one[r])
        for r in each_row
    ]
    (gin,) = together([e[1:] for e in ends])
    grad_inputs = trade(join_row([e[0] for e in ends]))
    got_one, got_two, passed_m = lax.optimization_barrier((got_one, got_two, passed_m, ends))[:3]
    sent_one = chip_send(da_one, got_one, n_dp, *one_way)
    sent_two = chip_send(da_two, got_two, n_dp, *two_way)
    passed_one = chip_pass(da_one, got_one, sent_one, n_dp, *one_way)
    passed_two = chip_pass(da_two, got_two, sent_two, n_dp, *two_way)

    def shard_sum(summed):
        return jnp.sum(trade(turn(summed.astype(BF), -tensor)).astype(F32), axis=0)

    sums_m = jnp.concatenate([chip_sum(passed) for passed in passed_m], axis=1)
    sums_a = jnp.concatenate([chip_sum(passed_one), chip_sum(passed_two)])
    gbs = jnp.concatenate([gb_one, gb_two])

    each = width // (n_dp * n_t)
    vectors = jnp.concatenate([gin[0:2], gvec[0:4]])
    vectors = vectors.reshape(6, n_dp, n_t, each).transpose(1, 2, 0, 3).reshape(n_dp, n_t, 6 * each)
    shard = jnp.concatenate(
        [
            gbs.reshape(n_t, 2, n_dp, part // n_dp).transpose(2, 0, 1, 3).reshape(n_dp, n_t, -1),
            gbup.reshape(n_t, n_dp, ff // n_dp).transpose(1, 0, 2),
        ],
        axis=2,
    )
    both = jnp.concatenate([vectors, jnp.roll(shard, tensor, axis=1)], axis=2)
    if n_dp == 8:
        for mask in (1, 2, 4):
            bit = (dp // mask) % 2
            split = both.reshape((both.shape[0] // 2, 2) + both.shape[1:])
            kept = lax.dynamic_index_in_dim(split, bit, 1, keepdims=False)
            sent = lax.dynamic_index_in_dim(split, 1 - bit, 1, keepdims=False)
            both = kept + swap(sent, n_dp, mask)
        both = both[0]
    else:
        both = lax.psum_scatter(both, "dp", scatter_dimension=0, tiled=False)
    parts = turn(jnp.concatenate([p[:, None] for p in in_parts(both)], axis=1), tensor)
    parts = jnp.pad(parts, ((0, 0), (0, 13), (0, width - parts.shape[2])))
    share = shard_sum(after(jnp.concatenate([sums_a.astype(BF), sums_m.astype(BF), parts], axis=1), grad_inputs))
    share_a, share_up, share_down = (share[i * rows : (i + 1) * rows] for i in range(3))
    mine = jnp.sum(share[3 * rows : 3 * rows + 3, 0 : both.shape[1]], axis=0)
    vec_out = mine[0 : 6 * each].reshape(6, each)
    share_b_qv = mine[6 * each : 6 * each + 2 * (part // n_dp)].reshape(2, part // n_dp)
    share_b_up = mine[6 * each + 2 * (part // n_dp) :]
    share_w_qkv = share_a[:, 0 : 3 * part].reshape(rows, 3, part)
    share_w_out = share_a[:, 3 * part :].T
    return (
        block_out,
        grad_inputs,
        vec_out[0],
        vec_out[1],
        share_w_qkv,
        share_b_qv,
        share_w_out,
        vec_out[2],
        vec_out[3],
        vec_out[4],
        share_up,
        share_b_up,
        share_down.T,
        vec_out[5],
    )


def solution(mesh):
    return jax.shard_map(
        functools.partial(local, mesh.shape["dp"], mesh.shape["tensor"]),
        mesh=mesh,
        in_specs=(
            P("dp", "tensor", None),
            P("dp", None),
            P(),
            P(),
            P(None, None, "tensor"),
            P(None, "tensor"),
            P("tensor", None),
            P(),
            P(),
            P(),
            P(None, "tensor"),
            P("tensor"),
            P("tensor", None),
            P(),
            P("dp", "tensor", None),
        ),
        out_specs=(
            P("dp", "tensor", None),
            P("dp", "tensor", None),
            P(("dp", "tensor")),
            P(("dp", "tensor")),
            P("dp", None, "tensor"),
            P(None, ("tensor", "dp")),
            P("tensor", "dp"),
            P(("dp", "tensor")),
            P(("dp", "tensor")),
            P(("dp", "tensor")),
            P("dp", "tensor"),
            P(("tensor", "dp")),
            P("tensor", "dp"),
            P(("dp", "tensor")),
        ),
        check_vma=False,
    )
```

```python
import functools

import jax
import jax.numpy as jnp
from jax import lax
from jax.experimental import pallas as pl
from jax.experimental.pallas import tpu as pltpu
from jax.sharding import PartitionSpec as P

BF = jnp.bfloat16
F32 = jnp.float32
HEAD = 64
EPS = 1e-05
GELU_C = 0.7978845608028654
GELU_A = 0.044715
BLOCK = 256
MIB = 1024 * 1024
KEEP = (0, 2, 6, 4)
PAIR = 1
LONG = 5 * 10**10


def dot(lhs, rhs, lhs_dim, rhs_dim):
    return lax.dot_general(
        lhs, rhs, (((lhs_dim,), (rhs_dim,)), ((), ())), preferred_element_type=F32
    )


def normalize(value):
    mean = jnp.mean(value, axis=-1, keepdims=True)
    centred = value - mean
    variance = jnp.mean(centred * centred, axis=-1, keepdims=True)
    rstd = lax.rsqrt(variance + EPS)
    return centred * rstd, rstd


def norm_backward(grad, xhat, rstd, gain):
    scaled = grad * gain
    mean_e = jnp.mean(scaled, axis=-1, keepdims=True)
    mean_ex = jnp.mean(scaled * xhat, axis=-1, keepdims=True)
    return rstd * (scaled - mean_e - xhat * mean_ex)


def column(line):
    return jnp.broadcast_to(line, (8, line.shape[1])).T[:, 0:1]


def block_rows(index, size=BLOCK):
    return pl.ds(pl.multiple_of(index * size, size), size)


VMEM = pl.BlockSpec(memory_space=pltpu.VMEM)
SMEM = pl.BlockSpec(memory_space=pltpu.SMEM)
HBM = pl.BlockSpec(memory_space=pl.ANY)


def call(kernel, name, outs, specs, args, out_specs=None, vmem=60, scratch=(), grid=(), flops=1):
    shapes = tuple(jax.ShapeDtypeStruct(*o) for o in outs)
    return pl.pallas_call(
        kernel,
        grid=grid,
        out_shape=shapes,
        in_specs=specs,
        out_specs=out_specs or (VMEM,) * len(outs),
        scratch_shapes=list(scratch),
        compiler_params=pltpu.CompilerParams(vmem_limit_bytes=vmem * MIB),
        name=name,
        cost_estimate=pl.CostEstimate(flops=flops, bytes_accessed=1, transcendentals=0),
    )(*args)


def fixed(shape):
    return pl.BlockSpec(shape, lambda *_: (0,) * len(shape), pipeline_mode=pl.Buffered(1))


def nth(shape, base=0):
    return pl.BlockSpec((1,) + tuple(shape[1:]), lambda t: (lax.rem(t + base, shape[0]),) + (0,) * (len(shape) - 1))


def own_copies(owns, wholes, sems):
    return [
        pltpu.make_async_copy(own, whole.at[0], sems.at[0, i]) for i, (own, whole) in enumerate(zip(owns, wholes))
    ]


def piece_copies(ids_ref, sources, plan, wholes, sems, k, slot):
    copies = []
    for src, (place, arrays) in zip(sources, plan):
        rows = src.shape[3]
        for m in range(src.shape[0]):
            at = pl.multiple_of(ids_ref[place + m] * rows, rows)
            for u, array in enumerate(arrays):
                copies.append(
                    pltpu.make_async_copy(
                        src.at[m, u, k - 1], wholes[array].at[slot, pl.ds(at, rows), :], sems.at[slot, len(copies)]
                    )
                )
    return copies


def piece_count(sources):
    return sum(src.shape[0] * src.shape[1] for src in sources)


def fetch(base, count, step, ids_ref, owns, sources, plan, wholes, sems):
    slot = lax.rem(step, 2)
    begins_own = base == 0

    def start():
        @pl.when(step == 0)
        def _():
            for copy in own_copies(owns, wholes, sems) if begins_own else piece_copies(
                ids_ref, sources, plan, wholes, sems, base, 0
            ):
                copy.start()

        @pl.when(step < count - 1)
        def _():
            for copy in piece_copies(ids_ref, sources, plan, wholes, sems, base + step + 1, lax.rem(step + 1, 2)):
                copy.start()

    def wait():
        if begins_own:
            @pl.when(step == 0)
            def _():
                for copy in own_copies(owns, wholes, sems):
                    copy.wait()

        @pl.when(step > 0 if begins_own else step >= 0)
        def _():
            for copy in piece_copies(ids_ref, sources, plan, wholes, sems, base + step, slot):
                copy.wait()

    return start, wait


def first_kernel(gain_ref, bias_ref, x_ref, n1t_ref):
    xhat, _ = normalize(x_ref[...].astype(F32))
    n1t_ref[...] = (xhat * gain_ref[...] + bias_ref[...]).astype(BF).T


def first(gain, bias, x):
    seq, width = x.shape
    return call(
        first_kernel,
        "first",
        [((width, seq), BF)],
        [fixed(gain.shape), fixed(bias.shape), pl.BlockSpec((BLOCK, width), lambda i: (i, 0))],
        (gain, bias, x),
        out_specs=(pl.BlockSpec((width, BLOCK), lambda i: (0, i)),),
        grid=(seq // BLOCK,),
    )[0]


def mask_bias(docs_ref, mask_ref):
    seq = mask_ref.shape[0]
    docs = docs_ref[...]
    docs_col = column(docs)
    for begin in range(0, seq, BLOCK):
        end = begin + BLOCK
        same = docs_col[0:end] == docs[:, begin:end]
        place_k = lax.broadcasted_iota(jnp.int32, (end, BLOCK), 0)
        place_q = begin + lax.broadcasted_iota(jnp.int32, (end, BLOCK), 1)
        allowed = same & (place_k <= place_q)
        mask_ref[0:end, begin:end] = jnp.where(allowed, 0.0, -1e30).astype(F32)


def attend_kernel(base, plan, ids_ref, n1t_ref, small_ref, docs_ref, own_ref, *refs):
    sources, (qkvt_ref, at_ref, lse_ref, a_ref, mask_ref, held_ref, sems) = refs[: len(plan)], refs[len(plan) :]
    step = pl.program_id(0)
    start, wait = fetch(base, pl.num_programs(0), step, ids_ref, [own_ref], sources, plan, [held_ref], sems)
    start()
    seq = n1t_ref.shape[1]
    part = at_ref.shape[1]

    @pl.when(pl.program_id(0) == 0)
    def _():
        mask_bias(docs_ref, mask_ref)

    wait()
    a_ref[0] = held_ref[lax.rem(step, 2)]
    proj = dot(a_ref[0, 0 : 3 * part, :], n1t_ref[...], 1, 0)
    qkvt_ref[0, 0:part, :] = (proj[0:part] + column(small_ref[0, 0:1, 0:part])).astype(BF)
    qkvt_ref[0, part : 2 * part, :] = proj[part : 2 * part].astype(BF)
    qkvt_ref[0, 2 * part :, :] = (proj[2 * part :] + column(small_ref[0, 1:2, 0:part])).astype(BF)
    heads = range(part // HEAD)

    def rows_of(which, h):
        return slice(which * part + h * HEAD, which * part + (h + 1) * HEAD)

    keys = [qkvt_ref[0, rows_of(1, h), :].T for h in heads]
    values = [jnp.concatenate([qkvt_ref[0, rows_of(2, h), :], jnp.ones((16, seq), BF)]) for h in heads]

    def scores_of(begin):
        end = begin + BLOCK
        mask = mask_ref[0:end, begin:end]
        return [dot(keys[h][0:end], qkvt_ref[0, rows_of(0, h), begin:end] * BF(0.125), 1, 0) + mask for h in heads]

    scores = scores_of(0)
    for begin in range(0, seq, BLOCK):
        end = begin + BLOCK
        now = scores
        top = [jnp.max(s, axis=0, keepdims=True) for s in now]
        if end < seq:
            scores = scores_of(end)
        expo = [jnp.exp(s - t).astype(BF) for s, t in zip(now, top)]
        out = [dot(values[h][:, 0:end], expo[h], 1, 0) for h in heads]
        for h in heads:
            total = out[h][HEAD : HEAD + 1]
            at_ref[0, h * HEAD : (h + 1) * HEAD, begin:end] = (out[h][0:HEAD] / total).astype(BF)
            lse_ref[0, h : h + 1, begin:end] = top[h] + jnp.log(total)


def attend(group, ids, n1t, own_a, sources, plan, smalls, docs):
    width, seq = n1t.shape
    base, count, part = group[0], len(group), own_a.shape[0] // 4
    shapes = [(count, 3 * part, seq), (count, part, seq), (count, 8, seq), (count,) + own_a.shape]
    return call(
        functools.partial(attend_kernel, base, plan),
        "attend",
        [(shapes[0], BF), (shapes[1], BF), (shapes[2], F32), (shapes[3], BF)],
        [SMEM, fixed(n1t.shape), nth(smalls.shape, base), fixed(docs.shape)] + [HBM] * (1 + len(sources)),
        (ids, n1t, smalls, docs, own_a) + tuple(sources),
        out_specs=tuple(nth(s) for s in shapes),
        grid=(count,),
        scratch=[
            pltpu.VMEM((seq, seq), F32),
            pltpu.VMEM((2,) + own_a.shape, BF),
            pltpu.SemaphoreType.DMA((2, piece_count(sources))),
        ],
    )


def split_rows(whole_ref, ids_ref, outs, array=0):
    for g, out in enumerate(outs):
        count, rows = out.shape[1], out.shape[3]
        for m in range(count):
            at = pl.multiple_of(ids_ref[g * count + m] * rows, rows)
            out[array, m, 0] = whole_ref[pl.ds(at, rows), :]


def attend_back_kernel(
    n_split, ids_ref, gmt_ref, n1t_ref, a_ref, qkvt_ref, at_ref, lse_ref, docs_ref, gpt_ref, gb_ref, *refs
):
    splits, (mask_ref, gat_ref, dkv_ref, da_ref) = refs[:n_split], refs[n_split:]
    seq = n1t_ref.shape[1]
    part = at_ref.shape[1]

    @pl.when(pl.program_id(0) == 0)
    def _():
        mask_bias(docs_ref, mask_ref)

    gat_ref[...] = dot(a_ref[0, 3 * part :, :], gmt_ref[...], 1, 0).astype(BF)
    heads = range(part // HEAD)

    def rows_of(which, h):
        return slice(which * part + h * HEAD, which * part + (h + 1) * HEAD)

    keys = [qkvt_ref[0, rows_of(1, h), :].T for h in heads]
    values = [qkvt_ref[0, rows_of(2, h), :].T for h in heads]
    items = [(begin, h) for begin in range(0, seq, BLOCK) for h in heads]

    def begin_item(begin, h):
        end = begin + BLOCK
        query = qkvt_ref[0, rows_of(0, h), begin:end] * BF(0.125)
        grad = gat_ref[rows_of(0, h), begin:end]
        scores = dot(keys[h][0:end], query, 1, 0) + mask_ref[0:end, begin:end]
        return query, grad, scores, dot(values[h][0:end], grad, 1, 0)

    ahead = begin_item(*items[0])
    for i, (begin, h) in enumerate(items):
        end = begin + BLOCK
        query, grad, scores, grad_probs = ahead
        if i + 1 < len(items):
            ahead = begin_item(*items[i + 1])
        delta = jnp.sum(
            grad.astype(F32) * at_ref[0, rows_of(0, h), begin:end].astype(F32), axis=0, keepdims=True
        )
        probs = jnp.exp(scores - lse_ref[0, h : h + 1, begin:end])
        grad_scores = (probs * (grad_probs - delta)).astype(BF)
        gpt_ref[0, rows_of(0, h), begin:end] = (
            0.125 * dot(qkvt_ref[0, rows_of(1, h), 0:end], grad_scores, 1, 0)
        ).astype(BF)
        for which, share in ((0, dot(query, grad_scores, 1, 1)), (1, dot(grad, probs.astype(BF), 1, 1))):
            if begin > 0:
                dkv_ref[h, which, :, 0:begin] += share[:, 0:begin]
            dkv_ref[h, which, :, begin:end] = share[:, begin:end]
    for h in heads:
        for which in range(2):
            gpt_ref[0, rows_of(1 + which, h), :] = dkv_ref[h, which].astype(BF)
    ones = jnp.ones((8, seq), BF)
    gb_ref[0, 0:1, :] = dot(ones, gpt_ref[0, 0:part, :], 1, 1)[0:1]
    gb_ref[0, 1:2, :] = dot(ones, gpt_ref[0, 2 * part : 3 * part, :], 1, 1)[0:1]
    da_ref[:, 0 : 3 * part] = dot(n1t_ref[...], gpt_ref[0], 1, 1).astype(BF)
    da_ref[:, 3 * part :] = dot(gmt_ref[...], at_ref[0], 1, 1).astype(BF)
    split_rows(da_ref, ids_ref, splits)


def attend_back(splits, ids, gmt, n1t, qkvt, at, lse, a_part, docs):
    width, seq = n1t.shape
    part = at.shape[1]
    n_split, blocks = splits
    count = at.shape[0]
    cut = (1, blocks, count, width // (n_split * blocks), 4 * part)
    cut_spec = pl.BlockSpec((1, blocks, 1) + cut[3:], lambda t: (0, 0, t, 0, 0))
    return call(
        functools.partial(attend_back_kernel, n_split),
        "attend_back",
        [((count, 3 * part, seq), BF), ((count, 2, part), F32)] + [(cut, BF)] * n_split,
        [SMEM, fixed(gmt.shape), fixed(n1t.shape), nth(a_part.shape), nth(qkvt.shape), nth(at.shape),
         nth(lse.shape), fixed(docs.shape)],
        (ids, gmt, n1t, a_part, qkvt, at, lse, docs),
        out_specs=(nth((count, 3 * part, seq)), nth((count, 2, part))) + (cut_spec,) * n_split,
        grid=(count,),
        scratch=[
            pltpu.VMEM((seq, seq), F32),
            pltpu.VMEM((part, seq), BF),
            pltpu.VMEM((part // HEAD, 2, HEAD, seq), F32),
            pltpu.VMEM((width, 4 * part), BF),
        ],
    )


def mlp_kernel(
    n_t, n_split, plan, ids_ref, x_ref, at_one_ref, at_two_ref, out_one_ref, out_two_ref, small_ref,
    out_bias_ref, gain_ref, bias_ref, down_bias_ref, own_up_ref, own_down_ref, *refs
):
    sources, refs = refs[: len(plan)], refs[len(plan) :]
    cot_ref, out_ref, *refs = refs
    gm_ref, gmt_ref, gvec_ref, gbup_ref = refs[:4]
    splits = refs[4 : 4 + n_split]
    (mixed_ref, n2_ref, n2t_ref, cott_ref, total_ref, grad_ref, act_ref, gpre_ref, dm_ref,
     up_all_ref, down_all_ref, sems) = refs[4 + n_split :]
    seq, width = x_ref.shape
    step_t = pl.program_id(0)
    blocks = seq // BLOCK
    slot = lax.rem(step_t, 2)
    wholes = [up_all_ref, down_all_ref]
    start, wait = fetch(0, n_t, step_t, ids_ref, [own_up_ref, own_down_ref], sources, plan, wholes, sems)
    up_ref, down_ref = up_all_ref.at[slot], down_all_ref.at[slot]
    start()

    @pl.when(step_t == 0)
    def _():
        gvec_ref[...] = jnp.zeros_like(gvec_ref)

        @pl.loop(0, blocks)
        def _(step):
            rows = block_rows(step)
            total = x_ref[rows, :].astype(F32) + out_bias_ref[...]
            for at_ref, w_out_ref in ((at_one_ref, out_one_ref), (at_two_ref, out_two_ref)):
                for t in range(at_ref.shape[0]):
                    total += dot(at_ref[t, :, rows].T, w_out_ref[t], 1, 0)
            mixed_ref[rows, :] = total
            xhat, _ = normalize(total)
            normed = (xhat * gain_ref[...] + bias_ref[...]).astype(BF)
            n2_ref[rows, :] = normed
            n2t_ref[:, rows] = normed.T
            held = cot_ref[rows, :]
            cott_ref[:, rows] = held.T
            gvec_ref[3:4, :] += jnp.sum(held.astype(F32), axis=0, keepdims=True)
            total_ref[rows, :] = jnp.zeros((BLOCK, width), F32)
            grad_ref[rows, :] = jnp.zeros((BLOCK, width), F32)

    wait()
    bias = small_ref[0, 2:3, :]

    def one(step, sums):
        rows = block_rows(step)
        pre = dot(n2_ref[rows, :], up_ref[...], 1, 0) + bias
        grad_act = dot(cot_ref[rows, :], down_ref[...], 1, 1)
        square = pre * pre
        curve = jnp.tanh(pre * (GELU_C + (GELU_C * GELU_A) * square))
        half = 0.5 + 0.5 * curve
        act = (pre * half).astype(BF)
        slope = half + (half - half * curve) * pre * (GELU_C + (3 * GELU_C * GELU_A) * square)
        grad_pre = (slope * grad_act).astype(BF)
        act_ref[rows, :] = act
        gpre_ref[rows, :] = grad_pre
        total_ref[rows, :] += dot(act, down_ref[...], 1, 0)
        grad_ref[rows, :] += dot(grad_pre, up_ref[...], 1, 1)
        return sums + jnp.sum(grad_pre.astype(F32), axis=0, keepdims=True)

    gbup_ref[0] = lax.fori_loop(0, blocks, one, jnp.zeros(bias.shape, F32), unroll=True)
    dm_ref[...] = dot(n2t_ref[...], gpre_ref[...], 1, 0).astype(BF)
    split_rows(dm_ref, ids_ref, splits, 0)
    dm_ref[...] = dot(cott_ref[...], act_ref[...], 1, 0).astype(BF)
    split_rows(dm_ref, ids_ref, splits, 1)

    @pl.when(step_t == n_t - 1)
    def _():
        @pl.loop(0, blocks)
        def _(step):
            rows = block_rows(step)
            xhat, rstd = normalize(mixed_ref[rows, :])
            grad_n = grad_ref[rows, :]
            grad_mixed = cot_ref[rows, :].astype(F32) + norm_backward(grad_n, xhat, rstd, gain_ref[...])
            gm_ref[rows, :] = grad_mixed.astype(BF)
            gmt_ref[:, rows] = grad_mixed.astype(BF).T
            gvec_ref[0:1, :] += jnp.sum(grad_mixed, axis=0, keepdims=True)
            gvec_ref[1:2, :] += jnp.sum(grad_n * xhat, axis=0, keepdims=True)
            gvec_ref[2:3, :] += jnp.sum(grad_n, axis=0, keepdims=True)
            out_ref[rows, :] = (mixed_ref[rows, :] + total_ref[rows, :] + down_bias_ref[...]).astype(BF)


def mlp(splits, ids, x, at_one, at_two, a_one, a_two, w_up, w_down, sources, plan, smalls, vecs, cot):
    seq, width = x.shape
    n_t, part = at_one.shape[0] + at_two.shape[0], at_one.shape[1]
    ff = w_up.shape[1]
    n_split, blocks = splits
    cut = (2, blocks, n_t, width // (n_split * blocks), ff)
    cut_spec = pl.BlockSpec((2, blocks, 1) + cut[3:], lambda t: (0, 0, t, 0, 0))
    gbup = (n_t, 1, ff)
    return call(
        functools.partial(mlp_kernel, n_t, n_split, plan),
        "mlp",
        [((seq, width), BF), ((seq, width), BF), ((width, seq), BF), ((8, width), F32), (gbup, F32)]
        + [(cut, BF)] * n_split,
        [SMEM, fixed(x.shape), fixed(at_one.shape), fixed(at_two.shape),
         *[pl.BlockSpec((a.shape[0], part, width), lambda t: (0, 3, 0), pipeline_mode=pl.Buffered(1)) for a in (a_one, a_two)],
         nth(smalls.shape)] + [fixed((1, width))] * 4 + [HBM] * (2 + len(sources)) + [fixed(cot.shape)],
        (ids, x, at_one, at_two, a_one, a_two, smalls) + tuple(vecs) + (w_up, w_down) + tuple(sources) + (cot,),
        out_specs=(fixed((seq, width)), fixed((seq, width)), fixed((width, seq)), fixed((8, width)), nth(gbup))
        + (cut_spec,) * n_split,
        grid=(n_t,),
        scratch=[
            pltpu.VMEM((seq, width), F32),
            pltpu.VMEM((seq, width), BF),
            pltpu.VMEM((width, seq), BF),
            pltpu.VMEM((width, seq), BF),
            pltpu.VMEM((seq, width), F32),
            pltpu.VMEM((seq, width), F32),
            pltpu.VMEM((seq, ff), BF),
            pltpu.VMEM((seq, ff), BF),
            pltpu.VMEM((width, ff), BF),
            pltpu.VMEM((2, width, ff), BF),
            pltpu.VMEM((2, ff, width), BF),
            pltpu.SemaphoreType.DMA((2, max(2, piece_count(sources)))),
        ],
    )


def input_back_kernel(x_ref, gm_ref, gain_ref, a_one_ref, a_two_ref, one_ref, two_ref, out_ref, gvec_ref):

    @pl.when(pl.program_id(0) == 0)
    def _():
        gvec_ref[...] = jnp.zeros_like(gvec_ref)

    gp = jnp.concatenate([ref[t] for ref in (one_ref, two_ref) for t in range(ref.shape[0])]).T
    weights = jnp.concatenate([ref[t] for ref in (a_one_ref, a_two_ref) for t in range(ref.shape[0])])
    grad_n = dot(gp, weights, 1, 0)
    xhat, rstd = normalize(x_ref[...].astype(F32))
    out_ref[...] = (gm_ref[...].astype(F32) + norm_backward(grad_n, xhat, rstd, gain_ref[...])).astype(BF)
    gvec_ref[0:1, :] += jnp.sum(grad_n * xhat, axis=0, keepdims=True)
    gvec_ref[1:2, :] += jnp.sum(grad_n, axis=0, keepdims=True)


def input_back(x, gm, gain, a_one, a_two, one, two):
    seq, width = x.shape
    part3 = one.shape[1]
    by_rows = pl.BlockSpec((BLOCK, width), lambda i: (i, 0))

    def by_columns(gpt):
        return pl.BlockSpec(gpt.shape[:2] + (BLOCK,), lambda i: (0, 0, i))

    return call(
        input_back_kernel,
        "input_back",
        [((seq, width), BF), ((8, width), F32)],
        [by_rows, by_rows, fixed(gain.shape), fixed((one.shape[0], part3, width)), fixed((two.shape[0], part3, width)),
         by_columns(one), by_columns(two)],
        (x, gm, gain, a_one, a_two, one, two),
        out_specs=(by_rows, fixed((8, width))),
        grid=(seq // BLOCK,),
        flops=LONG,
    )


def settle_kernel(value_ref, out_ref):
    out_ref[...] = value_ref[...]


def settle(value):
    spec = pl.BlockSpec((1,) + value.shape[1:], lambda i: (i, 0, 0))
    return call(
        settle_kernel, "settle", [(value.shape, value.dtype)], [spec], (value,), out_specs=(spec,), grid=value.shape[:1]
    )[0]


def trade(value):
    return lax.all_to_all(value, "tensor", 0, 0, tiled=True)


def turn(value, by):
    return jnp.roll(value, -by, axis=0)


def swap(value, n_dp, mask):
    return lax.ppermute(value, "dp", [(i, i ^ mask) for i in range(n_dp)])


def after(value, *others):
    return lax.optimization_barrier((value,) + others)[0]


def gather_others(value, tensor, n_t):
    if n_t != 4:
        gathered = trade(jnp.broadcast_to(value[None], (n_t,) + value.shape))
        return turn(gathered, tensor + 1)[: n_t - 1], gathered

    def line(item, pairs):
        return lax.ppermute(item, "tensor", pairs)

    two = line(value, [(0, 2), (1, 3), (2, 0), (3, 1)])
    up = line(value, [(0, 1), (1, 2), (2, 3)])
    down = line(value, [(1, 0), (2, 1), (3, 2)])
    far = line(two, [(2, 3), (1, 0)])
    return jnp.stack([jnp.where(tensor == 3, far, down), two, jnp.where(tensor == 0, far, up)]), (up, down, far)


def chip_pieces(pieces, n_dp):
    if n_dp != 8:
        return [(lax.all_gather(pieces, "dp", axis=2, tiled=True), 0, tuple(range(pieces.shape[0])))]
    arrays = tuple(range(pieces.shape[0]))
    if len(arrays) == 1:
        return [(pieces, 0, arrays)] + [(swap(pieces, n_dp, mask), m + 1, arrays) for m, mask in enumerate(KEEP[1:])]
    by_x, by_y = swap(pieces, n_dp, KEEP[1]), swap(pieces, n_dp, KEEP[3])
    return [(pieces, 0, arrays), (by_x, 1, arrays), (by_y, 3, arrays)]


def chip_forward(mine, n_dp, *others):
    if n_dp != 8:
        return mine
    pieces, by_x, by_y = mine
    from_x, from_y = lax.optimization_barrier((by_x[0], by_y[0]) + others)[:2]
    first_far = swap(from_y[0:1], n_dp, KEEP[1])
    second_far = swap(from_x[1:2], n_dp, KEEP[3])
    return [pieces, (from_x,) + by_x[1:], (from_y,) + by_y[1:], (first_far, 2, (0,)), (second_far, 2, (1,))]


def pair_pieces(mine, n_dp):
    if n_dp != 8:
        return [value[None] for value, _, _ in mine], tuple((place, arrays) for _, place, arrays in mine)
    both = mine + [(swap(value, n_dp, PAIR), place + len(KEEP), arrays) for value, place, arrays in mine]
    return [value[None] for value, _, _ in both], tuple((place, arrays) for _, place, arrays in both)


def pair_swap(parts, n_dp):
    return [swap(parts[1], n_dp, PAIR)] if n_dp == 8 else []


BY_X = (slice(1, 3), 2, 3, 4, 0)
BY_Y = (slice(2, 4), 4, 1, 2, 1)


def chip_send(parts, got, n_dp, way, select):
    if n_dp != 8:
        whole = parts[0][select, 0]
        return lax.psum_scatter(whole, "dp", scatter_dimension=whole.ndim - 2, tiled=True)
    places, near = way[:2]
    value = parts[0][select, places].astype(F32) + got[0][select, places].astype(F32)
    return swap(value.astype(BF), n_dp, near)


def pass_kernel(*refs):
    count = len(refs) // 8
    for i in range(count):
        keep, got, sent, keep_far, got_far, sent_far = (ref[...].astype(F32) for ref in refs[6 * i : 6 * i + 6])
        here_ref, there_ref = refs[6 * count + 2 * i : 6 * count + 2 * i + 2]
        here_ref[...] = (keep + got + sent).astype(BF)[0, 0]
        there_ref[...] = (keep_far + got_far + sent_far).astype(BF)[0, 0]


def chip_pass(parts, got, sents, n_dp, items):
    if n_dp != 8:
        return [[sent] for sent in sents]
    _, _, sets, rows, cols = parts[0].shape
    args, specs = [], []

    def take(value, select, place):
        args.append(value)
        specs.append(pl.BlockSpec((1, 1, 1, rows, cols), lambda t: (select, place, t, 0, 0)))

    for sent, (way, select) in zip(sents, items):
        _, _, far, _, first = way
        for place, back in ((0, first), (far, 1 - first)):
            take(parts[0], select, place)
            take(got[0], select, place)
            take(sent[None], 0, back)
    made = pl.pallas_call(
        pass_kernel,
        grid=(sets,),
        out_shape=(jax.ShapeDtypeStruct((sets, rows, cols), BF),) * (2 * len(items)),
        in_specs=specs,
        out_specs=(pl.BlockSpec((1, rows, cols), lambda t: (t, 0, 0)),) * (2 * len(items)),
        compiler_params=pltpu.CompilerParams(vmem_limit_bytes=60 * MIB),
        name="chip_pass",
        cost_estimate=pl.CostEstimate(flops=1, bytes_accessed=1, transcendentals=0),
    )(*args)
    return [[made[2 * i], swap(made[2 * i + 1], n_dp, way[3])] for i, (way, _) in enumerate(items)]


def pair_kernel(*refs):
    sources, outs = refs[: -len(KEEP)], refs[-len(KEEP) :]
    at = 0
    for keep, got in zip(sources[0::2], sources[1::2]):
        for m, out in enumerate(outs):
            for t in range(keep.shape[2]):
                out[at + t] = (keep[0, m, t].astype(F32) + got[0, m, t].astype(F32)).astype(BF)
        at += keep.shape[2]


def as_rows(vectors, width):
    pad = [(0, 0)] * (vectors.ndim - 1) + [(0, 15), (0, width - vectors.shape[-1])]
    return jnp.pad(vectors[..., None, :].astype(BF), pad)


def chip_direct(groups, n_dp):
    if n_dp != 8:
        whole = jnp.concatenate([parts[0][0, 0] for parts, _ in groups])
        return [lax.psum_scatter(whole, "dp", scatter_dimension=whole.ndim - 2, tiled=True)]
    args = [value for parts, got in groups for value in (parts[0], got[0])]
    shape = (sum(parts[0].shape[2] for parts, _ in groups),) + args[0].shape[3:]
    made = call(pair_kernel, "pair", [(shape, BF)] * len(KEEP), [VMEM] * len(args), tuple(args), flops=LONG)
    return [made[0]] + [swap(made[m + 1], n_dp, mask) for m, mask in enumerate(KEEP[1:])]


def vectors_direct(vectors, dp, width, n_dp):
    if n_dp != 8:
        return [as_rows(lax.psum_scatter(vectors, "dp", tiled=False), width)]
    kept, sent = (
        jnp.stack([lax.dynamic_index_in_dim(vectors, dp ^ mask ^ core, 0, keepdims=False) for mask in KEEP])
        for core in (0, PAIR)
    )
    lines = as_rows(kept + swap(sent, n_dp, PAIR), width)
    return [lines[0]] + [swap(lines[m + 1], n_dp, mask) for m, mask in enumerate(KEEP[1:])]


def chip_sum(terms):
    total = terms[0].astype(F32)
    for item in terms[1:]:
        total += item.astype(F32)
    return total


def gather_kernel(n_a, z_ref, *refs):
    out_ref, refs = refs[-1], refs[:-1]
    n_t = out_ref.shape[0]
    half = (len(refs) - 2 * n_a) // 2
    ends = (0, n_a, 2 * n_a, 2 * n_a + half, len(refs))
    for k in range(n_t):
        to = lax.rem(z_ref[0] + k, n_t)
        at = 0
        for terms in (refs[i:j] for i, j in zip(ends, ends[1:])):
            total = terms[0][k].astype(F32)
            for term in terms[1:]:
                total += term[k].astype(F32)
            rows = total.shape[0]
            out_ref[to, at : at + rows, :] = total.astype(BF)
            at += rows


def gather_shards(tensor, a_terms, lines, up_terms, down_terms):
    groups = (a_terms, lines, up_terms, down_terms)
    n_t, rows_a, width = a_terms[0].shape
    rows = sum(terms[0].shape[1] for terms in groups)
    if rows_a % 16 > 0:
        return turn(jnp.concatenate([chip_sum(terms).astype(BF) for terms in groups], axis=1), -tensor)
    args = tuple(term for terms in groups for term in terms)
    return call(
        functools.partial(gather_kernel, len(a_terms)),
        "gather_shards",
        [((n_t, rows, width), BF)],
        [SMEM] + [VMEM] * len(args),
        (tensor[None].astype(jnp.int32),) + args,
    )[0]


def in_parts(value):
    high = value.astype(BF)
    rest = value - high.astype(F32)
    middle = rest.astype(BF)
    return [high, middle, (rest - middle.astype(F32)).astype(BF)]


def small_vectors(b_qv, b_up):
    value = jnp.concatenate([jnp.pad(b_qv, ((0, 0), (0, b_up.shape[0] - b_qv.shape[1]))), b_up[None]])
    return jnp.concatenate(in_parts(value) + [jnp.zeros((7,) + b_up.shape, BF)])


def local(n_dp, n_t, inputs, doc_ids, ln1_gain, ln1_bias, w_qkv, b_qv, w_out, out_bias, ln2_gain, ln2_bias,
          w_up, b_up, w_down, down_bias, cotangent):
    width = inputs.shape[2]
    part, ff = w_out.shape[0], w_up.shape[1]
    dp = lax.axis_index("dp")
    tensor = lax.axis_index("tensor")
    own_rows = inputs.shape[0] // n_t
    rows = width // n_dp
    each_row = range(own_rows)
    splits = (2, 4) if n_dp == 8 else (1, 1)
    order = jnp.array(KEEP + tuple(m ^ PAIR for m in KEEP), jnp.int32)
    ids = order ^ dp if n_dp == 8 else jnp.zeros_like(order)
    half = n_t // 2
    groups = (tuple(range(half)), tuple(range(half, n_t)))

    def own_piece(whole):
        return lax.dynamic_slice_in_dim(whole, dp * rows, rows, 0)

    def split_row(values):
        values = values.reshape((n_t, own_rows) + values.shape[1:])
        return [values[:, r].reshape(-1, width) for r in each_row]

    def join_row(values):
        blocks = jnp.stack([v.reshape(n_t, -1, width) for v in values], axis=1)
        return blocks.reshape((n_t * own_rows,) + blocks.shape[2:])

    own_a = jnp.concatenate([w_qkv.transpose(1, 2, 0).reshape(3 * part, width), w_out])
    pieces = jnp.concatenate([own_piece(own_a), own_piece(w_up), own_piece(w_down), small_vectors(b_qv, b_up)])
    gathered, moved = gather_others(pieces, tensor, n_t)
    smalls = jnp.concatenate([pieces[None, 3 * rows :], gathered[:, 3 * rows :]]).astype(F32)
    smalls = smalls[:, 0:3] + smalls[:, 3:6] + smalls[:, 6:9]
    stack_a = gathered[None, :, :rows]
    stack_m = jnp.stack([gathered[:, rows : 2 * rows], gathered[:, 2 * rows : 3 * rows]])
    mine_a = chip_pieces(stack_a, n_dp)
    x_rows = trade(after(inputs, *moved))
    mine_m = chip_pieces(after(stack_m, mine_a[-1][0] if n_dp != 8 else (mine_a[1][0], mine_a[3][0])), n_dp)
    sources_a, plan_a = pair_pieces(mine_a, n_dp)
    values_m = [m[0] for m in mine_m]
    vecs = [v[None] for v in (out_bias, ln2_gain, ln2_bias, down_bias)]
    gain, bias = ln1_gain[None], ln1_bias[None]
    docs = lax.dynamic_slice_in_dim(doc_ids, tensor * own_rows, own_rows, 0)
    docs = [docs[r : r + 1] for r in each_row]
    sources_a, x_rows, own_a, vecs, gain, bias, docs, ids, smalls = lax.optimization_barrier(
        (sources_a, x_rows, own_a, vecs, gain, bias, docs, ids, smalls)
    )
    values_m, _, cotangent = lax.optimization_barrier((values_m, x_rows, cotangent))
    mine_m = [(value,) + m[1:] for value, m in zip(values_m, mine_m)]
    x_rows = split_row(x_rows)
    cot_rows = split_row(trade(cotangent))

    def total_of(*items):
        if len(items) == 1:
            return items[0]
        return sum(item.astype(F32) for item in items).astype(items[0].dtype)

    def together(results):
        return [jax.tree.map(total_of, *items) for items in zip(*results)]

    n1ts = [first(gain, bias, x) for x in x_rows]
    seen_one = [attend(groups[0], ids, n1ts[r], own_a, sources_a, plan_a, smalls, docs[r]) for r in each_row]
    mine_m = chip_forward(mine_m, n_dp, n1ts)
    n1ts, values_m = lax.optimization_barrier((n1ts, [m[0] for m in mine_m], seen_one))[:2]
    mine_m = [(value,) + m[1:] for value, m in zip(values_m, mine_m)]
    sources_m, plan_m = pair_pieces(mine_m, n_dp)
    seen_two = [attend(groups[1], ids, n1ts[r], own_a, sources_a, plan_a, smalls, docs[r]) for r in each_row]
    sources_m, cot_rows = lax.optimization_barrier((sources_m, cot_rows, seen_two))[:2]
    made = [
        mlp(splits, ids, x_rows[r], seen_one[r][1], seen_two[r][1], seen_one[r][3], seen_two[r][3], w_up, w_down,
            sources_m, plan_m, smalls, vecs, cot_rows[r])
        for r in each_row
    ]
    gvec, gbup, *dms = together([m[3:] for m in made])
    got_m = pair_swap(dms, n_dp)
    block_out = trade(join_row([m[0] for m in made]))

    def back(gmts, seen):
        items = [attend_back(splits, ids, gmts[r], n1ts[r], *seen[r], docs[r]) for r in each_row]
        return [i[0] for i in items], together([i[1:] for i in items])

    ways_m = ((BY_X, 0), (BY_Y, 1))
    gmts = [m[2] for m in made]
    gpt_two, (gb_two, *da_two) = back(gmts, seen_two)
    got_m, keep_m = lax.optimization_barrier((got_m, dms[0], gpt_two))[:2]
    dms = [keep_m]
    sent_m = [chip_send(dms, got_m, n_dp, *way) for way in ways_m]
    got_two = pair_swap(da_two, n_dp)
    gmts = lax.optimization_barrier((gmts, gpt_two))[0]
    gpt_one, (gb_one, *da_one) = back(gmts, seen_one)
    got_one = pair_swap(da_one, n_dp)
    block_out, got_two, sent_m = lax.optimization_barrier((block_out, got_two, sent_m, gpt_one))[:3]
    keep_m = after(keep_m, gpt_one)
    passed_m = chip_pass([keep_m], got_m, sent_m, n_dp, ways_m)
    gms = lax.optimization_barrier(([m[1] for m in made], gpt_one, block_out, [passed[0] for passed in passed_m]))[0]
    ends = [
        input_back(x_rows[r], gms[r], gain, seen_two[r][3], seen_one[r][3], gpt_two[r], gpt_one[r])
        for r in each_row
    ]
    (gin,) = together([e[1:] for e in ends])
    grad_inputs = trade(join_row([e[0] for e in ends]))
    got_one, got_two, passed_m = lax.optimization_barrier((got_one, got_two, passed_m, ends))[:3]
    block_out = settle(after(block_out, ends))
    gbs = jnp.concatenate([gb_one, gb_two])
    each = width // (n_dp * n_t)
    vectors = jnp.concatenate([gin[0:2], gvec[0:4]])
    vectors = vectors.reshape(6, n_dp, n_t, each).transpose(1, 2, 0, 3).reshape(n_dp, n_t, 6 * each)
    shard = jnp.concatenate(
        [
            gbs.reshape(n_t, 2, n_dp, part // n_dp).transpose(2, 0, 1, 3).reshape(n_dp, n_t, -1),
            gbup.reshape(n_t, n_dp, ff // n_dp).transpose(1, 0, 2),
        ],
        axis=2,
    )
    vectors = jnp.concatenate([jnp.roll(vectors, -tensor, axis=1), shard], axis=2)
    moved_a = chip_direct(((da_one, got_one), (da_two, got_two)), n_dp)
    lines = vectors_direct(after(vectors, moved_a[0]), dp, width, n_dp)
    moved_a, passed_m, lines, grad_inputs = lax.optimization_barrier((moved_a, passed_m, lines, grad_inputs))

    shards = gather_shards(tensor, moved_a, lines, *passed_m)
    share = jnp.sum(trade(shards).astype(F32), axis=0)
    share_a, lines, share_up, share_down = jnp.split(share, (rows, rows + 16, 2 * rows + 16))
    mine = lines[0]
    vec_out = mine[0 : 6 * each].reshape(6, each)
    share_b_qv = mine[6 * each : 6 * each + 2 * (part // n_dp)].reshape(2, part // n_dp)
    share_b_up = mine[6 * each + 2 * (part // n_dp) : 6 * each + (2 * part + ff) // n_dp]
    share_w_qkv = share_a[:, 0 : 3 * part].reshape(rows, 3, part)
    share_w_out = share_a[:, 3 * part :].T
    return (
        block_out,
        grad_inputs,
        vec_out[0],
        vec_out[1],
        share_w_qkv,
        share_b_qv,
        share_w_out,
        vec_out[2],
        vec_out[3],
        vec_out[4],
        share_up,
        share_b_up,
        share_down.T,
        vec_out[5],
    )


def solution(mesh):
    return jax.shard_map(
        functools.partial(local, mesh.shape["dp"], mesh.shape["tensor"]),
        mesh=mesh,
        in_specs=(
            P("dp", "tensor", None),
            P("dp", None),
            P(),
            P(),
            P(None, None, "tensor"),
            P(None, "tensor"),
            P("tensor", None),
            P(),
            P(),
            P(),
            P(None, "tensor"),
            P("tensor"),
            P("tensor", None),
            P(),
            P("dp", "tensor", None),
        ),
        out_specs=(
            P("dp", "tensor", None),
            P("dp", "tensor", None),
            P(("dp", "tensor")),
            P(("dp", "tensor")),
            P("dp", None, "tensor"),
            P(None, ("tensor", "dp")),
            P("tensor", "dp"),
            P(("dp", "tensor")),
            P(("dp", "tensor")),
            P(("dp", "tensor")),
            P("dp", "tensor"),
            P(("tensor", "dp")),
            P("tensor", "dp"),
            P(("dp", "tensor")),
        ),
        check_vma=False,
    )
```

```python
import functools

import jax
import jax.numpy as jnp
from jax import lax
from jax.experimental import pallas as pl
from jax.experimental.pallas import tpu as pltpu
from jax.sharding import PartitionSpec as P

BF = jnp.bfloat16
F32 = jnp.float32
HEAD = 64
EPS = 1e-05
GELU_C = 0.7978845608028654
GELU_A = 0.044715
BLOCK = 256
MIB = 1024 * 1024
KEEP = (0, 2, 6, 4)
PAIR = 1
LONG = 5 * 10**10


def dot(lhs, rhs, lhs_dim, rhs_dim):
    return lax.dot_general(
        lhs, rhs, (((lhs_dim,), (rhs_dim,)), ((), ())), preferred_element_type=F32
    )


def normalize(value):
    mean = jnp.mean(value, axis=-1, keepdims=True)
    centred = value - mean
    variance = jnp.mean(centred * centred, axis=-1, keepdims=True)
    rstd = lax.rsqrt(variance + EPS)
    return centred * rstd, rstd


def norm_backward(grad, xhat, rstd, gain):
    scaled = grad * gain
    mean_e = jnp.mean(scaled, axis=-1, keepdims=True)
    mean_ex = jnp.mean(scaled * xhat, axis=-1, keepdims=True)
    return rstd * (scaled - mean_e - xhat * mean_ex)


def column(line):
    return jnp.broadcast_to(line, (8, line.shape[1])).T[:, 0:1]


def block_rows(index, size=BLOCK):
    return pl.ds(pl.multiple_of(index * size, size), size)


VMEM = pl.BlockSpec(memory_space=pltpu.VMEM)
SMEM = pl.BlockSpec(memory_space=pltpu.SMEM)
HBM = pl.BlockSpec(memory_space=pl.ANY)


def call(kernel, name, outs, specs, args, out_specs=None, vmem=60, scratch=(), grid=(), flops=1):
    shapes = tuple(jax.ShapeDtypeStruct(*o) for o in outs)
    return pl.pallas_call(
        kernel,
        grid=grid,
        out_shape=shapes,
        in_specs=specs,
        out_specs=out_specs or (VMEM,) * len(outs),
        scratch_shapes=list(scratch),
        compiler_params=pltpu.CompilerParams(vmem_limit_bytes=vmem * MIB),
        name=name,
        cost_estimate=pl.CostEstimate(flops=flops, bytes_accessed=1, transcendentals=0),
    )(*args)


def fixed(shape):
    return pl.BlockSpec(shape, lambda *_: (0,) * len(shape), pipeline_mode=pl.Buffered(1))


def nth(shape, base=0):
    return pl.BlockSpec((1,) + tuple(shape[1:]), lambda t: (lax.rem(t + base, shape[0]),) + (0,) * (len(shape) - 1))


def own_copies(owns, wholes, sems):
    return [
        pltpu.make_async_copy(own, whole.at[0], sems.at[0, i]) for i, (own, whole) in enumerate(zip(owns, wholes))
    ]


def piece_copies(ids_ref, sources, plan, wholes, sems, k, slot):
    copies = []
    for src, (place, arrays) in zip(sources, plan):
        rows = src.shape[3]
        for m in range(src.shape[0]):
            at = pl.multiple_of(ids_ref[place + m] * rows, rows)
            for u, array in enumerate(arrays):
                copies.append(
                    pltpu.make_async_copy(
                        src.at[m, u, k - 1], wholes[array].at[slot, pl.ds(at, rows), :], sems.at[slot, len(copies)]
                    )
                )
    return copies


def piece_count(sources):
    return sum(src.shape[0] * src.shape[1] for src in sources)


def fetch(base, count, step, ids_ref, owns, sources, plan, wholes, sems):
    slot = lax.rem(step, 2)
    begins_own = base == 0

    def start():
        @pl.when(step == 0)
        def _():
            for copy in own_copies(owns, wholes, sems) if begins_own else piece_copies(
                ids_ref, sources, plan, wholes, sems, base, 0
            ):
                copy.start()

        @pl.when(step < count - 1)
        def _():
            for copy in piece_copies(ids_ref, sources, plan, wholes, sems, base + step + 1, lax.rem(step + 1, 2)):
                copy.start()

    def wait():
        if begins_own:
            @pl.when(step == 0)
            def _():
                for copy in own_copies(owns, wholes, sems):
                    copy.wait()

        @pl.when(step > 0 if begins_own else step >= 0)
        def _():
            for copy in piece_copies(ids_ref, sources, plan, wholes, sems, base + step, slot):
                copy.wait()

    return start, wait


def first_kernel(gain_ref, bias_ref, x_ref, n1t_ref):
    xhat, _ = normalize(x_ref[...].astype(F32))
    n1t_ref[...] = (xhat * gain_ref[...] + bias_ref[...]).astype(BF).T


def first(gain, bias, x):
    seq, width = x.shape
    return call(
        first_kernel,
        "first",
        [((width, seq), BF)],
        [fixed(gain.shape), fixed(bias.shape), pl.BlockSpec((BLOCK, width), lambda i: (i, 0))],
        (gain, bias, x),
        out_specs=(pl.BlockSpec((width, BLOCK), lambda i: (0, i)),),
        grid=(seq // BLOCK,),
    )[0]


def mask_bias(docs_ref, mask_ref):
    seq = mask_ref.shape[0]
    docs = docs_ref[...]
    docs_col = column(docs)
    for begin in range(0, seq, BLOCK):
        end = begin + BLOCK
        same = docs_col[0:end] == docs[:, begin:end]
        place_k = lax.broadcasted_iota(jnp.int32, (end, BLOCK), 0)
        place_q = begin + lax.broadcasted_iota(jnp.int32, (end, BLOCK), 1)
        allowed = same & (place_k <= place_q)
        mask_ref[0:end, begin:end] = jnp.where(allowed, 0.0, -1e30).astype(F32)


def attend_kernel(base, plan, ids_ref, n1t_ref, small_ref, docs_ref, own_ref, *refs):
    sources, (qkvt_ref, at_ref, lse_ref, a_ref, mask_ref, held_ref, sems) = refs[: len(plan)], refs[len(plan) :]
    step = pl.program_id(0)
    start, wait = fetch(base, pl.num_programs(0), step, ids_ref, [own_ref], sources, plan, [held_ref], sems)
    start()
    seq = n1t_ref.shape[1]
    part = at_ref.shape[1]

    @pl.when(pl.program_id(0) == 0)
    def _():
        mask_bias(docs_ref, mask_ref)

    wait()
    a_ref[0] = held_ref[lax.rem(step, 2)]
    proj = dot(a_ref[0, 0 : 3 * part, :], n1t_ref[...], 1, 0)
    qkvt_ref[0, 0:part, :] = (proj[0:part] + column(small_ref[0, 0:1, 0:part])).astype(BF)
    qkvt_ref[0, part : 2 * part, :] = proj[part : 2 * part].astype(BF)
    qkvt_ref[0, 2 * part :, :] = (proj[2 * part :] + column(small_ref[0, 1:2, 0:part])).astype(BF)
    heads = range(part // HEAD)

    def rows_of(which, h):
        return slice(which * part + h * HEAD, which * part + (h + 1) * HEAD)

    keys = [qkvt_ref[0, rows_of(1, h), :].T for h in heads]
    values = [jnp.concatenate([qkvt_ref[0, rows_of(2, h), :], jnp.ones((16, seq), BF)]) for h in heads]

    def scores_of(begin):
        end = begin + BLOCK
        mask = mask_ref[0:end, begin:end]
        return [dot(keys[h][0:end], qkvt_ref[0, rows_of(0, h), begin:end] * BF(0.125), 1, 0) + mask for h in heads]

    scores = scores_of(0)
    for begin in range(0, seq, BLOCK):
        end = begin + BLOCK
        now = scores
        top = [jnp.max(s, axis=0, keepdims=True) for s in now]
        if end < seq:
            scores = scores_of(end)
        expo = [jnp.exp(s - t).astype(BF) for s, t in zip(now, top)]
        out = [dot(values[h][:, 0:end], expo[h], 1, 0) for h in heads]
        for h in heads:
            total = out[h][HEAD : HEAD + 1]
            at_ref[0, h * HEAD : (h + 1) * HEAD, begin:end] = (out[h][0:HEAD] / total).astype(BF)
            lse_ref[0, h : h + 1, begin:end] = top[h] + jnp.log(total)


def attend(group, ids, n1t, own_a, sources, plan, smalls, docs):
    width, seq = n1t.shape
    base, count, part = group[0], len(group), own_a.shape[0] // 4
    shapes = [(count, 3 * part, seq), (count, part, seq), (count, 8, seq), (count,) + own_a.shape]
    return call(
        functools.partial(attend_kernel, base, plan),
        "attend",
        [(shapes[0], BF), (shapes[1], BF), (shapes[2], F32), (shapes[3], BF)],
        [SMEM, fixed(n1t.shape), nth(smalls.shape, base), fixed(docs.shape)] + [HBM] * (1 + len(sources)),
        (ids, n1t, smalls, docs, own_a) + tuple(sources),
        out_specs=tuple(nth(s) for s in shapes),
        grid=(count,),
        scratch=[
            pltpu.VMEM((seq, seq), F32),
            pltpu.VMEM((2,) + own_a.shape, BF),
            pltpu.SemaphoreType.DMA((2, piece_count(sources))),
        ],
    )


def split_rows(whole_ref, ids_ref, outs, array=0):
    for g, out in enumerate(outs):
        count, rows = out.shape[1], out.shape[3]
        for m in range(count):
            at = pl.multiple_of(ids_ref[g * count + m] * rows, rows)
            out[array, m, 0] = whole_ref[pl.ds(at, rows), :]


def attend_back_kernel(
    n_split, ids_ref, gmt_ref, n1t_ref, a_ref, qkvt_ref, at_ref, lse_ref, docs_ref, gpt_ref, gb_ref, *refs
):
    splits, (mask_ref, gat_ref, dkv_ref, da_ref) = refs[:n_split], refs[n_split:]
    seq = n1t_ref.shape[1]
    part = at_ref.shape[1]

    @pl.when(pl.program_id(0) == 0)
    def _():
        mask_bias(docs_ref, mask_ref)

    gat_ref[...] = dot(a_ref[0, 3 * part :, :], gmt_ref[...], 1, 0).astype(BF)
    heads = range(part // HEAD)

    def rows_of(which, h):
        return slice(which * part + h * HEAD, which * part + (h + 1) * HEAD)

    keys = [qkvt_ref[0, rows_of(1, h), :].T for h in heads]
    values = [qkvt_ref[0, rows_of(2, h), :].T for h in heads]
    items = [(begin, h) for begin in range(0, seq, BLOCK) for h in heads]

    def begin_item(begin, h):
        end = begin + BLOCK
        query = qkvt_ref[0, rows_of(0, h), begin:end] * BF(0.125)
        grad = gat_ref[rows_of(0, h), begin:end]
        scores = dot(keys[h][0:end], query, 1, 0) + mask_ref[0:end, begin:end]
        return query, grad, scores, dot(values[h][0:end], grad, 1, 0)

    ahead = begin_item(*items[0])
    for i, (begin, h) in enumerate(items):
        end = begin + BLOCK
        query, grad, scores, grad_probs = ahead
        if i + 1 < len(items):
            ahead = begin_item(*items[i + 1])
        delta = jnp.sum(
            grad.astype(F32) * at_ref[0, rows_of(0, h), begin:end].astype(F32), axis=0, keepdims=True
        )
        probs = jnp.exp(scores - lse_ref[0, h : h + 1, begin:end])
        grad_scores = (probs * (grad_probs - delta)).astype(BF)
        gpt_ref[0, rows_of(0, h), begin:end] = (
            0.125 * dot(qkvt_ref[0, rows_of(1, h), 0:end], grad_scores, 1, 0)
        ).astype(BF)
        for which, share in ((0, dot(query, grad_scores, 1, 1)), (1, dot(grad, probs.astype(BF), 1, 1))):
            if begin > 0:
                dkv_ref[h, which, :, 0:begin] += share[:, 0:begin]
            dkv_ref[h, which, :, begin:end] = share[:, begin:end]
    for h in heads:
        for which in range(2):
            gpt_ref[0, rows_of(1 + which, h), :] = dkv_ref[h, which].astype(BF)
    ones = jnp.ones((8, seq), BF)
    gb_ref[0, 0:1, :] = dot(ones, gpt_ref[0, 0:part, :], 1, 1)[0:1]
    gb_ref[0, 1:2, :] = dot(ones, gpt_ref[0, 2 * part : 3 * part, :], 1, 1)[0:1]
    da_ref[:, 0 : 3 * part] = dot(n1t_ref[...], gpt_ref[0], 1, 1).astype(BF)
    da_ref[:, 3 * part :] = dot(gmt_ref[...], at_ref[0], 1, 1).astype(BF)
    split_rows(da_ref, ids_ref, splits)


def attend_back(splits, ids, gmt, n1t, qkvt, at, lse, a_part, docs):
    width, seq = n1t.shape
    part = at.shape[1]
    n_split, blocks = splits
    count = at.shape[0]
    cut = (1, blocks, count, width // (n_split * blocks), 4 * part)
    cut_spec = pl.BlockSpec((1, blocks, 1) + cut[3:], lambda t: (0, 0, t, 0, 0))
    return call(
        functools.partial(attend_back_kernel, n_split),
        "attend_back",
        [((count, 3 * part, seq), BF), ((count, 2, part), F32)] + [(cut, BF)] * n_split,
        [SMEM, fixed(gmt.shape), fixed(n1t.shape), nth(a_part.shape), nth(qkvt.shape), nth(at.shape),
         nth(lse.shape), fixed(docs.shape)],
        (ids, gmt, n1t, a_part, qkvt, at, lse, docs),
        out_specs=(nth((count, 3 * part, seq)), nth((count, 2, part))) + (cut_spec,) * n_split,
        grid=(count,),
        scratch=[
            pltpu.VMEM((seq, seq), F32),
            pltpu.VMEM((part, seq), BF),
            pltpu.VMEM((part // HEAD, 2, HEAD, seq), F32),
            pltpu.VMEM((width, 4 * part), BF),
        ],
    )


def mlp_kernel(
    n_t, n_split, plan, ids_ref, x_ref, at_one_ref, at_two_ref, out_one_ref, out_two_ref, small_ref,
    out_bias_ref, gain_ref, bias_ref, down_bias_ref, own_up_ref, own_down_ref, *refs
):
    sources, refs = refs[: len(plan)], refs[len(plan) :]
    cot_ref, out_ref, *refs = refs
    gm_ref, gmt_ref, gvec_ref, gbup_ref = refs[:4]
    splits = refs[4 : 4 + n_split]
    (mixed_ref, n2_ref, n2t_ref, cott_ref, total_ref, grad_ref, act_ref, gpre_ref, dm_ref,
     up_all_ref, down_all_ref, sems) = refs[4 + n_split :]
    seq, width = x_ref.shape
    step_t = pl.program_id(0)
    blocks = seq // BLOCK
    slot = lax.rem(step_t, 2)
    wholes = [up_all_ref, down_all_ref]
    start, wait = fetch(0, n_t, step_t, ids_ref, [own_up_ref, own_down_ref], sources, plan, wholes, sems)
    up_ref, down_ref = up_all_ref.at[slot], down_all_ref.at[slot]
    start()

    @pl.when(step_t == 0)
    def _():
        gvec_ref[...] = jnp.zeros_like(gvec_ref)

        @pl.loop(0, blocks)
        def _(step):
            rows = block_rows(step)
            total = x_ref[rows, :].astype(F32) + out_bias_ref[...]
            for at_ref, w_out_ref in ((at_one_ref, out_one_ref), (at_two_ref, out_two_ref)):
                for t in range(at_ref.shape[0]):
                    total += dot(at_ref[t, :, rows].T, w_out_ref[t], 1, 0)
            mixed_ref[rows, :] = total
            xhat, _ = normalize(total)
            normed = (xhat * gain_ref[...] + bias_ref[...]).astype(BF)
            n2_ref[rows, :] = normed
            n2t_ref[:, rows] = normed.T
            held = cot_ref[rows, :]
            cott_ref[:, rows] = held.T
            gvec_ref[3:4, :] += jnp.sum(held.astype(F32), axis=0, keepdims=True)
            total_ref[rows, :] = jnp.zeros((BLOCK, width), F32)
            grad_ref[rows, :] = jnp.zeros((BLOCK, width), F32)

    wait()
    bias = small_ref[0, 2:3, :]

    def one(step, sums):
        rows = block_rows(step)
        pre = dot(n2_ref[rows, :], up_ref[...], 1, 0) + bias
        grad_act = dot(cot_ref[rows, :], down_ref[...], 1, 1)
        square = pre * pre
        curve = jnp.tanh(pre * (GELU_C + (GELU_C * GELU_A) * square))
        half = 0.5 + 0.5 * curve
        act = (pre * half).astype(BF)
        slope = half + (half - half * curve) * pre * (GELU_C + (3 * GELU_C * GELU_A) * square)
        grad_pre = (slope * grad_act).astype(BF)
        act_ref[rows, :] = act
        gpre_ref[rows, :] = grad_pre
        total_ref[rows, :] += dot(act, down_ref[...], 1, 0)
        grad_ref[rows, :] += dot(grad_pre, up_ref[...], 1, 1)
        return sums + jnp.sum(grad_pre.astype(F32), axis=0, keepdims=True)

    gbup_ref[0] = lax.fori_loop(0, blocks, one, jnp.zeros(bias.shape, F32), unroll=True)
    dm_ref[...] = dot(n2t_ref[...], gpre_ref[...], 1, 0).astype(BF)
    split_rows(dm_ref, ids_ref, splits, 0)
    dm_ref[...] = dot(cott_ref[...], act_ref[...], 1, 0).astype(BF)
    split_rows(dm_ref, ids_ref, splits, 1)

    @pl.when(step_t == n_t - 1)
    def _():
        @pl.loop(0, blocks)
        def _(step):
            rows = block_rows(step)
            xhat, rstd = normalize(mixed_ref[rows, :])
            grad_n = grad_ref[rows, :]
            grad_mixed = cot_ref[rows, :].astype(F32) + norm_backward(grad_n, xhat, rstd, gain_ref[...])
            gm_ref[rows, :] = grad_mixed.astype(BF)
            gmt_ref[:, rows] = grad_mixed.astype(BF).T
            gvec_ref[0:1, :] += jnp.sum(grad_mixed, axis=0, keepdims=True)
            gvec_ref[1:2, :] += jnp.sum(grad_n * xhat, axis=0, keepdims=True)
            gvec_ref[2:3, :] += jnp.sum(grad_n, axis=0, keepdims=True)
            out_ref[rows, :] = (mixed_ref[rows, :] + total_ref[rows, :] + down_bias_ref[...]).astype(BF)


def mlp(splits, ids, x, at_one, at_two, a_one, a_two, w_up, w_down, sources, plan, smalls, vecs, cot):
    seq, width = x.shape
    n_t, part = at_one.shape[0] + at_two.shape[0], at_one.shape[1]
    ff = w_up.shape[1]
    n_split, blocks = splits
    cut = (2, blocks, n_t, width // (n_split * blocks), ff)
    cut_spec = pl.BlockSpec((2, blocks, 1) + cut[3:], lambda t: (0, 0, t, 0, 0))
    gbup = (n_t, 1, ff)
    return call(
        functools.partial(mlp_kernel, n_t, n_split, plan),
        "mlp",
        [((seq, width), BF), ((seq, width), BF), ((width, seq), BF), ((8, width), F32), (gbup, F32)]
        + [(cut, BF)] * n_split,
        [SMEM, fixed(x.shape), fixed(at_one.shape), fixed(at_two.shape),
         *[pl.BlockSpec((a.shape[0], part, width), lambda t: (0, 3, 0), pipeline_mode=pl.Buffered(1)) for a in (a_one, a_two)],
         nth(smalls.shape)] + [fixed((1, width))] * 4 + [HBM] * (2 + len(sources)) + [fixed(cot.shape)],
        (ids, x, at_one, at_two, a_one, a_two, smalls) + tuple(vecs) + (w_up, w_down) + tuple(sources) + (cot,),
        out_specs=(fixed((seq, width)), fixed((seq, width)), fixed((width, seq)), fixed((8, width)), nth(gbup))
        + (cut_spec,) * n_split,
        grid=(n_t,),
        scratch=[
            pltpu.VMEM((seq, width), F32),
            pltpu.VMEM((seq, width), BF),
            pltpu.VMEM((width, seq), BF),
            pltpu.VMEM((width, seq), BF),
            pltpu.VMEM((seq, width), F32),
            pltpu.VMEM((seq, width), F32),
            pltpu.VMEM((seq, ff), BF),
            pltpu.VMEM((seq, ff), BF),
            pltpu.VMEM((width, ff), BF),
            pltpu.VMEM((2, width, ff), BF),
            pltpu.VMEM((2, ff, width), BF),
            pltpu.SemaphoreType.DMA((2, max(2, piece_count(sources)))),
        ],
    )


def input_back_kernel(x_ref, gm_ref, gain_ref, a_one_ref, a_two_ref, one_ref, two_ref, out_ref, gvec_ref):

    @pl.when(pl.program_id(0) == 0)
    def _():
        gvec_ref[...] = jnp.zeros_like(gvec_ref)

    gp = jnp.concatenate([ref[t] for ref in (one_ref, two_ref) for t in range(ref.shape[0])]).T
    weights = jnp.concatenate([ref[t] for ref in (a_one_ref, a_two_ref) for t in range(ref.shape[0])])
    grad_n = dot(gp, weights, 1, 0)
    xhat, rstd = normalize(x_ref[...].astype(F32))
    out_ref[...] = (gm_ref[...].astype(F32) + norm_backward(grad_n, xhat, rstd, gain_ref[...])).astype(BF)
    gvec_ref[0:1, :] += jnp.sum(grad_n * xhat, axis=0, keepdims=True)
    gvec_ref[1:2, :] += jnp.sum(grad_n, axis=0, keepdims=True)


def input_back(x, gm, gain, a_one, a_two, one, two):
    seq, width = x.shape
    part3 = one.shape[1]
    by_rows = pl.BlockSpec((BLOCK, width), lambda i: (i, 0))

    def by_columns(gpt):
        return pl.BlockSpec(gpt.shape[:2] + (BLOCK,), lambda i: (0, 0, i))

    return call(
        input_back_kernel,
        "input_back",
        [((seq, width), BF), ((8, width), F32)],
        [by_rows, by_rows, fixed(gain.shape), fixed((one.shape[0], part3, width)), fixed((two.shape[0], part3, width)),
         by_columns(one), by_columns(two)],
        (x, gm, gain, a_one, a_two, one, two),
        out_specs=(by_rows, fixed((8, width))),
        grid=(seq // BLOCK,),
        flops=LONG,
    )


def settle_kernel(value_ref, out_ref):
    out_ref[...] = value_ref[...]


def settle(value):
    spec = pl.BlockSpec((1,) + value.shape[1:], lambda i: (i, 0, 0))
    return call(
        settle_kernel, "settle", [(value.shape, value.dtype)], [spec], (value,), out_specs=(spec,), grid=value.shape[:1]
    )[0]


def trade(value):
    return lax.all_to_all(value, "tensor", 0, 0, tiled=True)


def turn(value, by):
    return jnp.roll(value, -by, axis=0)


def swap(value, n_dp, mask):
    return lax.ppermute(value, "dp", [(i, i ^ mask) for i in range(n_dp)])


def after(value, *others):
    return lax.optimization_barrier((value,) + others)[0]


def gather_others(value, tensor, n_t):
    if n_t != 4:
        gathered = trade(jnp.broadcast_to(value[None], (n_t,) + value.shape))
        return turn(gathered, tensor + 1)[: n_t - 1], gathered

    def line(item, pairs):
        return lax.ppermute(item, "tensor", pairs)

    two = line(value, [(0, 2), (1, 3), (2, 0), (3, 1)])
    up = line(value, [(0, 1), (1, 2), (2, 3)])
    down = line(value, [(1, 0), (2, 1), (3, 2)])
    far = line(two, [(2, 3), (1, 0)])
    return jnp.stack([jnp.where(tensor == 3, far, down), two, jnp.where(tensor == 0, far, up)]), (up, down, far)


def chip_pieces(pieces, n_dp):
    if n_dp != 8:
        return [(lax.all_gather(pieces, "dp", axis=2, tiled=True), 0, tuple(range(pieces.shape[0])))]
    arrays = tuple(range(pieces.shape[0]))
    if len(arrays) == 1:
        return [(pieces, 0, arrays)] + [(swap(pieces, n_dp, mask), m + 1, arrays) for m, mask in enumerate(KEEP[1:])]
    by_x, by_y = swap(pieces, n_dp, KEEP[1]), swap(pieces, n_dp, KEEP[3])
    return [(pieces, 0, arrays), (by_x, 1, arrays), (by_y, 3, arrays)]


def chip_forward(mine, n_dp, *others):
    if n_dp != 8:
        return mine
    pieces, by_x, by_y = mine
    from_x, from_y = lax.optimization_barrier((by_x[0], by_y[0]) + others)[:2]
    first_far = swap(from_y[0:1], n_dp, KEEP[1])
    second_far = swap(from_x[1:2], n_dp, KEEP[3])
    return [pieces, (from_x,) + by_x[1:], (from_y,) + by_y[1:], (first_far, 2, (0,)), (second_far, 2, (1,))]


def pair_pieces(mine, n_dp):
    if n_dp != 8:
        return [value[None] for value, _, _ in mine], tuple((place, arrays) for _, place, arrays in mine)
    both = mine + [(swap(value, n_dp, PAIR), place + len(KEEP), arrays) for value, place, arrays in mine]
    return [value[None] for value, _, _ in both], tuple((place, arrays) for _, place, arrays in both)


def pair_swap(parts, n_dp):
    return [swap(parts[1], n_dp, PAIR)] if n_dp == 8 else []


BY_X = (slice(1, 3), 2, 3, 4, 0)
BY_Y = (slice(2, 4), 4, 1, 2, 1)


def chip_send(parts, got, n_dp, way, select):
    if n_dp != 8:
        whole = parts[0][select, 0]
        return lax.psum_scatter(whole, "dp", scatter_dimension=whole.ndim - 2, tiled=True)
    places, near = way[:2]
    value = parts[0][select, places].astype(F32) + got[0][select, places].astype(F32)
    return swap(value.astype(BF), n_dp, near)


def pass_kernel(*refs):
    count = len(refs) // 8
    for i in range(count):
        keep, got, sent, keep_far, got_far, sent_far = (ref[...].astype(F32) for ref in refs[6 * i : 6 * i + 6])
        here_ref, there_ref = refs[6 * count + 2 * i : 6 * count + 2 * i + 2]
        here_ref[...] = (keep + got + sent).astype(BF)[0, 0]
        there_ref[...] = (keep_far + got_far + sent_far).astype(BF)[0, 0]


def chip_pass(parts, got, sents, n_dp, items):
    if n_dp != 8:
        return [[sent] for sent in sents]
    _, _, sets, rows, cols = parts[0].shape
    args, specs = [], []

    def take(value, select, place):
        args.append(value)
        specs.append(pl.BlockSpec((1, 1, 1, rows, cols), lambda t: (select, place, t, 0, 0)))

    for sent, (way, select) in zip(sents, items):
        _, _, far, _, first = way
        for place, back in ((0, first), (far, 1 - first)):
            take(parts[0], select, place)
            take(got[0], select, place)
            take(sent[None], 0, back)
    made = pl.pallas_call(
        pass_kernel,
        grid=(sets,),
        out_shape=(jax.ShapeDtypeStruct((sets, rows, cols), BF),) * (2 * len(items)),
        in_specs=specs,
        out_specs=(pl.BlockSpec((1, rows, cols), lambda t: (t, 0, 0)),) * (2 * len(items)),
        compiler_params=pltpu.CompilerParams(vmem_limit_bytes=60 * MIB),
        name="chip_pass",
        cost_estimate=pl.CostEstimate(flops=LONG, bytes_accessed=1, transcendentals=0),
    )(*args)
    return [[made[2 * i], swap(made[2 * i + 1], n_dp, way[3])] for i, (way, _) in enumerate(items)]


def pair_kernel(*refs):
    sources, outs = refs[: -len(KEEP)], refs[-len(KEEP) :]
    at = 0
    for keep, got in zip(sources[0::2], sources[1::2]):
        for m, out in enumerate(outs):
            for t in range(keep.shape[2]):
                out[at + t] = (keep[0, m, t].astype(F32) + got[0, m, t].astype(F32)).astype(BF)
        at += keep.shape[2]


def as_rows(vectors, width):
    pad = [(0, 0)] * (vectors.ndim - 1) + [(0, 15), (0, width - vectors.shape[-1])]
    return jnp.pad(vectors[..., None, :].astype(BF), pad)


def chip_direct(groups, n_dp):
    if n_dp != 8:
        whole = jnp.concatenate([parts[0][0, 0] for parts, _ in groups])
        return [lax.psum_scatter(whole, "dp", scatter_dimension=whole.ndim - 2, tiled=True)]
    args = [value for parts, got in groups for value in (parts[0], got[0])]
    shape = (sum(parts[0].shape[2] for parts, _ in groups),) + args[0].shape[3:]
    made = call(pair_kernel, "pair", [(shape, BF)] * len(KEEP), [VMEM] * len(args), tuple(args))
    return [made[0]] + [swap(made[m + 1], n_dp, mask) for m, mask in enumerate(KEEP[1:])]


def vectors_direct(vectors, dp, width, n_dp):
    if n_dp != 8:
        return [as_rows(lax.psum_scatter(vectors, "dp", tiled=False), width)]
    kept, sent = (
        jnp.stack([lax.dynamic_index_in_dim(vectors, dp ^ mask ^ core, 0, keepdims=False) for mask in KEEP])
        for core in (0, PAIR)
    )
    lines = as_rows(kept + swap(sent, n_dp, PAIR), width)
    return [lines[0]] + [swap(lines[m + 1], n_dp, mask) for m, mask in enumerate(KEEP[1:])]


def chip_sum(terms):
    total = terms[0].astype(F32)
    for item in terms[1:]:
        total += item.astype(F32)
    return total


def gather_kernel(n_a, z_ref, *refs):
    out_ref, refs = refs[-1], refs[:-1]
    n_t = out_ref.shape[0]
    half = (len(refs) - 2 * n_a) // 2
    ends = (0, n_a, 2 * n_a, 2 * n_a + half, len(refs))
    for k in range(n_t):
        to = lax.rem(z_ref[0] + k, n_t)
        at = 0
        for terms in (refs[i:j] for i, j in zip(ends, ends[1:])):
            total = terms[0][k].astype(F32)
            for term in terms[1:]:
                total += term[k].astype(F32)
            rows = total.shape[0]
            out_ref[to, at : at + rows, :] = total.astype(BF)
            at += rows


def gather_shards(tensor, a_terms, lines, up_terms, down_terms):
    groups = (a_terms, lines, up_terms, down_terms)
    n_t, rows_a, width = a_terms[0].shape
    rows = sum(terms[0].shape[1] for terms in groups)
    if rows_a % 16 > 0:
        return turn(jnp.concatenate([chip_sum(terms).astype(BF) for terms in groups], axis=1), -tensor)
    args = tuple(term for terms in groups for term in terms)
    return call(
        functools.partial(gather_kernel, len(a_terms)),
        "gather_shards",
        [((n_t, rows, width), BF)],
        [SMEM] + [VMEM] * len(args),
        (tensor[None].astype(jnp.int32),) + args,
    )[0]


def in_parts(value):
    high = value.astype(BF)
    rest = value - high.astype(F32)
    middle = rest.astype(BF)
    return [high, middle, (rest - middle.astype(F32)).astype(BF)]


def small_vectors(b_qv, b_up):
    value = jnp.concatenate([jnp.pad(b_qv, ((0, 0), (0, b_up.shape[0] - b_qv.shape[1]))), b_up[None]])
    return jnp.concatenate(in_parts(value) + [jnp.zeros((7,) + b_up.shape, BF)])


def local(n_dp, n_t, inputs, doc_ids, ln1_gain, ln1_bias, w_qkv, b_qv, w_out, out_bias, ln2_gain, ln2_bias,
          w_up, b_up, w_down, down_bias, cotangent):
    width = inputs.shape[2]
    part, ff = w_out.shape[0], w_up.shape[1]
    dp = lax.axis_index("dp")
    tensor = lax.axis_index("tensor")
    own_rows = inputs.shape[0] // n_t
    rows = width // n_dp
    each_row = range(own_rows)
    splits = (2, 4) if n_dp == 8 else (1, 1)
    order = jnp.array(KEEP + tuple(m ^ PAIR for m in KEEP), jnp.int32)
    ids = order ^ dp if n_dp == 8 else jnp.zeros_like(order)
    half = n_t // 2
    groups = (tuple(range(half)), tuple(range(half, n_t)))

    def own_piece(whole):
        return lax.dynamic_slice_in_dim(whole, dp * rows, rows, 0)

    def split_row(values):
        values = values.reshape((n_t, own_rows) + values.shape[1:])
        return [values[:, r].reshape(-1, width) for r in each_row]

    def join_row(values):
        blocks = jnp.stack([v.reshape(n_t, -1, width) for v in values], axis=1)
        return blocks.reshape((n_t * own_rows,) + blocks.shape[2:])

    own_a = jnp.concatenate([w_qkv.transpose(1, 2, 0).reshape(3 * part, width), w_out])
    pieces = jnp.concatenate([own_piece(own_a), own_piece(w_up), own_piece(w_down), small_vectors(b_qv, b_up)])
    gathered, moved = gather_others(pieces, tensor, n_t)
    smalls = jnp.concatenate([pieces[None, 3 * rows :], gathered[:, 3 * rows :]]).astype(F32)
    smalls = smalls[:, 0:3] + smalls[:, 3:6] + smalls[:, 6:9]
    stack_a = gathered[None, :, :rows]
    stack_m = jnp.stack([gathered[:, rows : 2 * rows], gathered[:, 2 * rows : 3 * rows]])
    mine_a = chip_pieces(stack_a, n_dp)
    x_rows = trade(after(inputs, *moved))
    mine_m = chip_pieces(after(stack_m, mine_a[-1][0] if n_dp != 8 else (mine_a[1][0], mine_a[3][0])), n_dp)
    sources_a, plan_a = pair_pieces(mine_a, n_dp)
    values_m = [m[0] for m in mine_m]
    vecs = [v[None] for v in (out_bias, ln2_gain, ln2_bias, down_bias)]
    gain, bias = ln1_gain[None], ln1_bias[None]
    docs = lax.dynamic_slice_in_dim(doc_ids, tensor * own_rows, own_rows, 0)
    docs = [docs[r : r + 1] for r in each_row]
    sources_a, x_rows, own_a, vecs, gain, bias, docs, ids, smalls = lax.optimization_barrier(
        (sources_a, x_rows, own_a, vecs, gain, bias, docs, ids, smalls)
    )
    values_m, _, cotangent = lax.optimization_barrier((values_m, x_rows, cotangent))
    mine_m = [(value,) + m[1:] for value, m in zip(values_m, mine_m)]
    x_rows = split_row(x_rows)
    cot_rows = split_row(trade(cotangent))

    def total_of(*items):
        if len(items) == 1:
            return items[0]
        return sum(item.astype(F32) for item in items).astype(items[0].dtype)

    def together(results):
        return [jax.tree.map(total_of, *items) for items in zip(*results)]

    n1ts = [first(gain, bias, x) for x in x_rows]
    seen_one = [attend(groups[0], ids, n1ts[r], own_a, sources_a, plan_a, smalls, docs[r]) for r in each_row]
    mine_m = chip_forward(mine_m, n_dp, n1ts)
    n1ts, values_m = lax.optimization_barrier((n1ts, [m[0] for m in mine_m], seen_one))[:2]
    mine_m = [(value,) + m[1:] for value, m in zip(values_m, mine_m)]
    sources_m, plan_m = pair_pieces(mine_m, n_dp)
    seen_two = [attend(groups[1], ids, n1ts[r], own_a, sources_a, plan_a, smalls, docs[r]) for r in each_row]
    sources_m, cot_rows = lax.optimization_barrier((sources_m, cot_rows, seen_two))[:2]
    made = [
        mlp(splits, ids, x_rows[r], seen_one[r][1], seen_two[r][1], seen_one[r][3], seen_two[r][3], w_up, w_down,
            sources_m, plan_m, smalls, vecs, cot_rows[r])
        for r in each_row
    ]
    gvec, gbup, *dms = together([m[3:] for m in made])
    got_m = pair_swap(dms, n_dp)
    block_out = trade(join_row([m[0] for m in made]))

    def back(gmts, seen):
        items = [attend_back(splits, ids, gmts[r], n1ts[r], *seen[r], docs[r]) for r in each_row]
        return [i[0] for i in items], together([i[1:] for i in items])

    ways_m = ((BY_X, 0), (BY_Y, 1))
    gmts = [m[2] for m in made]
    gpt_two, (gb_two, *da_two) = back(gmts, seen_two)
    got_m, keep_m = lax.optimization_barrier((got_m, dms[0], gpt_two))[:2]
    dms = [keep_m]
    sent_m = [chip_send(dms, got_m, n_dp, *way) for way in ways_m]
    got_two = pair_swap(da_two, n_dp)
    gmts = lax.optimization_barrier((gmts, gpt_two))[0]
    gpt_one, (gb_one, *da_one) = back(gmts, seen_one)
    got_one = pair_swap(da_one, n_dp)
    block_out, got_two, sent_m = lax.optimization_barrier((block_out, got_two, sent_m, gpt_one))[:3]
    moved_a = chip_direct(((da_one, got_one), (da_two, got_two)), n_dp)
    gms = lax.optimization_barrier(([m[1] for m in made], gpt_one, block_out, sent_m, moved_a[0]))[0]
    ends = [
        input_back(x_rows[r], gms[r], gain, seen_two[r][3], seen_one[r][3], gpt_two[r], gpt_one[r])
        for r in each_row
    ]
    (gin,) = together([e[1:] for e in ends])
    grad_inputs = trade(join_row([e[0] for e in ends]))
    gbs = jnp.concatenate([gb_one, gb_two])
    each = width // (n_dp * n_t)
    vectors = jnp.concatenate([gin[0:2], gvec[0:4]])
    vectors = vectors.reshape(6, n_dp, n_t, each).transpose(1, 2, 0, 3).reshape(n_dp, n_t, 6 * each)
    shard = jnp.concatenate(
        [
            gbs.reshape(n_t, 2, n_dp, part // n_dp).transpose(2, 0, 1, 3).reshape(n_dp, n_t, -1),
            gbup.reshape(n_t, n_dp, ff // n_dp).transpose(1, 0, 2),
        ],
        axis=2,
    )
    vectors = jnp.concatenate([jnp.roll(vectors, -tensor, axis=1), shard], axis=2)
    lines = vectors_direct(after(vectors, moved_a[1:2]), dp, width, n_dp)
    passed_m = chip_pass([after(keep_m, ends, moved_a)], got_m, sent_m, n_dp, ways_m)
    block_out = settle(after(block_out, ends))
    moved_a, passed_m, lines, grad_inputs = lax.optimization_barrier((moved_a, passed_m, lines, grad_inputs))

    shards = gather_shards(tensor, moved_a, lines, *passed_m)
    share = jnp.sum(trade(shards).astype(F32), axis=0)
    share_a, lines, share_up, share_down = jnp.split(share, (rows, rows + 16, 2 * rows + 16))
    mine = lines[0]
    vec_out = mine[0 : 6 * each].reshape(6, each)
    share_b_qv = mine[6 * each : 6 * each + 2 * (part // n_dp)].reshape(2, part // n_dp)
    share_b_up = mine[6 * each + 2 * (part // n_dp) : 6 * each + (2 * part + ff) // n_dp]
    share_w_qkv = share_a[:, 0 : 3 * part].reshape(rows, 3, part)
    share_w_out = share_a[:, 3 * part :].T
    return (
        block_out,
        grad_inputs,
        vec_out[0],
        vec_out[1],
        share_w_qkv,
        share_b_qv,
        share_w_out,
        vec_out[2],
        vec_out[3],
        vec_out[4],
        share_up,
        share_b_up,
        share_down.T,
        vec_out[5],
    )


def solution(mesh):
    return jax.shard_map(
        functools.partial(local, mesh.shape["dp"], mesh.shape["tensor"]),
        mesh=mesh,
        in_specs=(
            P("dp", "tensor", None),
            P("dp", None),
            P(),
            P(),
            P(None, None, "tensor"),
            P(None, "tensor"),
            P("tensor", None),
            P(),
            P(),
            P(),
            P(None, "tensor"),
            P("tensor"),
            P("tensor", None),
            P(),
            P("dp", "tensor", None),
        ),
        out_specs=(
            P("dp", "tensor", None),
            P("dp", "tensor", None),
            P(("dp", "tensor")),
            P(("dp", "tensor")),
            P("dp", None, "tensor"),
            P(None, ("tensor", "dp")),
            P("tensor", "dp"),
            P(("dp", "tensor")),
            P(("dp", "tensor")),
            P(("dp", "tensor")),
            P("dp", "tensor"),
            P(("tensor", "dp")),
            P("tensor", "dp"),
            P(("dp", "tensor")),
        ),
        check_vma=False,
    )
```

```python
import functools

import jax
import jax.numpy as jnp
from jax import lax
from jax.experimental import pallas as pl
from jax.experimental.pallas import tpu as pltpu
from jax.sharding import PartitionSpec as P

BF = jnp.bfloat16
F32 = jnp.float32
HEAD = 64
EPS = 1e-05
GELU_C = 0.7978845608028654
GELU_A = 0.044715
BLOCK = 256
MIB = 1024 * 1024
KEEP = (0, 2, 6, 4)
PAIR = 1
LONG = 5 * 10**10


def dot(lhs, rhs, lhs_dim, rhs_dim):
    return lax.dot_general(
        lhs, rhs, (((lhs_dim,), (rhs_dim,)), ((), ())), preferred_element_type=F32
    )


def normalize(value):
    mean = jnp.mean(value, axis=-1, keepdims=True)
    centred = value - mean
    variance = jnp.mean(centred * centred, axis=-1, keepdims=True)
    rstd = lax.rsqrt(variance + EPS)
    return centred * rstd, rstd


def norm_backward(grad, xhat, rstd, gain):
    scaled = grad * gain
    mean_e = jnp.mean(scaled, axis=-1, keepdims=True)
    mean_ex = jnp.mean(scaled * xhat, axis=-1, keepdims=True)
    return rstd * (scaled - mean_e - xhat * mean_ex)


def column(line):
    return jnp.broadcast_to(line, (8, line.shape[1])).T[:, 0:1]


def block_rows(index, size=BLOCK):
    return pl.ds(pl.multiple_of(index * size, size), size)


VMEM = pl.BlockSpec(memory_space=pltpu.VMEM)
SMEM = pl.BlockSpec(memory_space=pltpu.SMEM)
HBM = pl.BlockSpec(memory_space=pl.ANY)


def call(kernel, name, outs, specs, args, out_specs=None, vmem=60, scratch=(), grid=(), flops=1):
    shapes = tuple(jax.ShapeDtypeStruct(*o) for o in outs)
    return pl.pallas_call(
        kernel,
        grid=grid,
        out_shape=shapes,
        in_specs=specs,
        out_specs=out_specs or (VMEM,) * len(outs),
        scratch_shapes=list(scratch),
        compiler_params=pltpu.CompilerParams(vmem_limit_bytes=vmem * MIB),
        name=name,
        cost_estimate=pl.CostEstimate(flops=flops, bytes_accessed=1, transcendentals=0),
    )(*args)


def fixed(shape):
    return pl.BlockSpec(shape, lambda *_: (0,) * len(shape), pipeline_mode=pl.Buffered(1))


def nth(shape, base=0):
    return pl.BlockSpec((1,) + tuple(shape[1:]), lambda t: (lax.rem(t + base, shape[0]),) + (0,) * (len(shape) - 1))


def own_copies(owns, wholes, sems):
    return [
        pltpu.make_async_copy(own, whole.at[0], sems.at[0, i]) for i, (own, whole) in enumerate(zip(owns, wholes))
    ]


def piece_copies(ids_ref, sources, plan, wholes, sems, k, slot):
    copies = []
    for src, (place, arrays) in zip(sources, plan):
        rows = src.shape[3]
        for m in range(src.shape[0]):
            at = pl.multiple_of(ids_ref[place + m] * rows, rows)
            for u, array in enumerate(arrays):
                copies.append(
                    pltpu.make_async_copy(
                        src.at[m, u, k - 1], wholes[array].at[slot, pl.ds(at, rows), :], sems.at[slot, len(copies)]
                    )
                )
    return copies


def piece_count(sources):
    return sum(src.shape[0] * src.shape[1] for src in sources)


def fetch(base, count, step, ids_ref, owns, sources, plan, wholes, sems):
    slot = lax.rem(step, 2)
    begins_own = base == 0

    def start():
        @pl.when(step == 0)
        def _():
            for copy in own_copies(owns, wholes, sems) if begins_own else piece_copies(
                ids_ref, sources, plan, wholes, sems, base, 0
            ):
                copy.start()

        @pl.when(step < count - 1)
        def _():
            for copy in piece_copies(ids_ref, sources, plan, wholes, sems, base + step + 1, lax.rem(step + 1, 2)):
                copy.start()

    def wait():
        if begins_own:
            @pl.when(step == 0)
            def _():
                for copy in own_copies(owns, wholes, sems):
                    copy.wait()

        @pl.when(step > 0 if begins_own else step >= 0)
        def _():
            for copy in piece_copies(ids_ref, sources, plan, wholes, sems, base + step, slot):
                copy.wait()

    return start, wait


def first_kernel(gain_ref, bias_ref, x_ref, n1t_ref):
    xhat, _ = normalize(x_ref[...].astype(F32))
    n1t_ref[...] = (xhat * gain_ref[...] + bias_ref[...]).astype(BF).T


def first(gain, bias, x):
    seq, width = x.shape
    return call(
        first_kernel,
        "first",
        [((width, seq), BF)],
        [fixed(gain.shape), fixed(bias.shape), pl.BlockSpec((BLOCK, width), lambda i: (i, 0))],
        (gain, bias, x),
        out_specs=(pl.BlockSpec((width, BLOCK), lambda i: (0, i)),),
        grid=(seq // BLOCK,),
    )[0]


def mask_bias(docs_ref, mask_ref):
    seq = mask_ref.shape[0]
    docs = docs_ref[...]
    docs_col = column(docs)
    for begin in range(0, seq, BLOCK):
        end = begin + BLOCK
        same = docs_col[0:end] == docs[:, begin:end]
        place_k = lax.broadcasted_iota(jnp.int32, (end, BLOCK), 0)
        place_q = begin + lax.broadcasted_iota(jnp.int32, (end, BLOCK), 1)
        allowed = same & (place_k <= place_q)
        mask_ref[0:end, begin:end] = jnp.where(allowed, 0.0, -1e30).astype(F32)


def attend_kernel(base, plan, ids_ref, n1t_ref, small_ref, docs_ref, own_ref, *refs):
    sources, (qkvt_ref, at_ref, lse_ref, a_ref, mask_ref, held_ref, sems) = refs[: len(plan)], refs[len(plan) :]
    step = pl.program_id(0)
    start, wait = fetch(base, pl.num_programs(0), step, ids_ref, [own_ref], sources, plan, [held_ref], sems)
    start()
    seq = n1t_ref.shape[1]
    part = at_ref.shape[1]

    @pl.when(pl.program_id(0) == 0)
    def _():
        mask_bias(docs_ref, mask_ref)

    wait()
    a_ref[0] = held_ref[lax.rem(step, 2)]
    proj = dot(a_ref[0, 0 : 3 * part, :], n1t_ref[...], 1, 0)
    qkvt_ref[0, 0:part, :] = (proj[0:part] + column(small_ref[0, 0:1, 0:part])).astype(BF)
    qkvt_ref[0, part : 2 * part, :] = proj[part : 2 * part].astype(BF)
    qkvt_ref[0, 2 * part :, :] = (proj[2 * part :] + column(small_ref[0, 1:2, 0:part])).astype(BF)
    heads = range(part // HEAD)

    def rows_of(which, h):
        return slice(which * part + h * HEAD, which * part + (h + 1) * HEAD)

    keys = [qkvt_ref[0, rows_of(1, h), :].T for h in heads]
    values = [jnp.concatenate([qkvt_ref[0, rows_of(2, h), :], jnp.ones((16, seq), BF)]) for h in heads]

    def scores_of(begin):
        end = begin + BLOCK
        mask = mask_ref[0:end, begin:end]
        return [dot(keys[h][0:end], qkvt_ref[0, rows_of(0, h), begin:end] * BF(0.125), 1, 0) + mask for h in heads]

    scores = scores_of(0)
    for begin in range(0, seq, BLOCK):
        end = begin + BLOCK
        now = scores
        top = [jnp.max(s, axis=0, keepdims=True) for s in now]
        if end < seq:
            scores = scores_of(end)
        expo = [jnp.exp(s - t).astype(BF) for s, t in zip(now, top)]
        out = [dot(values[h][:, 0:end], expo[h], 1, 0) for h in heads]
        for h in heads:
            total = out[h][HEAD : HEAD + 1]
            at_ref[0, h * HEAD : (h + 1) * HEAD, begin:end] = (out[h][0:HEAD] / total).astype(BF)
            lse_ref[0, h : h + 1, begin:end] = top[h] + jnp.log(total)


def attend(group, ids, n1t, own_a, sources, plan, smalls, docs):
    width, seq = n1t.shape
    base, count, part = group[0], len(group), own_a.shape[0] // 4
    shapes = [(count, 3 * part, seq), (count, part, seq), (count, 8, seq), (count,) + own_a.shape]
    return call(
        functools.partial(attend_kernel, base, plan),
        "attend",
        [(shapes[0], BF), (shapes[1], BF), (shapes[2], F32), (shapes[3], BF)],
        [SMEM, fixed(n1t.shape), nth(smalls.shape, base), fixed(docs.shape)] + [HBM] * (1 + len(sources)),
        (ids, n1t, smalls, docs, own_a) + tuple(sources),
        out_specs=tuple(nth(s) for s in shapes),
        grid=(count,),
        scratch=[
            pltpu.VMEM((seq, seq), F32),
            pltpu.VMEM((2,) + own_a.shape, BF),
            pltpu.SemaphoreType.DMA((2, piece_count(sources))),
        ],
    )


def split_rows(whole_ref, ids_ref, outs, array=0):
    for g, out in enumerate(outs):
        count, rows = out.shape[1], out.shape[3]
        for m in range(count):
            at = pl.multiple_of(ids_ref[g * count + m] * rows, rows)
            out[array, m, 0] = whole_ref[pl.ds(at, rows), :]


def attend_back_kernel(
    n_split, ids_ref, gmt_ref, n1t_ref, a_ref, qkvt_ref, at_ref, lse_ref, docs_ref, gpt_ref, gb_ref, *refs
):
    splits, (mask_ref, gat_ref, dkv_ref, da_ref) = refs[:n_split], refs[n_split:]
    seq = n1t_ref.shape[1]
    part = at_ref.shape[1]

    @pl.when(pl.program_id(0) == 0)
    def _():
        mask_bias(docs_ref, mask_ref)

    gat_ref[...] = dot(a_ref[0, 3 * part :, :], gmt_ref[...], 1, 0).astype(BF)
    heads = range(part // HEAD)

    def rows_of(which, h):
        return slice(which * part + h * HEAD, which * part + (h + 1) * HEAD)

    keys = [qkvt_ref[0, rows_of(1, h), :].T for h in heads]
    values = [qkvt_ref[0, rows_of(2, h), :].T for h in heads]
    items = [(begin, h) for begin in range(0, seq, BLOCK) for h in heads]

    def begin_item(begin, h):
        end = begin + BLOCK
        query = qkvt_ref[0, rows_of(0, h), begin:end] * BF(0.125)
        grad = gat_ref[rows_of(0, h), begin:end]
        scores = dot(keys[h][0:end], query, 1, 0) + mask_ref[0:end, begin:end]
        return query, grad, scores, dot(values[h][0:end], grad, 1, 0)

    ahead = begin_item(*items[0])
    for i, (begin, h) in enumerate(items):
        end = begin + BLOCK
        query, grad, scores, grad_probs = ahead
        if i + 1 < len(items):
            ahead = begin_item(*items[i + 1])
        delta = jnp.sum(
            grad.astype(F32) * at_ref[0, rows_of(0, h), begin:end].astype(F32), axis=0, keepdims=True
        )
        probs = jnp.exp(scores - lse_ref[0, h : h + 1, begin:end])
        grad_scores = (probs * (grad_probs - delta)).astype(BF)
        gpt_ref[0, rows_of(0, h), begin:end] = (
            0.125 * dot(qkvt_ref[0, rows_of(1, h), 0:end], grad_scores, 1, 0)
        ).astype(BF)
        for which, share in ((0, dot(query, grad_scores, 1, 1)), (1, dot(grad, probs.astype(BF), 1, 1))):
            if begin > 0:
                dkv_ref[h, which, :, 0:begin] += share[:, 0:begin]
            dkv_ref[h, which, :, begin:end] = share[:, begin:end]
    for h in heads:
        for which in range(2):
            gpt_ref[0, rows_of(1 + which, h), :] = dkv_ref[h, which].astype(BF)
    ones = jnp.ones((8, seq), BF)
    gb_ref[0, 0:1, :] = dot(ones, gpt_ref[0, 0:part, :], 1, 1)[0:1]
    gb_ref[0, 1:2, :] = dot(ones, gpt_ref[0, 2 * part : 3 * part, :], 1, 1)[0:1]
    da_ref[:, 0 : 3 * part] = dot(n1t_ref[...], gpt_ref[0], 1, 1).astype(BF)
    da_ref[:, 3 * part :] = dot(gmt_ref[...], at_ref[0], 1, 1).astype(BF)
    split_rows(da_ref, ids_ref, splits)


def attend_back(splits, ids, gmt, n1t, qkvt, at, lse, a_part, docs):
    width, seq = n1t.shape
    part = at.shape[1]
    n_split, blocks = splits
    count = at.shape[0]
    cut = (1, blocks, count, width // (n_split * blocks), 4 * part)
    cut_spec = pl.BlockSpec((1, blocks, 1) + cut[3:], lambda t: (0, 0, t, 0, 0))
    return call(
        functools.partial(attend_back_kernel, n_split),
        "attend_back",
        [((count, 3 * part, seq), BF), ((count, 2, part), F32)] + [(cut, BF)] * n_split,
        [SMEM, fixed(gmt.shape), fixed(n1t.shape), nth(a_part.shape), nth(qkvt.shape), nth(at.shape),
         nth(lse.shape), fixed(docs.shape)],
        (ids, gmt, n1t, a_part, qkvt, at, lse, docs),
        out_specs=(nth((count, 3 * part, seq)), nth((count, 2, part))) + (cut_spec,) * n_split,
        grid=(count,),
        scratch=[
            pltpu.VMEM((seq, seq), F32),
            pltpu.VMEM((part, seq), BF),
            pltpu.VMEM((part // HEAD, 2, HEAD, seq), F32),
            pltpu.VMEM((width, 4 * part), BF),
        ],
    )


def mlp_kernel(
    n_t, n_split, plan, ids_ref, x_ref, at_one_ref, at_two_ref, out_one_ref, out_two_ref, small_ref,
    out_bias_ref, gain_ref, bias_ref, down_bias_ref, own_up_ref, own_down_ref, *refs
):
    sources, refs = refs[: len(plan)], refs[len(plan) :]
    cot_ref, out_ref, *refs = refs
    gm_ref, gmt_ref, gvec_ref, gbup_ref = refs[:4]
    splits = refs[4 : 4 + n_split]
    (mixed_ref, n2_ref, n2t_ref, cott_ref, total_ref, grad_ref, act_ref, gpre_ref, dm_ref,
     up_all_ref, down_all_ref, sems) = refs[4 + n_split :]
    seq, width = x_ref.shape
    step_t = pl.program_id(0)
    blocks = seq // BLOCK
    slot = lax.rem(step_t, 2)
    wholes = [up_all_ref, down_all_ref]
    start, wait = fetch(0, n_t, step_t, ids_ref, [own_up_ref, own_down_ref], sources, plan, wholes, sems)
    up_ref, down_ref = up_all_ref.at[slot], down_all_ref.at[slot]
    start()

    @pl.when(step_t == 0)
    def _():
        gvec_ref[...] = jnp.zeros_like(gvec_ref)

        @pl.loop(0, blocks)
        def _(step):
            rows = block_rows(step)
            total = x_ref[rows, :].astype(F32) + out_bias_ref[...]
            for at_ref, w_out_ref in ((at_one_ref, out_one_ref), (at_two_ref, out_two_ref)):
                for t in range(at_ref.shape[0]):
                    total += dot(at_ref[t, :, rows].T, w_out_ref[t], 1, 0)
            mixed_ref[rows, :] = total
            xhat, _ = normalize(total)
            normed = (xhat * gain_ref[...] + bias_ref[...]).astype(BF)
            n2_ref[rows, :] = normed
            n2t_ref[:, rows] = normed.T
            held = cot_ref[rows, :]
            cott_ref[:, rows] = held.T
            gvec_ref[3:4, :] += jnp.sum(held.astype(F32), axis=0, keepdims=True)
            total_ref[rows, :] = jnp.zeros((BLOCK, width), F32)
            grad_ref[rows, :] = jnp.zeros((BLOCK, width), F32)

    wait()
    bias = small_ref[0, 2:3, :]

    def one(step, sums):
        rows = block_rows(step)
        pre = dot(n2_ref[rows, :], up_ref[...], 1, 0) + bias
        grad_act = dot(cot_ref[rows, :], down_ref[...], 1, 1)
        square = pre * pre
        curve = jnp.tanh(pre * (GELU_C + (GELU_C * GELU_A) * square))
        half = 0.5 + 0.5 * curve
        act = (pre * half).astype(BF)
        slope = half + (half - half * curve) * pre * (GELU_C + (3 * GELU_C * GELU_A) * square)
        grad_pre = (slope * grad_act).astype(BF)
        act_ref[rows, :] = act
        gpre_ref[rows, :] = grad_pre
        total_ref[rows, :] += dot(act, down_ref[...], 1, 0)
        grad_ref[rows, :] += dot(grad_pre, up_ref[...], 1, 1)
        return sums + jnp.sum(grad_pre.astype(F32), axis=0, keepdims=True)

    gbup_ref[0] = lax.fori_loop(0, blocks, one, jnp.zeros(bias.shape, F32), unroll=True)
    dm_ref[...] = dot(n2t_ref[...], gpre_ref[...], 1, 0).astype(BF)
    split_rows(dm_ref, ids_ref, splits, 0)
    dm_ref[...] = dot(cott_ref[...], act_ref[...], 1, 0).astype(BF)
    split_rows(dm_ref, ids_ref, splits, 1)

    @pl.when(step_t == n_t - 1)
    def _():
        @pl.loop(0, blocks)
        def _(step):
            rows = block_rows(step)
            xhat, rstd = normalize(mixed_ref[rows, :])
            grad_n = grad_ref[rows, :]
            grad_mixed = cot_ref[rows, :].astype(F32) + norm_backward(grad_n, xhat, rstd, gain_ref[...])
            gm_ref[rows, :] = grad_mixed.astype(BF)
            gmt_ref[:, rows] = grad_mixed.astype(BF).T
            gvec_ref[0:1, :] += jnp.sum(grad_mixed, axis=0, keepdims=True)
            gvec_ref[1:2, :] += jnp.sum(grad_n * xhat, axis=0, keepdims=True)
            gvec_ref[2:3, :] += jnp.sum(grad_n, axis=0, keepdims=True)
            out_ref[rows, :] = (mixed_ref[rows, :] + total_ref[rows, :] + down_bias_ref[...]).astype(BF)


def mlp(splits, ids, x, at_one, at_two, a_one, a_two, w_up, w_down, sources, plan, smalls, vecs, cot):
    seq, width = x.shape
    n_t, part = at_one.shape[0] + at_two.shape[0], at_one.shape[1]
    ff = w_up.shape[1]
    n_split, blocks = splits
    cut = (2, blocks, n_t, width // (n_split * blocks), ff)
    cut_spec = pl.BlockSpec((2, blocks, 1) + cut[3:], lambda t: (0, 0, t, 0, 0))
    gbup = (n_t, 1, ff)
    return call(
        functools.partial(mlp_kernel, n_t, n_split, plan),
        "mlp",
        [((seq, width), BF), ((seq, width), BF), ((width, seq), BF), ((8, width), F32), (gbup, F32)]
        + [(cut, BF)] * n_split,
        [SMEM, fixed(x.shape), fixed(at_one.shape), fixed(at_two.shape),
         *[pl.BlockSpec((a.shape[0], part, width), lambda t: (0, 3, 0), pipeline_mode=pl.Buffered(1)) for a in (a_one, a_two)],
         nth(smalls.shape)] + [fixed((1, width))] * 4 + [HBM] * (2 + len(sources)) + [fixed(cot.shape)],
        (ids, x, at_one, at_two, a_one, a_two, smalls) + tuple(vecs) + (w_up, w_down) + tuple(sources) + (cot,),
        out_specs=(fixed((seq, width)), fixed((seq, width)), fixed((width, seq)), fixed((8, width)), nth(gbup))
        + (cut_spec,) * n_split,
        grid=(n_t,),
        scratch=[
            pltpu.VMEM((seq, width), F32),
            pltpu.VMEM((seq, width), BF),
            pltpu.VMEM((width, seq), BF),
            pltpu.VMEM((width, seq), BF),
            pltpu.VMEM((seq, width), F32),
            pltpu.VMEM((seq, width), F32),
            pltpu.VMEM((seq, ff), BF),
            pltpu.VMEM((seq, ff), BF),
            pltpu.VMEM((width, ff), BF),
            pltpu.VMEM((2, width, ff), BF),
            pltpu.VMEM((2, ff, width), BF),
            pltpu.SemaphoreType.DMA((2, max(2, piece_count(sources)))),
        ],
    )


def input_back_kernel(x_ref, gm_ref, gain_ref, a_one_ref, a_two_ref, one_ref, two_ref, out_ref, gvec_ref):

    @pl.when(pl.program_id(0) == 0)
    def _():
        gvec_ref[...] = jnp.zeros_like(gvec_ref)

    gp = jnp.concatenate([ref[t] for ref in (one_ref, two_ref) for t in range(ref.shape[0])]).T
    weights = jnp.concatenate([ref[t] for ref in (a_one_ref, a_two_ref) for t in range(ref.shape[0])])
    grad_n = dot(gp, weights, 1, 0)
    xhat, rstd = normalize(x_ref[...].astype(F32))
    out_ref[...] = (gm_ref[...].astype(F32) + norm_backward(grad_n, xhat, rstd, gain_ref[...])).astype(BF)
    gvec_ref[0:1, :] += jnp.sum(grad_n * xhat, axis=0, keepdims=True)
    gvec_ref[1:2, :] += jnp.sum(grad_n, axis=0, keepdims=True)


def input_back(x, gm, gain, a_one, a_two, one, two):
    seq, width = x.shape
    part3 = one.shape[1]
    by_rows = pl.BlockSpec((BLOCK, width), lambda i: (i, 0))

    def by_columns(gpt):
        return pl.BlockSpec(gpt.shape[:2] + (BLOCK,), lambda i: (0, 0, i))

    return call(
        input_back_kernel,
        "input_back",
        [((seq, width), BF), ((8, width), F32)],
        [by_rows, by_rows, fixed(gain.shape), fixed((one.shape[0], part3, width)), fixed((two.shape[0], part3, width)),
         by_columns(one), by_columns(two)],
        (x, gm, gain, a_one, a_two, one, two),
        out_specs=(by_rows, fixed((8, width))),
        grid=(seq // BLOCK,),
        flops=LONG,
    )


def settle_kernel(value_ref, out_ref):
    out_ref[...] = value_ref[...]


def settle(value):
    spec = pl.BlockSpec((1,) + value.shape[1:], lambda i: (i, 0, 0))
    return call(
        settle_kernel, "settle", [(value.shape, value.dtype)], [spec], (value,), out_specs=(spec,), grid=value.shape[:1]
    )[0]


def trade(value):
    return lax.all_to_all(value, "tensor", 0, 0, tiled=True)


def turn(value, by):
    return jnp.roll(value, -by, axis=0)


def swap(value, n_dp, mask):
    return lax.ppermute(value, "dp", [(i, i ^ mask) for i in range(n_dp)])


def after(value, *others):
    return lax.optimization_barrier((value,) + others)[0]


def gather_others(value, tensor, n_t):
    if n_t != 4:
        gathered = trade(jnp.broadcast_to(value[None], (n_t,) + value.shape))
        return turn(gathered, tensor + 1)[: n_t - 1], gathered

    def line(item, pairs):
        return lax.ppermute(item, "tensor", pairs)

    two = line(value, [(0, 2), (1, 3), (2, 0), (3, 1)])
    up = line(value, [(0, 1), (1, 2), (2, 3)])
    down = line(value, [(1, 0), (2, 1), (3, 2)])
    far = line(two, [(2, 3), (1, 0)])
    return jnp.stack([jnp.where(tensor == 3, far, down), two, jnp.where(tensor == 0, far, up)]), (up, down, far)


def chip_pieces(pieces, n_dp):
    if n_dp != 8:
        return [(lax.all_gather(pieces, "dp", axis=2, tiled=True), 0, tuple(range(pieces.shape[0])))]
    arrays = tuple(range(pieces.shape[0]))
    if len(arrays) == 1:
        return [(pieces, 0, arrays)] + [(swap(pieces, n_dp, mask), m + 1, arrays) for m, mask in enumerate(KEEP[1:])]
    by_x, by_y = swap(pieces, n_dp, KEEP[1]), swap(pieces, n_dp, KEEP[3])
    return [(pieces, 0, arrays), (by_x, 1, arrays), (by_y, 3, arrays)]


def chip_forward(mine, n_dp, *others):
    if n_dp != 8:
        return mine
    pieces, by_x, by_y = mine
    from_x, from_y = lax.optimization_barrier((by_x[0], by_y[0]) + others)[:2]
    first_far = swap(from_y[0:1], n_dp, KEEP[1])
    second_far = swap(from_x[1:2], n_dp, KEEP[3])
    return [pieces, (from_x,) + by_x[1:], (from_y,) + by_y[1:], (first_far, 2, (0,)), (second_far, 2, (1,))]


def pair_pieces(mine, n_dp):
    if n_dp != 8:
        return [value[None] for value, _, _ in mine], tuple((place, arrays) for _, place, arrays in mine)
    both = mine + [(swap(value, n_dp, PAIR), place + len(KEEP), arrays) for value, place, arrays in mine]
    return [value[None] for value, _, _ in both], tuple((place, arrays) for _, place, arrays in both)


def pair_swap(parts, n_dp):
    return [swap(parts[1], n_dp, PAIR)] if n_dp == 8 else []


BY_X = (slice(1, 3), 2, 3, 4, 0)
BY_Y = (slice(2, 4), 4, 1, 2, 1)


def chip_send(parts, got, n_dp, way, select):
    if n_dp != 8:
        whole = parts[0][select, 0]
        return lax.psum_scatter(whole, "dp", scatter_dimension=whole.ndim - 2, tiled=True)
    places, near = way[:2]
    value = parts[0][select, places].astype(F32) + got[0][select, places].astype(F32)
    return swap(value.astype(BF), n_dp, near)


def pass_kernel(*refs):
    count = len(refs) // 8
    for i in range(count):
        keep, got, sent, keep_far, got_far, sent_far = (ref[...].astype(F32) for ref in refs[6 * i : 6 * i + 6])
        here_ref, there_ref = refs[6 * count + 2 * i : 6 * count + 2 * i + 2]
        here_ref[...] = (keep + got + sent).astype(BF)[0, 0]
        there_ref[...] = (keep_far + got_far + sent_far).astype(BF)[0, 0]


def chip_pass(parts, got, sents, n_dp, items):
    if n_dp != 8:
        return [[sent] for sent in sents]
    _, _, sets, rows, cols = parts[0].shape
    args, specs = [], []

    def take(value, select, place):
        args.append(value)
        specs.append(pl.BlockSpec((1, 1, 1, rows, cols), lambda t: (select, place, t, 0, 0)))

    for sent, (way, select) in zip(sents, items):
        _, _, far, _, first = way
        for place, back in ((0, first), (far, 1 - first)):
            take(parts[0], select, place)
            take(got[0], select, place)
            take(sent[None], 0, back)
    made = pl.pallas_call(
        pass_kernel,
        grid=(sets,),
        out_shape=(jax.ShapeDtypeStruct((sets, rows, cols), BF),) * (2 * len(items)),
        in_specs=specs,
        out_specs=(pl.BlockSpec((1, rows, cols), lambda t: (t, 0, 0)),) * (2 * len(items)),
        compiler_params=pltpu.CompilerParams(vmem_limit_bytes=60 * MIB),
        name="chip_pass",
        cost_estimate=pl.CostEstimate(flops=LONG, bytes_accessed=1, transcendentals=0),
    )(*args)
    return [[made[2 * i], swap(made[2 * i + 1], n_dp, way[3])] for i, (way, _) in enumerate(items)]


def pair_kernel(*refs):
    sources, outs = refs[: -len(KEEP)], refs[-len(KEEP) :]
    at = 0
    for keep, got in zip(sources[0::2], sources[1::2]):
        for m, out in enumerate(outs):
            for t in range(keep.shape[2]):
                out[at + t] = (keep[0, m, t].astype(F32) + got[0, m, t].astype(F32)).astype(BF)
        at += keep.shape[2]


def as_rows(vectors, width):
    pad = [(0, 0)] * (vectors.ndim - 1) + [(0, 15), (0, width - vectors.shape[-1])]
    return jnp.pad(vectors[..., None, :].astype(BF), pad)


def chip_direct(groups, n_dp):
    if n_dp != 8:
        whole = jnp.concatenate([parts[0][0, 0] for parts, _ in groups])
        return [lax.psum_scatter(whole, "dp", scatter_dimension=whole.ndim - 2, tiled=True)]
    args = [value for parts, got in groups for value in (parts[0], got[0])]
    shape = (sum(parts[0].shape[2] for parts, _ in groups),) + args[0].shape[3:]
    made = call(pair_kernel, "pair", [(shape, BF)] * len(KEEP), [VMEM] * len(args), tuple(args))
    return [made[0]] + [swap(made[m + 1], n_dp, mask) for m, mask in enumerate(KEEP[1:])]


def vectors_direct(vectors, dp, width, n_dp):
    if n_dp != 8:
        return [as_rows(lax.psum_scatter(vectors, "dp", tiled=False), width)]
    kept, sent = (
        jnp.stack([lax.dynamic_index_in_dim(vectors, dp ^ mask ^ core, 0, keepdims=False) for mask in KEEP])
        for core in (0, PAIR)
    )
    lines = as_rows(kept + swap(sent, n_dp, PAIR), width)
    return [lines[0]] + [swap(lines[m + 1], n_dp, mask) for m, mask in enumerate(KEEP[1:])]


def chip_sum(terms):
    total = terms[0].astype(F32)
    for item in terms[1:]:
        total += item.astype(F32)
    return total


def gather_kernel(n_a, z_ref, *refs):
    out_ref, refs = refs[-1], refs[:-1]
    n_t = out_ref.shape[0]
    half = (len(refs) - 2 * n_a) // 2
    ends = (0, n_a, 2 * n_a, 2 * n_a + half, len(refs))
    for k in range(n_t):
        to = lax.rem(z_ref[0] + k, n_t)
        at = 0
        for terms in (refs[i:j] for i, j in zip(ends, ends[1:])):
            total = terms[0][k].astype(F32)
            for term in terms[1:]:
                total += term[k].astype(F32)
            rows = total.shape[0]
            out_ref[to, at : at + rows, :] = total.astype(BF)
            at += rows


def gather_shards(tensor, a_terms, lines, up_terms, down_terms):
    groups = (a_terms, lines, up_terms, down_terms)
    n_t, rows_a, width = a_terms[0].shape
    rows = sum(terms[0].shape[1] for terms in groups)
    if rows_a % 16 > 0:
        return turn(jnp.concatenate([chip_sum(terms).astype(BF) for terms in groups], axis=1), -tensor)
    args = tuple(term for terms in groups for term in terms)
    return call(
        functools.partial(gather_kernel, len(a_terms)),
        "gather_shards",
        [((n_t, rows, width), BF)],
        [SMEM] + [VMEM] * len(args),
        (tensor[None].astype(jnp.int32),) + args,
    )[0]


def in_parts(value):
    high = value.astype(BF)
    rest = value - high.astype(F32)
    middle = rest.astype(BF)
    return [high, middle, (rest - middle.astype(F32)).astype(BF)]


def pack_kernel(rows, dp_ref, qkv_ref, out_ref, up_ref, down_ref, bqv_ref, bup_ref, pieces_ref, sems):
    dp = dp_ref[0]
    split = qkv_ref.shape[0] // rows

    def start(src, place, at, sem):
        begin = pl.multiple_of(place * rows, rows)
        copy = pltpu.make_async_copy(src.at[pl.ds(begin, rows), :], pieces_ref.at[pl.ds(at * rows, rows), :], sems.at[sem])
        copy.start()
        return copy

    up = start(up_ref, dp, 1, 0)
    down = start(down_ref, dp, 2, 1)

    @pl.when(dp < split)
    def _():
        start(qkv_ref, dp, 0, 2).wait()

    @pl.when(dp >= split)
    def _():
        start(out_ref, dp - split, 0, 2).wait()

    pad = jnp.zeros((2, bup_ref.shape[1] - bqv_ref.shape[1]), F32)
    value = jnp.concatenate([jnp.concatenate([bqv_ref[...], pad], axis=1), bup_ref[...], jnp.zeros((13, bup_ref.shape[1]), F32)])
    high = value.astype(BF).astype(F32)
    middle = (value - high).astype(BF).astype(F32)
    low = value - high - middle
    lines = jnp.concatenate([high[0:3], middle[0:3], low[0:3], value[9:16]])
    pieces_ref[3 * rows :, :] = lines.astype(BF)
    up.wait()
    down.wait()


def pack(dp, w_qkv, w_out, w_up, w_down, b_qv, b_up, rows):
    width = w_up.shape[1]
    return call(
        functools.partial(pack_kernel, rows),
        "pack",
        [((3 * rows + 16, width), BF)],
        [SMEM] + [HBM] * 4 + [VMEM] * 2,
        (dp[None].astype(jnp.int32), w_qkv, w_out, w_up, w_down, b_qv, b_up[None]),
        scratch=[pltpu.SemaphoreType.DMA((3,))],
    )[0]


def small_vectors(b_qv, b_up):
    value = jnp.concatenate([jnp.pad(b_qv, ((0, 0), (0, b_up.shape[0] - b_qv.shape[1]))), b_up[None]])
    return jnp.concatenate(in_parts(value) + [jnp.zeros((7,) + b_up.shape, BF)])


def local(n_dp, n_t, inputs, doc_ids, ln1_gain, ln1_bias, w_qkv, b_qv, w_out, out_bias, ln2_gain, ln2_bias,
          w_up, b_up, w_down, down_bias, cotangent):
    width = inputs.shape[2]
    part, ff = w_out.shape[0], w_up.shape[1]
    dp = lax.axis_index("dp")
    tensor = lax.axis_index("tensor")
    own_rows = inputs.shape[0] // n_t
    rows = width // n_dp
    each_row = range(own_rows)
    splits = (2, 4) if n_dp == 8 else (1, 1)
    order = jnp.array(KEEP + tuple(m ^ PAIR for m in KEEP), jnp.int32)
    ids = order ^ dp if n_dp == 8 else jnp.zeros_like(order)
    half = n_t // 2
    groups = (tuple(range(half)), tuple(range(half, n_t)))

    def own_piece(whole):
        return lax.dynamic_slice_in_dim(whole, dp * rows, rows, 0)

    def split_row(values):
        values = values.reshape((n_t, own_rows) + values.shape[1:])
        return [values[:, r].reshape(-1, width) for r in each_row]

    def join_row(values):
        blocks = jnp.stack([v.reshape(n_t, -1, width) for v in values], axis=1)
        return blocks.reshape((n_t * own_rows,) + blocks.shape[2:])

    own_a = jnp.concatenate([w_qkv.transpose(1, 2, 0).reshape(3 * part, width), w_out])
    w_rows = w_qkv.transpose(1, 2, 0).reshape(3 * part, width)
    if n_dp == 8 and ff == width and 3 * part % rows == 0:
        pieces = pack(dp, w_rows, w_out, w_up, w_down, b_qv, b_up, rows)
    else:
        pieces = jnp.concatenate([own_piece(own_a), own_piece(w_up), own_piece(w_down), small_vectors(b_qv, b_up)])
    gathered, moved = gather_others(pieces, tensor, n_t)
    smalls = jnp.concatenate([pieces[None, 3 * rows :], gathered[:, 3 * rows :]]).astype(F32)
    smalls = smalls[:, 0:3] + smalls[:, 3:6] + smalls[:, 6:9]
    stack_a = gathered[None, :, :rows]
    stack_m = jnp.stack([gathered[:, rows : 2 * rows], gathered[:, 2 * rows : 3 * rows]])
    mine_a = chip_pieces(stack_a, n_dp)
    x_rows = trade(after(inputs, *moved))
    mine_m = chip_pieces(after(stack_m, mine_a[-1][0] if n_dp != 8 else (mine_a[1][0], mine_a[3][0])), n_dp)
    sources_a, plan_a = pair_pieces(mine_a, n_dp)
    values_m = [m[0] for m in mine_m]
    vecs = [v[None] for v in (out_bias, ln2_gain, ln2_bias, down_bias)]
    gain, bias = ln1_gain[None], ln1_bias[None]
    docs = lax.dynamic_slice_in_dim(doc_ids, tensor * own_rows, own_rows, 0)
    docs = [docs[r : r + 1] for r in each_row]
    sources_a, x_rows, own_a, vecs, gain, bias, docs, ids, smalls = lax.optimization_barrier(
        (sources_a, x_rows, own_a, vecs, gain, bias, docs, ids, smalls)
    )
    values_m, _, cotangent = lax.optimization_barrier((values_m, x_rows, cotangent))
    mine_m = [(value,) + m[1:] for value, m in zip(values_m, mine_m)]
    x_rows = split_row(x_rows)
    cot_rows = split_row(trade(cotangent))

    def total_of(*items):
        if len(items) == 1:
            return items[0]
        return sum(item.astype(F32) for item in items).astype(items[0].dtype)

    def together(results):
        return [jax.tree.map(total_of, *items) for items in zip(*results)]

    n1ts = [first(gain, bias, x) for x in x_rows]
    seen_one = [attend(groups[0], ids, n1ts[r], own_a, sources_a, plan_a, smalls, docs[r]) for r in each_row]
    mine_m = chip_forward(mine_m, n_dp, n1ts)
    n1ts, values_m = lax.optimization_barrier((n1ts, [m[0] for m in mine_m], seen_one))[:2]
    mine_m = [(value,) + m[1:] for value, m in zip(values_m, mine_m)]
    sources_m, plan_m = pair_pieces(mine_m, n_dp)
    seen_two = [attend(groups[1], ids, n1ts[r], own_a, sources_a, plan_a, smalls, docs[r]) for r in each_row]
    sources_m, cot_rows = lax.optimization_barrier((sources_m, cot_rows, seen_two))[:2]
    made = [
        mlp(splits, ids, x_rows[r], seen_one[r][1], seen_two[r][1], seen_one[r][3], seen_two[r][3], w_up, w_down,
            sources_m, plan_m, smalls, vecs, cot_rows[r])
        for r in each_row
    ]
    gvec, gbup, *dms = together([m[3:] for m in made])
    got_m = pair_swap(dms, n_dp)
    block_out = trade(join_row([m[0] for m in made]))

    def back(gmts, seen):
        items = [attend_back(splits, ids, gmts[r], n1ts[r], *seen[r], docs[r]) for r in each_row]
        return [i[0] for i in items], together([i[1:] for i in items])

    ways_m = ((BY_X, 0), (BY_Y, 1))
    gmts = [m[2] for m in made]
    gpt_two, (gb_two, *da_two) = back(gmts, seen_two)
    got_m, keep_m = lax.optimization_barrier((got_m, dms[0], gpt_two))[:2]
    dms = [keep_m]
    sent_m = [chip_send(dms, got_m, n_dp, *way) for way in ways_m]
    got_two = pair_swap(da_two, n_dp)
    gmts = lax.optimization_barrier((gmts, gpt_two))[0]
    gpt_one, (gb_one, *da_one) = back(gmts, seen_one)
    got_one = pair_swap(da_one, n_dp)
    block_out, got_two, sent_m = lax.optimization_barrier((block_out, got_two, sent_m, gpt_one))[:3]
    moved_a = chip_direct(((da_one, got_one), (da_two, got_two)), n_dp)
    gms = lax.optimization_barrier(([m[1] for m in made], gpt_one, block_out, sent_m, moved_a[0]))[0]
    ends = [
        input_back(x_rows[r], gms[r], gain, seen_two[r][3], seen_one[r][3], gpt_two[r], gpt_one[r])
        for r in each_row
    ]
    (gin,) = together([e[1:] for e in ends])
    grad_inputs = trade(join_row([e[0] for e in ends]))
    gbs = jnp.concatenate([gb_one, gb_two])
    each = width // (n_dp * n_t)
    vectors = jnp.concatenate([gin[0:2], gvec[0:4]])
    vectors = vectors.reshape(6, n_dp, n_t, each).transpose(1, 2, 0, 3).reshape(n_dp, n_t, 6 * each)
    shard = jnp.concatenate(
        [
            gbs.reshape(n_t, 2, n_dp, part // n_dp).transpose(2, 0, 1, 3).reshape(n_dp, n_t, -1),
            gbup.reshape(n_t, n_dp, ff // n_dp).transpose(1, 0, 2),
        ],
        axis=2,
    )
    vectors = jnp.concatenate([jnp.roll(vectors, -tensor, axis=1), shard], axis=2)
    lines = vectors_direct(after(vectors, moved_a[1:2]), dp, width, n_dp)
    passed_m = chip_pass([after(keep_m, ends, moved_a)], got_m, sent_m, n_dp, ways_m)
    block_out = settle(after(block_out, ends))
    moved_a, passed_m, lines, grad_inputs = lax.optimization_barrier((moved_a, passed_m, lines, grad_inputs))

    shards = gather_shards(tensor, moved_a, lines, *passed_m)
    grad_inputs = settle(after(grad_inputs, shards))
    share = jnp.sum(trade(shards).astype(F32), axis=0)
    share_a, lines, share_up, share_down = jnp.split(share, (rows, rows + 16, 2 * rows + 16))
    mine = lines[0]
    vec_out = mine[0 : 6 * each].reshape(6, each)
    share_b_qv = mine[6 * each : 6 * each + 2 * (part // n_dp)].reshape(2, part // n_dp)
    share_b_up = mine[6 * each + 2 * (part // n_dp) : 6 * each + (2 * part + ff) // n_dp]
    share_w_qkv = share_a[:, 0 : 3 * part].reshape(rows, 3, part)
    share_w_out = share_a[:, 3 * part :].T
    return (
        block_out,
        grad_inputs,
        vec_out[0],
        vec_out[1],
        share_w_qkv,
        share_b_qv,
        share_w_out,
        vec_out[2],
        vec_out[3],
        vec_out[4],
        share_up,
        share_b_up,
        share_down.T,
        vec_out[5],
    )


def solution(mesh):
    return jax.shard_map(
        functools.partial(local, mesh.shape["dp"], mesh.shape["tensor"]),
        mesh=mesh,
        in_specs=(
            P("dp", "tensor", None),
            P("dp", None),
            P(),
            P(),
            P(None, None, "tensor"),
            P(None, "tensor"),
            P("tensor", None),
            P(),
            P(),
            P(),
            P(None, "tensor"),
            P("tensor"),
            P("tensor", None),
            P(),
            P("dp", "tensor", None),
        ),
        out_specs=(
            P("dp", "tensor", None),
            P("dp", "tensor", None),
            P(("dp", "tensor")),
            P(("dp", "tensor")),
            P("dp", None, "tensor"),
            P(None, ("tensor", "dp")),
            P("tensor", "dp"),
            P(("dp", "tensor")),
            P(("dp", "tensor")),
            P(("dp", "tensor")),
            P("dp", "tensor"),
            P(("tensor", "dp")),
            P("tensor", "dp"),
            P(("dp", "tensor")),
        ),
        check_vma=False,
    )
```

```python
import functools

import jax
import jax.numpy as jnp
from jax import lax
from jax.experimental import pallas as pl
from jax.experimental.pallas import tpu as pltpu
from jax.sharding import PartitionSpec as P

BF = jnp.bfloat16
F32 = jnp.float32
HEAD = 64
EPS = 1e-05
GELU_C = 0.7978845608028654
GELU_A = 0.044715
BLOCK = 256
MIB = 1024 * 1024
KEEP = (0, 2, 6, 4)
PAIR = 1
LONG = 5 * 10**10


def dot(lhs, rhs, lhs_dim, rhs_dim):
    return lax.dot_general(
        lhs, rhs, (((lhs_dim,), (rhs_dim,)), ((), ())), preferred_element_type=F32
    )


def normalize(value):
    mean = jnp.mean(value, axis=-1, keepdims=True)
    centred = value - mean
    variance = jnp.mean(centred * centred, axis=-1, keepdims=True)
    rstd = lax.rsqrt(variance + EPS)
    return centred * rstd, rstd


def norm_backward(grad, xhat, rstd, gain):
    scaled = grad * gain
    mean_e = jnp.mean(scaled, axis=-1, keepdims=True)
    mean_ex = jnp.mean(scaled * xhat, axis=-1, keepdims=True)
    return rstd * (scaled - mean_e - xhat * mean_ex)


def column(line):
    return jnp.broadcast_to(line, (8, line.shape[1])).T[:, 0:1]


def block_rows(index, size=BLOCK):
    return pl.ds(pl.multiple_of(index * size, size), size)


VMEM = pl.BlockSpec(memory_space=pltpu.VMEM)
SMEM = pl.BlockSpec(memory_space=pltpu.SMEM)
HBM = pl.BlockSpec(memory_space=pl.ANY)


def call(kernel, name, outs, specs, args, out_specs=None, vmem=60, scratch=(), grid=(), flops=1):
    shapes = tuple(jax.ShapeDtypeStruct(*o) for o in outs)
    return pl.pallas_call(
        kernel,
        grid=grid,
        out_shape=shapes,
        in_specs=specs,
        out_specs=out_specs or (VMEM,) * len(outs),
        scratch_shapes=list(scratch),
        compiler_params=pltpu.CompilerParams(vmem_limit_bytes=vmem * MIB),
        name=name,
        cost_estimate=pl.CostEstimate(flops=flops, bytes_accessed=1, transcendentals=0),
    )(*args)


def fixed(shape):
    return pl.BlockSpec(shape, lambda *_: (0,) * len(shape), pipeline_mode=pl.Buffered(1))


def nth(shape, base=0):
    return pl.BlockSpec((1,) + tuple(shape[1:]), lambda t: (lax.rem(t + base, shape[0]),) + (0,) * (len(shape) - 1))


def own_copies(owns, wholes, sems):
    return [
        pltpu.make_async_copy(own, whole.at[0], sems.at[0, i]) for i, (own, whole) in enumerate(zip(owns, wholes))
    ]


def piece_copies(ids_ref, sources, plan, wholes, sems, k, slot):
    copies = []
    for src, (place, arrays) in zip(sources, plan):
        rows = src.shape[3]
        for m in range(src.shape[0]):
            at = pl.multiple_of(ids_ref[place + m] * rows, rows)
            for u, array in enumerate(arrays):
                copies.append(
                    pltpu.make_async_copy(
                        src.at[m, u, k - 1], wholes[array].at[slot, pl.ds(at, rows), :], sems.at[slot, len(copies)]
                    )
                )
    return copies


def piece_count(sources):
    return sum(src.shape[0] * src.shape[1] for src in sources)


def fetch(base, count, step, ids_ref, owns, sources, plan, wholes, sems):
    slot = lax.rem(step, 2)
    begins_own = base == 0

    def start():
        @pl.when(step == 0)
        def _():
            for copy in own_copies(owns, wholes, sems) if begins_own else piece_copies(
                ids_ref, sources, plan, wholes, sems, base, 0
            ):
                copy.start()

        @pl.when(step < count - 1)
        def _():
            for copy in piece_copies(ids_ref, sources, plan, wholes, sems, base + step + 1, lax.rem(step + 1, 2)):
                copy.start()

    def wait():
        if begins_own:
            @pl.when(step == 0)
            def _():
                for copy in own_copies(owns, wholes, sems):
                    copy.wait()

        @pl.when(step > 0 if begins_own else step >= 0)
        def _():
            for copy in piece_copies(ids_ref, sources, plan, wholes, sems, base + step, slot):
                copy.wait()

    return start, wait


def first_kernel(gain_ref, bias_ref, x_ref, n1t_ref):
    xhat, _ = normalize(x_ref[...].astype(F32))
    n1t_ref[...] = (xhat * gain_ref[...] + bias_ref[...]).astype(BF).T


def first(gain, bias, x):
    seq, width = x.shape
    return call(
        first_kernel,
        "first",
        [((width, seq), BF)],
        [fixed(gain.shape), fixed(bias.shape), pl.BlockSpec((BLOCK, width), lambda i: (i, 0))],
        (gain, bias, x),
        out_specs=(pl.BlockSpec((width, BLOCK), lambda i: (0, i)),),
        grid=(seq // BLOCK,),
    )[0]


def mask_bias(docs_ref, mask_ref):
    seq = mask_ref.shape[0]
    docs = docs_ref[...]
    docs_col = column(docs)
    for begin in range(0, seq, BLOCK):
        end = begin + BLOCK
        same = docs_col[0:end] == docs[:, begin:end]
        place_k = lax.broadcasted_iota(jnp.int32, (end, BLOCK), 0)
        place_q = begin + lax.broadcasted_iota(jnp.int32, (end, BLOCK), 1)
        allowed = same & (place_k <= place_q)
        mask_ref[0:end, begin:end] = jnp.where(allowed, 0.0, -1e30).astype(F32)


def attend_kernel(base, plan, ids_ref, n1t_ref, small_ref, docs_ref, own_ref, *refs):
    sources, (qkvt_ref, at_ref, lse_ref, a_ref, mask_ref, held_ref, sems) = refs[: len(plan)], refs[len(plan) :]
    step = pl.program_id(0)
    start, wait = fetch(base, pl.num_programs(0), step, ids_ref, [own_ref], sources, plan, [held_ref], sems)
    start()
    seq = n1t_ref.shape[1]
    part = at_ref.shape[1]

    @pl.when(pl.program_id(0) == 0)
    def _():
        mask_bias(docs_ref, mask_ref)

    wait()
    a_ref[0] = held_ref[lax.rem(step, 2)]
    proj = dot(a_ref[0, 0 : 3 * part, :], n1t_ref[...], 1, 0)
    qkvt_ref[0, 0:part, :] = (proj[0:part] + column(small_ref[0, 0:1, 0:part])).astype(BF)
    qkvt_ref[0, part : 2 * part, :] = proj[part : 2 * part].astype(BF)
    qkvt_ref[0, 2 * part :, :] = (proj[2 * part :] + column(small_ref[0, 1:2, 0:part])).astype(BF)
    heads = range(part // HEAD)

    def rows_of(which, h):
        return slice(which * part + h * HEAD, which * part + (h + 1) * HEAD)

    keys = [qkvt_ref[0, rows_of(1, h), :].T for h in heads]
    values = [jnp.concatenate([qkvt_ref[0, rows_of(2, h), :], jnp.ones((16, seq), BF)]) for h in heads]

    def scores_of(begin):
        end = begin + BLOCK
        mask = mask_ref[0:end, begin:end]
        return [dot(keys[h][0:end], qkvt_ref[0, rows_of(0, h), begin:end] * BF(0.125), 1, 0) + mask for h in heads]

    scores = scores_of(0)
    for begin in range(0, seq, BLOCK):
        end = begin + BLOCK
        now = scores
        top = [jnp.max(s, axis=0, keepdims=True) for s in now]
        if end < seq:
            scores = scores_of(end)
        expo = [jnp.exp(s - t).astype(BF) for s, t in zip(now, top)]
        out = [dot(values[h][:, 0:end], expo[h], 1, 0) for h in heads]
        for h in heads:
            total = out[h][HEAD : HEAD + 1]
            at_ref[0, h * HEAD : (h + 1) * HEAD, begin:end] = (out[h][0:HEAD] / total).astype(BF)
            lse_ref[0, h : h + 1, begin:end] = top[h] + jnp.log(total)


def attend(group, ids, n1t, own_a, sources, plan, smalls, docs):
    width, seq = n1t.shape
    base, count, part = group[0], len(group), own_a.shape[0] // 4
    shapes = [(count, 3 * part, seq), (count, part, seq), (count, 8, seq), (count,) + own_a.shape]
    return call(
        functools.partial(attend_kernel, base, plan),
        "attend",
        [(shapes[0], BF), (shapes[1], BF), (shapes[2], F32), (shapes[3], BF)],
        [SMEM, fixed(n1t.shape), nth(smalls.shape, base), fixed(docs.shape)] + [HBM] * (1 + len(sources)),
        (ids, n1t, smalls, docs, own_a) + tuple(sources),
        out_specs=tuple(nth(s) for s in shapes),
        grid=(count,),
        scratch=[
            pltpu.VMEM((seq, seq), F32),
            pltpu.VMEM((2,) + own_a.shape, BF),
            pltpu.SemaphoreType.DMA((2, piece_count(sources))),
        ],
    )


def split_rows(whole_ref, ids_ref, outs, array=0):
    for g, out in enumerate(outs):
        count, rows = out.shape[1], out.shape[3]
        for m in range(count):
            at = pl.multiple_of(ids_ref[g * count + m] * rows, rows)
            out[array, m, 0] = whole_ref[pl.ds(at, rows), :]


def attend_back_kernel(
    n_split, ids_ref, gmt_ref, n1t_ref, a_ref, qkvt_ref, at_ref, lse_ref, docs_ref, gpt_ref, gb_ref, *refs
):
    splits, (mask_ref, gat_ref, dkv_ref, da_ref) = refs[:n_split], refs[n_split:]
    seq = n1t_ref.shape[1]
    part = at_ref.shape[1]

    @pl.when(pl.program_id(0) == 0)
    def _():
        mask_bias(docs_ref, mask_ref)

    gat_ref[...] = dot(a_ref[0, 3 * part :, :], gmt_ref[...], 1, 0).astype(BF)
    heads = range(part // HEAD)

    def rows_of(which, h):
        return slice(which * part + h * HEAD, which * part + (h + 1) * HEAD)

    keys = [qkvt_ref[0, rows_of(1, h), :].T for h in heads]
    values = [qkvt_ref[0, rows_of(2, h), :].T for h in heads]
    items = [(begin, h) for begin in range(0, seq, BLOCK) for h in heads]

    def begin_item(begin, h):
        end = begin + BLOCK
        query = qkvt_ref[0, rows_of(0, h), begin:end] * BF(0.125)
        grad = gat_ref[rows_of(0, h), begin:end]
        scores = dot(keys[h][0:end], query, 1, 0) + mask_ref[0:end, begin:end]
        return query, grad, scores, dot(values[h][0:end], grad, 1, 0)

    ahead = begin_item(*items[0])
    for i, (begin, h) in enumerate(items):
        end = begin + BLOCK
        query, grad, scores, grad_probs = ahead
        if i + 1 < len(items):
            ahead = begin_item(*items[i + 1])
        delta = jnp.sum(
            grad.astype(F32) * at_ref[0, rows_of(0, h), begin:end].astype(F32), axis=0, keepdims=True
        )
        probs = jnp.exp(scores - lse_ref[0, h : h + 1, begin:end])
        grad_scores = (probs * (grad_probs - delta)).astype(BF)
        gpt_ref[0, rows_of(0, h), begin:end] = (
            0.125 * dot(qkvt_ref[0, rows_of(1, h), 0:end], grad_scores, 1, 0)
        ).astype(BF)
        for which, share in ((0, dot(query, grad_scores, 1, 1)), (1, dot(grad, probs.astype(BF), 1, 1))):
            if begin > 0:
                dkv_ref[h, which, :, 0:begin] += share[:, 0:begin]
            dkv_ref[h, which, :, begin:end] = share[:, begin:end]
    for h in heads:
        for which in range(2):
            gpt_ref[0, rows_of(1 + which, h), :] = dkv_ref[h, which].astype(BF)
    ones = jnp.ones((8, seq), BF)
    gb_ref[0, 0:1, :] = dot(ones, gpt_ref[0, 0:part, :], 1, 1)[0:1]
    gb_ref[0, 1:2, :] = dot(ones, gpt_ref[0, 2 * part : 3 * part, :], 1, 1)[0:1]
    da_ref[:, 0 : 3 * part] = dot(n1t_ref[...], gpt_ref[0], 1, 1).astype(BF)
    da_ref[:, 3 * part :] = dot(gmt_ref[...], at_ref[0], 1, 1).astype(BF)
    split_rows(da_ref, ids_ref, splits)


def attend_back(splits, ids, gmt, n1t, qkvt, at, lse, a_part, docs):
    width, seq = n1t.shape
    part = at.shape[1]
    n_split, blocks = splits
    count = at.shape[0]
    cut = (1, blocks, count, width // (n_split * blocks), 4 * part)
    cut_spec = pl.BlockSpec((1, blocks, 1) + cut[3:], lambda t: (0, 0, t, 0, 0))
    return call(
        functools.partial(attend_back_kernel, n_split),
        "attend_back",
        [((count, 3 * part, seq), BF), ((count, 2, part), F32)] + [(cut, BF)] * n_split,
        [SMEM, fixed(gmt.shape), fixed(n1t.shape), nth(a_part.shape), nth(qkvt.shape), nth(at.shape),
         nth(lse.shape), fixed(docs.shape)],
        (ids, gmt, n1t, a_part, qkvt, at, lse, docs),
        out_specs=(nth((count, 3 * part, seq)), nth((count, 2, part))) + (cut_spec,) * n_split,
        grid=(count,),
        scratch=[
            pltpu.VMEM((seq, seq), F32),
            pltpu.VMEM((part, seq), BF),
            pltpu.VMEM((part // HEAD, 2, HEAD, seq), F32),
            pltpu.VMEM((width, 4 * part), BF),
        ],
    )


def mlp_kernel(
    n_t, n_split, plan, ids_ref, x_ref, at_one_ref, at_two_ref, out_one_ref, out_two_ref, small_ref,
    out_bias_ref, gain_ref, bias_ref, down_bias_ref, own_up_ref, own_down_ref, *refs
):
    sources, refs = refs[: len(plan)], refs[len(plan) :]
    cot_ref, out_ref, *refs = refs
    gm_ref, gmt_ref, gvec_ref, gbup_ref = refs[:4]
    splits = refs[4 : 4 + n_split]
    (mixed_ref, n2_ref, n2t_ref, cott_ref, total_ref, grad_ref, act_ref, gpre_ref, dm_ref,
     up_all_ref, down_all_ref, sems) = refs[4 + n_split :]
    seq, width = x_ref.shape
    step_t = pl.program_id(0)
    blocks = seq // BLOCK
    slot = lax.rem(step_t, 2)
    wholes = [up_all_ref, down_all_ref]
    start, wait = fetch(0, n_t, step_t, ids_ref, [own_up_ref, own_down_ref], sources, plan, wholes, sems)
    up_ref, down_ref = up_all_ref.at[slot], down_all_ref.at[slot]
    start()

    @pl.when(step_t == 0)
    def _():
        gvec_ref[...] = jnp.zeros_like(gvec_ref)

        @pl.loop(0, blocks)
        def _(step):
            rows = block_rows(step)
            total = x_ref[rows, :].astype(F32) + out_bias_ref[...]
            for at_ref, w_out_ref in ((at_one_ref, out_one_ref), (at_two_ref, out_two_ref)):
                for t in range(at_ref.shape[0]):
                    total += dot(at_ref[t, :, rows].T, w_out_ref[t], 1, 0)
            mixed_ref[rows, :] = total
            xhat, _ = normalize(total)
            normed = (xhat * gain_ref[...] + bias_ref[...]).astype(BF)
            n2_ref[rows, :] = normed
            n2t_ref[:, rows] = normed.T
            held = cot_ref[rows, :]
            cott_ref[:, rows] = held.T
            gvec_ref[3:4, :] += jnp.sum(held.astype(F32), axis=0, keepdims=True)
            total_ref[rows, :] = jnp.zeros((BLOCK, width), F32)
            grad_ref[rows, :] = jnp.zeros((BLOCK, width), F32)

    wait()
    bias = small_ref[0, 2:3, :]

    def one(step, sums):
        rows = block_rows(step)
        pre = dot(n2_ref[rows, :], up_ref[...], 1, 0) + bias
        grad_act = dot(cot_ref[rows, :], down_ref[...], 1, 1)
        square = pre * pre
        curve = jnp.tanh(pre * (GELU_C + (GELU_C * GELU_A) * square))
        half = 0.5 + 0.5 * curve
        act = (pre * half).astype(BF)
        slope = half + (half - half * curve) * pre * (GELU_C + (3 * GELU_C * GELU_A) * square)
        grad_pre = (slope * grad_act).astype(BF)
        act_ref[rows, :] = act
        gpre_ref[rows, :] = grad_pre
        total_ref[rows, :] += dot(act, down_ref[...], 1, 0)
        grad_ref[rows, :] += dot(grad_pre, up_ref[...], 1, 1)
        return sums + jnp.sum(grad_pre.astype(F32), axis=0, keepdims=True)

    gbup_ref[0] = lax.fori_loop(0, blocks, one, jnp.zeros(bias.shape, F32), unroll=True)
    dm_ref[...] = dot(n2t_ref[...], gpre_ref[...], 1, 0).astype(BF)
    split_rows(dm_ref, ids_ref, splits, 0)
    dm_ref[...] = dot(cott_ref[...], act_ref[...], 1, 0).astype(BF)
    split_rows(dm_ref, ids_ref, splits, 1)

    @pl.when(step_t == n_t - 1)
    def _():
        @pl.loop(0, blocks)
        def _(step):
            rows = block_rows(step)
            xhat, rstd = normalize(mixed_ref[rows, :])
            grad_n = grad_ref[rows, :]
            grad_mixed = cot_ref[rows, :].astype(F32) + norm_backward(grad_n, xhat, rstd, gain_ref[...])
            gm_ref[rows, :] = grad_mixed.astype(BF)
            gmt_ref[:, rows] = grad_mixed.astype(BF).T
            gvec_ref[0:1, :] += jnp.sum(grad_mixed, axis=0, keepdims=True)
            gvec_ref[1:2, :] += jnp.sum(grad_n * xhat, axis=0, keepdims=True)
            gvec_ref[2:3, :] += jnp.sum(grad_n, axis=0, keepdims=True)
            out_ref[rows, :] = (mixed_ref[rows, :] + total_ref[rows, :] + down_bias_ref[...]).astype(BF)


def mlp(splits, ids, x, at_one, at_two, a_one, a_two, w_up, w_down, sources, plan, smalls, vecs, cot):
    seq, width = x.shape
    n_t, part = at_one.shape[0] + at_two.shape[0], at_one.shape[1]
    ff = w_up.shape[1]
    n_split, blocks = splits
    cut = (2, blocks, n_t, width // (n_split * blocks), ff)
    cut_spec = pl.BlockSpec((2, blocks, 1) + cut[3:], lambda t: (0, 0, t, 0, 0))
    gbup = (n_t, 1, ff)
    return call(
        functools.partial(mlp_kernel, n_t, n_split, plan),
        "mlp",
        [((seq, width), BF), ((seq, width), BF), ((width, seq), BF), ((8, width), F32), (gbup, F32)]
        + [(cut, BF)] * n_split,
        [SMEM, fixed(x.shape), fixed(at_one.shape), fixed(at_two.shape),
         *[pl.BlockSpec((a.shape[0], part, width), lambda t: (0, 3, 0), pipeline_mode=pl.Buffered(1)) for a in (a_one, a_two)],
         nth(smalls.shape)] + [fixed((1, width))] * 4 + [HBM] * (2 + len(sources)) + [fixed(cot.shape)],
        (ids, x, at_one, at_two, a_one, a_two, smalls) + tuple(vecs) + (w_up, w_down) + tuple(sources) + (cot,),
        out_specs=(fixed((seq, width)), fixed((seq, width)), fixed((width, seq)), fixed((8, width)), nth(gbup))
        + (cut_spec,) * n_split,
        grid=(n_t,),
        scratch=[
            pltpu.VMEM((seq, width), F32),
            pltpu.VMEM((seq, width), BF),
            pltpu.VMEM((width, seq), BF),
            pltpu.VMEM((width, seq), BF),
            pltpu.VMEM((seq, width), F32),
            pltpu.VMEM((seq, width), F32),
            pltpu.VMEM((seq, ff), BF),
            pltpu.VMEM((seq, ff), BF),
            pltpu.VMEM((width, ff), BF),
            pltpu.VMEM((2, width, ff), BF),
            pltpu.VMEM((2, ff, width), BF),
            pltpu.SemaphoreType.DMA((2, max(2, piece_count(sources)))),
        ],
    )


def input_back_kernel(x_ref, gm_ref, gain_ref, a_one_ref, a_two_ref, one_ref, two_ref, out_ref, gvec_ref):

    @pl.when(pl.program_id(0) == 0)
    def _():
        gvec_ref[...] = jnp.zeros_like(gvec_ref)

    gp = jnp.concatenate([ref[t] for ref in (one_ref, two_ref) for t in range(ref.shape[0])]).T
    weights = jnp.concatenate([ref[t] for ref in (a_one_ref, a_two_ref) for t in range(ref.shape[0])])
    grad_n = dot(gp, weights, 1, 0)
    xhat, rstd = normalize(x_ref[...].astype(F32))
    out_ref[...] = (gm_ref[...].astype(F32) + norm_backward(grad_n, xhat, rstd, gain_ref[...])).astype(BF)
    gvec_ref[0:1, :] += jnp.sum(grad_n * xhat, axis=0, keepdims=True)
    gvec_ref[1:2, :] += jnp.sum(grad_n, axis=0, keepdims=True)


def input_back(x, gm, gain, a_one, a_two, one, two):
    seq, width = x.shape
    part3 = one.shape[1]
    by_rows = pl.BlockSpec((BLOCK, width), lambda i: (i, 0))

    def by_columns(gpt):
        return pl.BlockSpec(gpt.shape[:2] + (BLOCK,), lambda i: (0, 0, i))

    return call(
        input_back_kernel,
        "input_back",
        [((seq, width), BF), ((8, width), F32)],
        [by_rows, by_rows, fixed(gain.shape), fixed((one.shape[0], part3, width)), fixed((two.shape[0], part3, width)),
         by_columns(one), by_columns(two)],
        (x, gm, gain, a_one, a_two, one, two),
        out_specs=(by_rows, fixed((8, width))),
        grid=(seq // BLOCK,),
        flops=LONG,
    )


def settle_kernel(value_ref, out_ref):
    out_ref[...] = value_ref[...]


def settle(value):
    spec = pl.BlockSpec((1,) + value.shape[1:], lambda i: (i, 0, 0))
    return call(
        settle_kernel, "settle", [(value.shape, value.dtype)], [spec], (value,), out_specs=(spec,), grid=value.shape[:1]
    )[0]


def trade(value):
    return lax.all_to_all(value, "tensor", 0, 0, tiled=True)


def turn(value, by):
    return jnp.roll(value, -by, axis=0)


def swap(value, n_dp, mask):
    return lax.ppermute(value, "dp", [(i, i ^ mask) for i in range(n_dp)])


def after(value, *others):
    return lax.optimization_barrier((value,) + others)[0]


def gather_others(value, tensor, n_t):
    if n_t != 4:
        gathered = trade(jnp.broadcast_to(value[None], (n_t,) + value.shape))
        return turn(gathered, tensor + 1)[: n_t - 1], gathered

    def line(item, pairs):
        return lax.ppermute(item, "tensor", pairs)

    two = line(value, [(0, 2), (1, 3), (2, 0), (3, 1)])
    up = line(value, [(0, 1), (1, 2), (2, 3)])
    down = line(value, [(1, 0), (2, 1), (3, 2)])
    far = line(two, [(2, 3), (1, 0)])
    return jnp.stack([jnp.where(tensor == 3, far, down), two, jnp.where(tensor == 0, far, up)]), (up, down, far)


def chip_pieces(pieces, n_dp):
    if n_dp != 8:
        return [(lax.all_gather(pieces, "dp", axis=2, tiled=True), 0, tuple(range(pieces.shape[0])))]
    arrays = tuple(range(pieces.shape[0]))
    if len(arrays) == 1:
        return [(pieces, 0, arrays)] + [(swap(pieces, n_dp, mask), m + 1, arrays) for m, mask in enumerate(KEEP[1:])]
    by_x, by_y = swap(pieces, n_dp, KEEP[1]), swap(pieces, n_dp, KEEP[3])
    return [(pieces, 0, arrays), (by_x, 1, arrays), (by_y, 3, arrays)]


def chip_forward(mine, n_dp, *others):
    if n_dp != 8:
        return mine
    pieces, by_x, by_y = mine
    from_x, from_y = lax.optimization_barrier((by_x[0], by_y[0]) + others)[:2]
    first_far = swap(from_y[0:1], n_dp, KEEP[1])
    second_far = swap(from_x[1:2], n_dp, KEEP[3])
    return [pieces, (from_x,) + by_x[1:], (from_y,) + by_y[1:], (first_far, 2, (0,)), (second_far, 2, (1,))]


def pair_pieces(mine, n_dp):
    if n_dp != 8:
        return [value[None] for value, _, _ in mine], tuple((place, arrays) for _, place, arrays in mine)
    both = mine + [(swap(value, n_dp, PAIR), place + len(KEEP), arrays) for value, place, arrays in mine]
    return [value[None] for value, _, _ in both], tuple((place, arrays) for _, place, arrays in both)


def pair_swap(parts, n_dp):
    return [swap(parts[1], n_dp, PAIR)] if n_dp == 8 else []


BY_X = (slice(1, 3), 2, 3, 4, 0)
BY_Y = (slice(2, 4), 4, 1, 2, 1)


def chip_send(parts, got, n_dp, way, select):
    if n_dp != 8:
        whole = parts[0][select, 0]
        return lax.psum_scatter(whole, "dp", scatter_dimension=whole.ndim - 2, tiled=True)
    places, near = way[:2]
    value = parts[0][select, places].astype(F32) + got[0][select, places].astype(F32)
    return swap(value.astype(BF), n_dp, near)


def pass_kernel(*refs):
    count = len(refs) // 8
    for i in range(count):
        keep, got, sent, keep_far, got_far, sent_far = (ref[...].astype(F32) for ref in refs[6 * i : 6 * i + 6])
        here_ref, there_ref = refs[6 * count + 2 * i : 6 * count + 2 * i + 2]
        here_ref[...] = (keep + got + sent).astype(BF)[0, 0]
        there_ref[...] = (keep_far + got_far + sent_far).astype(BF)[0, 0]


def chip_pass(parts, got, sents, n_dp, items):
    if n_dp != 8:
        return [[sent] for sent in sents]
    _, _, sets, rows, cols = parts[0].shape
    args, specs = [], []

    def take(value, select, place):
        args.append(value)
        specs.append(pl.BlockSpec((1, 1, 1, rows, cols), lambda t: (select, place, t, 0, 0)))

    for sent, (way, select) in zip(sents, items):
        _, _, far, _, first = way
        for place, back in ((0, first), (far, 1 - first)):
            take(parts[0], select, place)
            take(got[0], select, place)
            take(sent[None], 0, back)
    made = pl.pallas_call(
        pass_kernel,
        grid=(sets,),
        out_shape=(jax.ShapeDtypeStruct((sets, rows, cols), BF),) * (2 * len(items)),
        in_specs=specs,
        out_specs=(pl.BlockSpec((1, rows, cols), lambda t: (t, 0, 0)),) * (2 * len(items)),
        compiler_params=pltpu.CompilerParams(vmem_limit_bytes=60 * MIB),
        name="chip_pass",
        cost_estimate=pl.CostEstimate(flops=LONG, bytes_accessed=1, transcendentals=0),
    )(*args)
    return [[made[2 * i], swap(made[2 * i + 1], n_dp, way[3])] for i, (way, _) in enumerate(items)]


def pair_kernel(*refs):
    sources, outs = refs[: -len(KEEP)], refs[-len(KEEP) :]
    at = 0
    for keep, got in zip(sources[0::2], sources[1::2]):
        for m, out in enumerate(outs):
            for t in range(keep.shape[2]):
                out[at + t] = (keep[0, m, t].astype(F32) + got[0, m, t].astype(F32)).astype(BF)
        at += keep.shape[2]


def as_rows(vectors, width):
    pad = [(0, 0)] * (vectors.ndim - 1) + [(0, 15), (0, width - vectors.shape[-1])]
    return jnp.pad(vectors[..., None, :].astype(BF), pad)


def chip_direct(groups, n_dp):
    if n_dp != 8:
        whole = jnp.concatenate([parts[0][0, 0] for parts, _ in groups])
        return [lax.psum_scatter(whole, "dp", scatter_dimension=whole.ndim - 2, tiled=True)]
    args = [value for parts, got in groups for value in (parts[0], got[0])]
    shape = (sum(parts[0].shape[2] for parts, _ in groups),) + args[0].shape[3:]
    made = call(pair_kernel, "pair", [(shape, BF)] * len(KEEP), [VMEM] * len(args), tuple(args))
    return [made[0]] + [swap(made[m + 1], n_dp, mask) for m, mask in enumerate(KEEP[1:])]


def vectors_direct(vectors, dp, width, n_dp):
    if n_dp != 8:
        return [as_rows(lax.psum_scatter(vectors, "dp", tiled=False), width)]
    kept, sent = (
        jnp.stack([lax.dynamic_index_in_dim(vectors, dp ^ mask ^ core, 0, keepdims=False) for mask in KEEP])
        for core in (0, PAIR)
    )
    lines = as_rows(kept + swap(sent, n_dp, PAIR), width)
    return [lines[0]] + [swap(lines[m + 1], n_dp, mask) for m, mask in enumerate(KEEP[1:])]


def chip_sum(terms):
    total = terms[0].astype(F32)
    for item in terms[1:]:
        total += item.astype(F32)
    return total


def gather_kernel(n_a, z_ref, *refs):
    out_ref, refs = refs[-1], refs[:-1]
    n_t = out_ref.shape[0]
    half = (len(refs) - 2 * n_a) // 2
    ends = (0, n_a, 2 * n_a, 2 * n_a + half, len(refs))
    for k in range(n_t):
        to = lax.rem(z_ref[0] + k, n_t)
        at = 0
        for terms in (refs[i:j] for i, j in zip(ends, ends[1:])):
            total = terms[0][k].astype(F32)
            for term in terms[1:]:
                total += term[k].astype(F32)
            rows = total.shape[0]
            out_ref[to, at : at + rows, :] = total.astype(BF)
            at += rows


def gather_shards(tensor, a_terms, lines, up_terms, down_terms):
    groups = (a_terms, lines, up_terms, down_terms)
    n_t, rows_a, width = a_terms[0].shape
    rows = sum(terms[0].shape[1] for terms in groups)
    if rows_a % 16 > 0:
        return turn(jnp.concatenate([chip_sum(terms).astype(BF) for terms in groups], axis=1), -tensor)
    args = tuple(term for terms in groups for term in terms)
    return call(
        functools.partial(gather_kernel, len(a_terms)),
        "gather_shards",
        [((n_t, rows, width), BF)],
        [SMEM] + [VMEM] * len(args),
        (tensor[None].astype(jnp.int32),) + args,
    )[0]


def in_parts(value):
    high = value.astype(BF)
    rest = value - high.astype(F32)
    middle = rest.astype(BF)
    return [high, middle, (rest - middle.astype(F32)).astype(BF)]


def pack_kernel(rows, dp_ref, qkv_ref, out_ref, up_ref, down_ref, bqv_ref, bup_ref, pieces_ref, sems):
    dp = dp_ref[0]
    split = qkv_ref.shape[0] // rows

    def start(src, place, at, sem):
        begin = pl.multiple_of(place * rows, rows)
        copy = pltpu.make_async_copy(src.at[pl.ds(begin, rows), :], pieces_ref.at[pl.ds(at * rows, rows), :], sems.at[sem])
        copy.start()
        return copy

    up = start(up_ref, dp, 1, 0)
    down = start(down_ref, dp, 2, 1)

    @pl.when(dp < split)
    def _():
        start(qkv_ref, dp, 0, 2).wait()

    @pl.when(dp >= split)
    def _():
        start(out_ref, dp - split, 0, 2).wait()

    width = pieces_ref.shape[1]
    bias = jnp.concatenate([bup_ref[i : i + 1, :] for i in range(bup_ref.shape[0])], axis=1)
    pad = jnp.zeros((2, width - bqv_ref.shape[1]), F32)
    value = jnp.concatenate([jnp.concatenate([bqv_ref[...], pad], axis=1), bias, jnp.zeros((13, width), F32)])
    high = value.astype(BF).astype(F32)
    middle = (value - high).astype(BF).astype(F32)
    low = value - high - middle
    lines = jnp.concatenate([high[0:3], middle[0:3], low[0:3], value[9:16]])
    pieces_ref[3 * rows :, :] = lines.astype(BF)
    up.wait()
    down.wait()


def pack(dp, w_qkv, w_out, w_up, w_down, b_qv, b_up, rows):
    width = w_up.shape[1]
    return call(
        functools.partial(pack_kernel, rows),
        "pack",
        [((3 * rows + 16, width), BF)],
        [SMEM] + [HBM] * 4 + [VMEM] * 2,
        (dp[None].astype(jnp.int32), w_qkv, w_out, w_up, w_down, b_qv, b_up.reshape(-1, 128)),
        scratch=[pltpu.SemaphoreType.DMA((3,))],
    )[0]


def small_vectors(b_qv, b_up):
    value = jnp.concatenate([jnp.pad(b_qv, ((0, 0), (0, b_up.shape[0] - b_qv.shape[1]))), b_up[None]])
    return jnp.concatenate(in_parts(value) + [jnp.zeros((7,) + b_up.shape, BF)])


def local(n_dp, n_t, inputs, doc_ids, ln1_gain, ln1_bias, w_qkv, b_qv, w_out, out_bias, ln2_gain, ln2_bias,
          w_up, b_up, w_down, down_bias, cotangent):
    width = inputs.shape[2]
    part, ff = w_out.shape[0], w_up.shape[1]
    dp = lax.axis_index("dp")
    tensor = lax.axis_index("tensor")
    own_rows = inputs.shape[0] // n_t
    rows = width // n_dp
    each_row = range(own_rows)
    splits = (2, 4) if n_dp == 8 else (1, 1)
    order = jnp.array(KEEP + tuple(m ^ PAIR for m in KEEP), jnp.int32)
    ids = order ^ dp if n_dp == 8 else jnp.zeros_like(order)
    half = n_t // 2
    groups = (tuple(range(half)), tuple(range(half, n_t)))

    def own_piece(whole):
        return lax.dynamic_slice_in_dim(whole, dp * rows, rows, 0)

    def split_row(values):
        values = values.reshape((n_t, own_rows) + values.shape[1:])
        return [values[:, r].reshape(-1, width) for r in each_row]

    def join_row(values):
        blocks = jnp.stack([v.reshape(n_t, -1, width) for v in values], axis=1)
        return blocks.reshape((n_t * own_rows,) + blocks.shape[2:])

    own_a = jnp.concatenate([w_qkv.transpose(1, 2, 0).reshape(3 * part, width), w_out])
    w_rows = w_qkv.transpose(1, 2, 0).reshape(3 * part, width)
    if n_dp == 8 and ff == width and ff % 128 == 0 and 3 * part % rows == 0:
        pieces = pack(dp, w_rows, w_out, w_up, w_down, b_qv, b_up, rows)
    else:
        pieces = jnp.concatenate([own_piece(own_a), own_piece(w_up), own_piece(w_down), small_vectors(b_qv, b_up)])
    gathered, moved = gather_others(pieces, tensor, n_t)
    smalls = jnp.concatenate([pieces[None, 3 * rows :], gathered[:, 3 * rows :]]).astype(F32)
    smalls = smalls[:, 0:3] + smalls[:, 3:6] + smalls[:, 6:9]
    stack_a = gathered[None, :, :rows]
    stack_m = jnp.stack([gathered[:, rows : 2 * rows], gathered[:, 2 * rows : 3 * rows]])
    mine_a = chip_pieces(stack_a, n_dp)
    x_rows = trade(after(inputs, *moved))
    mine_m = chip_pieces(after(stack_m, mine_a[-1][0] if n_dp != 8 else (mine_a[1][0], mine_a[3][0])), n_dp)
    sources_a, plan_a = pair_pieces(mine_a, n_dp)
    values_m = [m[0] for m in mine_m]
    vecs = [v[None] for v in (out_bias, ln2_gain, ln2_bias, down_bias)]
    gain, bias = ln1_gain[None], ln1_bias[None]
    docs = lax.dynamic_slice_in_dim(doc_ids, tensor * own_rows, own_rows, 0)
    docs = [docs[r : r + 1] for r in each_row]
    sources_a, x_rows, own_a, vecs, gain, bias, docs, ids, smalls = lax.optimization_barrier(
        (sources_a, x_rows, own_a, vecs, gain, bias, docs, ids, smalls)
    )
    values_m, _, cotangent = lax.optimization_barrier((values_m, x_rows, cotangent))
    mine_m = [(value,) + m[1:] for value, m in zip(values_m, mine_m)]
    x_rows = split_row(x_rows)
    cot_rows = split_row(trade(cotangent))

    def total_of(*items):
        if len(items) == 1:
            return items[0]
        return sum(item.astype(F32) for item in items).astype(items[0].dtype)

    def together(results):
        return [jax.tree.map(total_of, *items) for items in zip(*results)]

    n1ts = [first(gain, bias, x) for x in x_rows]
    seen_one = [attend(groups[0], ids, n1ts[r], own_a, sources_a, plan_a, smalls, docs[r]) for r in each_row]
    mine_m = chip_forward(mine_m, n_dp, n1ts)
    n1ts, values_m = lax.optimization_barrier((n1ts, [m[0] for m in mine_m], seen_one))[:2]
    mine_m = [(value,) + m[1:] for value, m in zip(values_m, mine_m)]
    sources_m, plan_m = pair_pieces(mine_m, n_dp)
    seen_two = [attend(groups[1], ids, n1ts[r], own_a, sources_a, plan_a, smalls, docs[r]) for r in each_row]
    sources_m, cot_rows = lax.optimization_barrier((sources_m, cot_rows, seen_two))[:2]
    made = [
        mlp(splits, ids, x_rows[r], seen_one[r][1], seen_two[r][1], seen_one[r][3], seen_two[r][3], w_up, w_down,
            sources_m, plan_m, smalls, vecs, cot_rows[r])
        for r in each_row
    ]
    gvec, gbup, *dms = together([m[3:] for m in made])
    got_m = pair_swap(dms, n_dp)
    block_out = trade(join_row([m[0] for m in made]))

    def back(gmts, seen):
        items = [attend_back(splits, ids, gmts[r], n1ts[r], *seen[r], docs[r]) for r in each_row]
        return [i[0] for i in items], together([i[1:] for i in items])

    ways_m = ((BY_X, 0), (BY_Y, 1))
    gmts = [m[2] for m in made]
    gpt_two, (gb_two, *da_two) = back(gmts, seen_two)
    got_m, keep_m = lax.optimization_barrier((got_m, dms[0], gpt_two))[:2]
    dms = [keep_m]
    sent_m = [chip_send(dms, got_m, n_dp, *way) for way in ways_m]
    got_two = pair_swap(da_two, n_dp)
    gmts = lax.optimization_barrier((gmts, gpt_two))[0]
    gpt_one, (gb_one, *da_one) = back(gmts, seen_one)
    got_one = pair_swap(da_one, n_dp)
    block_out, got_two, sent_m = lax.optimization_barrier((block_out, got_two, sent_m, gpt_one))[:3]
    moved_a = chip_direct(((da_one, got_one), (da_two, got_two)), n_dp)
    gms = lax.optimization_barrier(([m[1] for m in made], gpt_one, block_out, sent_m, moved_a[0]))[0]
    ends = [
        input_back(x_rows[r], gms[r], gain, seen_two[r][3], seen_one[r][3], gpt_two[r], gpt_one[r])
        for r in each_row
    ]
    (gin,) = together([e[1:] for e in ends])
    grad_inputs = trade(join_row([e[0] for e in ends]))
    gbs = jnp.concatenate([gb_one, gb_two])
    each = width // (n_dp * n_t)
    vectors = jnp.concatenate([gin[0:2], gvec[0:4]])
    vectors = vectors.reshape(6, n_dp, n_t, each).transpose(1, 2, 0, 3).reshape(n_dp, n_t, 6 * each)
    shard = jnp.concatenate(
        [
            gbs.reshape(n_t, 2, n_dp, part // n_dp).transpose(2, 0, 1, 3).reshape(n_dp, n_t, -1),
            gbup.reshape(n_t, n_dp, ff // n_dp).transpose(1, 0, 2),
        ],
        axis=2,
    )
    vectors = jnp.concatenate([jnp.roll(vectors, -tensor, axis=1), shard], axis=2)
    lines = vectors_direct(after(vectors, moved_a[1:2]), dp, width, n_dp)
    passed_m = chip_pass([after(keep_m, ends, moved_a)], got_m, sent_m, n_dp, ways_m)
    block_out = settle(after(block_out, ends))
    moved_a, passed_m, lines, grad_inputs = lax.optimization_barrier((moved_a, passed_m, lines, grad_inputs))

    shards = gather_shards(tensor, moved_a, lines, *passed_m)
    grad_inputs = settle(after(grad_inputs, shards))
    share = jnp.sum(trade(shards).astype(F32), axis=0)
    share_a, lines, share_up, share_down = jnp.split(share, (rows, rows + 16, 2 * rows + 16))
    mine = lines[0]
    vec_out = mine[0 : 6 * each].reshape(6, each)
    share_b_qv = mine[6 * each : 6 * each + 2 * (part // n_dp)].reshape(2, part // n_dp)
    share_b_up = mine[6 * each + 2 * (part // n_dp) : 6 * each + (2 * part + ff) // n_dp]
    share_w_qkv = share_a[:, 0 : 3 * part].reshape(rows, 3, part)
    share_w_out = share_a[:, 3 * part :].T
    return (
        block_out,
        grad_inputs,
        vec_out[0],
        vec_out[1],
        share_w_qkv,
        share_b_qv,
        share_w_out,
        vec_out[2],
        vec_out[3],
        vec_out[4],
        share_up,
        share_b_up,
        share_down.T,
        vec_out[5],
    )


def solution(mesh):
    return jax.shard_map(
        functools.partial(local, mesh.shape["dp"], mesh.shape["tensor"]),
        mesh=mesh,
        in_specs=(
            P("dp", "tensor", None),
            P("dp", None),
            P(),
            P(),
            P(None, None, "tensor"),
            P(None, "tensor"),
            P("tensor", None),
            P(),
            P(),
            P(),
            P(None, "tensor"),
            P("tensor"),
            P("tensor", None),
            P(),
            P("dp", "tensor", None),
        ),
        out_specs=(
            P("dp", "tensor", None),
            P("dp", "tensor", None),
            P(("dp", "tensor")),
            P(("dp", "tensor")),
            P("dp", None, "tensor"),
            P(None, ("tensor", "dp")),
            P("tensor", "dp"),
            P(("dp", "tensor")),
            P(("dp", "tensor")),
            P(("dp", "tensor")),
            P("dp", "tensor"),
            P(("tensor", "dp")),
            P("tensor", "dp"),
            P(("dp", "tensor")),
        ),
        check_vma=False,
    )
```
